32 devices in a mesh: seq: 8 (over z, x), fsdp: 4 (over y, core).
Axes of the slice: x: 2, y: 2, z: 4, core: 2. Of those that a mesh axis runs over, the one named last changes fastest.
Arguments:
- tokens: bfloat16 [4, 4096, 1536], P('fsdp', 'seq'), may hold values from -6 to 6
- norm_gain: float32 [1536], replicated, may hold values from 0.25 to 1.75
- w_in: bfloat16 [1536, 6448], P('fsdp'), may hold values from -0.15625 to 0.15625
- conv_weight: float32 [4, 3328], replicated, may hold values from -3 to 3
- conv_bias: float32 [3328], replicated, may hold values from -1.5 to 1.5
- dt_bias: float32 [48], replicated, may hold values from -6 to -2
- a_log: float32 [48], replicated, may hold values from -4 to 1
- skip_gain: float32 [48], replicated, may hold values from 0.5 to 1.5
- out_gain: float32 [3072], replicated, may hold values from 0.25 to 1.75
- w_out: bfloat16 [3072, 1536], P('fsdp'), may hold values from -0.109375 to 0.109375
- cotangent: bfloat16 [4, 4096, 1536], P('fsdp', 'seq'), may hold values from -6 to 6
Outputs:
- block_out: float32 [4, 4096, 1536], P('fsdp', 'seq')
- d_tokens: float32 [4, 4096, 1536], P('fsdp', 'seq')
- d_norm_gain: float32 [1536], replicated
- d_w_in: float32 [1536, 6448], P(('seq', 'fsdp'))
- d_conv_weight: float32 [4, 3328], replicated
- d_conv_bias: float32 [3328], replicated
- d_dt_bias: float32 [48], replicated
- d_a_log: float32 [48], replicated
- d_skip_gain: float32 [48], replicated
- d_out_gain: float32 [3072], replicated
- d_w_out: float32 [3072, 1536], P(('seq', 'fsdp'))
The draws below stay inside these ranges and needn't reach their ends.
All inputs are finite; a program needn't handle non-finite values.
Results may differ from the reference program's by a relative error of at most 0.0089.
Values may be sent and summed in bfloat16 or wider, within the bound.
No kernel may reach another device: no remote copies, remote signals or barrier semaphores. Data moves between devices by JAX's collectives and lax.ppermute only.
A program may use at most 256 MiB of HBM per device.

```python
import jax
import jax.numpy as jnp
from jax import lax

D = 1536
HEADS = 48
STATE = 128
KW = 4
SPAN = 256
INNER = 3072
CONV = 3328
PROJ = 6448
LEN = 4096
SEQS = 4


def level_of(stream_key, extent, cuts, least, high):
    def one(position, parts):
        draws = jax.random.uniform(jax.random.fold_in(jax.random.fold_in(stream_key, 6), position), (parts,), jnp.float32, least / len(cuts), high / len(cuts))
        return jnp.repeat(jnp.exp(draws), extent[position] // parts).reshape((-1,) + (1,) * (len(extent) - position - 1))

    loudness = one(*cuts[0])
    for cut in cuts[1:]:
        loudness = loudness * one(*cut)
    return loudness


def bell_draw(rng, shape, width, bound, shards=(), kind=jnp.bfloat16):
    gain = level_of(rng, shape, shards, -0.22, 0.18) if shards else 1.0
    entries = jax.random.normal(rng, shape, jnp.float32) * width * gain
    return jnp.minimum(jnp.maximum(entries, -bound), bound).astype(kind)


def setup_inputs(seed: int = 0) -> dict:
    keys = jax.random.split(jax.random.key(seed), 12)
    tokens = bell_draw(keys[0], (SEQS, LEN, D), 1.0, 6.0, ((0, 4), (1, 8)))
    norm_gain = jnp.clip(1.0 + 0.15 * jax.random.normal(keys[1], (D,), jnp.float32), 0.25, 1.75)
    w_in = bell_draw(keys[2], (D, PROJ), D ** -0.5, 0.15625, ((0, 4),))
    conv_weight = bell_draw(keys[3], (KW, CONV), KW ** -0.5, 3.0, (), jnp.float32)
    conv_bias = bell_draw(keys[4], (CONV,), 0.3, 1.5, (), jnp.float32)
    dt_bias = jnp.clip(jax.random.uniform(keys[5], (HEADS,), jnp.float32, -6.0, -2.0), -6.0, -2.0)
    a_log = jnp.clip(jax.random.uniform(keys[6], (HEADS,), jnp.float32, -4.0, 1.0), -4.0, 1.0)
    skip_gain = jnp.clip(jax.random.uniform(keys[7], (HEADS,), jnp.float32, 0.5, 1.5), 0.5, 1.5)
    out_gain = jnp.clip(1.0 + 0.15 * jax.random.normal(keys[8], (INNER,), jnp.float32), 0.25, 1.75)
    w_out = bell_draw(keys[9], (INNER, D), INNER ** -0.5, 0.109375, ((0, 4),))
    cotangent = bell_draw(keys[10], (SEQS, LEN, D), 1.0, 6.0, ((0, 4), (1, 8)))
    return {"tokens": tokens, "norm_gain": norm_gain, "w_in": w_in, "conv_weight": conv_weight, "conv_bias": conv_bias, "dt_bias": dt_bias, "a_log": a_log, "skip_gain": skip_gain, "out_gain": out_gain, "w_out": w_out, "cotangent": cotangent}


EPSILON = 1e-05
HIGHEST = lax.Precision.HIGHEST

@jax.custom_vjp
def low(v):
    return lax.optimization_barrier(v.astype(jnp.bfloat16)).astype(jnp.float32)

@jax.custom_vjp
def low_back(v):
    return v

def low_keep(v):
    return (low(v), None)

def low_pass(kept, grad):
    return (grad,)

def back_keep(v):
    return (v, None)

def back_low(kept, grad):
    return (low(grad),)
low.defvjp(low_keep, low_pass)
low_back.defvjp(back_keep, back_low)

def pre_norm(values, gain_vec):
    inverse = lax.rsqrt(lax.optimization_barrier(jnp.mean(values * values, axis=-1, keepdims=True)) + EPSILON)
    return values * inverse * gain_vec

def gate_norm(mixed_in, gate_in, gain_vec):
    gated = mixed_in * jax.nn.silu(gate_in)
    inverse = lax.rsqrt(lax.optimization_barrier(jnp.mean(gated * gated, axis=-1, keepdims=True)) + EPSILON)
    return gated * inverse * gain_vec

def causal_conv(values, kernel, offset):
    width_k = kernel.shape[0]
    length = values.shape[0]
    padded = jnp.pad(values, ((width_k - 1, 0), (0, 0)))
    result = offset + kernel[0] * padded[0:length]
    for tap_idx in range(1, width_k):
        result = result + kernel[tap_idx] * padded[tap_idx:tap_idx + length]
    return result

def head_mix(x_pre, bc_pre, dt_raw, conv_x_w, conv_x_b, conv_bc_w, conv_bc_b, dt_shift, log_rate, skip_vec):
    length = x_pre.shape[0]
    head_count = dt_raw.shape[1]
    head_width = x_pre.shape[1] // head_count
    x_act = jax.nn.silu(causal_conv(x_pre, conv_x_w, conv_x_b))
    bc_act = jax.nn.silu(causal_conv(bc_pre, conv_bc_w, conv_bc_b))
    state_width = bc_act.shape[1] // 2
    step_len = jax.nn.softplus(dt_raw + dt_shift)
    decay_rate = -jnp.exp(log_rate)
    block_count = length // SPAN
    x_blocks = x_act.reshape(block_count, SPAN, head_count, head_width)
    b_blocks = bc_act[:, :state_width].reshape(block_count, SPAN, state_width)
    c_blocks = bc_act[:, state_width:].reshape(block_count, SPAN, state_width)
    d_blocks = step_len.reshape(block_count, SPAN, head_count)
    lower_mask = (jnp.arange(SPAN)[:, None] >= jnp.arange(SPAN)[None, :])[:, :, None]

    def one_block(carry_state, pieces):
        x_blk, b_blk, c_blk, d_blk = pieces
        cumulative = jnp.cumsum(d_blk * decay_rate, axis=0)
        scores = jnp.dot(c_blk, b_blk.T, precision=HIGHEST)
        differ = cumulative[:, None, :] - cumulative[None, :, :]
        weights = scores[:, :, None] * jnp.exp(jnp.where(lower_mask, differ, -1e+30)) * d_blk[None, :, :]
        inside = jnp.einsum('tsh,shp->thp', weights, x_blk, precision=HIGHEST)
        earlier = jnp.einsum('tn,hnp->thp', c_blk, carry_state, precision=HIGHEST) * jnp.exp(cumulative)[:, :, None]
        remain = jnp.exp(cumulative[-1:, :] - cumulative) * d_blk
        fresh_part = jnp.einsum('sn,shp->hnp', b_blk, x_blk * remain[:, :, None], precision=HIGHEST)
        new_state = jnp.exp(cumulative[-1])[:, None, None] * carry_state + fresh_part
        return (new_state, inside + earlier)
    start_state = jnp.zeros((head_count, state_width, head_width), x_act.dtype)
    _, outputs = lax.scan(jax.checkpoint(one_block), start_state, (x_blocks, b_blocks, c_blocks, d_blocks))
    outputs = outputs.reshape(length, head_count, head_width) + skip_vec[:, None] * x_act.reshape(length, head_count, head_width)
    return outputs.reshape(length, head_count * head_width)

def block_forward(values, norm_gain, w_in, conv_weight, conv_bias, dt_bias, a_log, skip_gain, out_gain, w_out):
    normed = low(pre_norm(values, norm_gain))
    projected = low_back(low(jnp.dot(normed, w_in, precision=HIGHEST)))
    gate_in = projected[:, :INNER]
    x_pre = projected[:, INNER:2 * INNER]
    bc_pre = projected[:, 2 * INNER:2 * INNER + 2 * STATE]
    dt_raw = projected[:, 2 * INNER + 2 * STATE:]
    mixed_out = head_mix(x_pre, bc_pre, dt_raw, conv_weight[:, :INNER], conv_bias[:INNER], conv_weight[:, INNER:], conv_bias[INNER:], dt_bias, a_log, skip_gain)
    mixed_out = low_back(low(mixed_out))
    normed_out = low(gate_norm(mixed_out, gate_in, out_gain))
    return values + jnp.dot(normed_out, w_out, precision=HIGHEST)

def reference(tokens, norm_gain, w_in, conv_weight, conv_bias, dt_bias, a_log, skip_gain, out_gain, w_out, cotangent):
    params = (norm_gain, w_in.astype(jnp.float32), conv_weight, conv_bias, dt_bias, a_log, skip_gain, out_gain, w_out.astype(jnp.float32))

    def one_sequence(summed, pieces):
        seq_tokens, seq_cotan = pieces
        result, back_fn = jax.vjp(block_forward, seq_tokens.astype(jnp.float32), *params)
        grads = back_fn(seq_cotan.astype(jnp.float32))
        summed = jax.tree.map(jnp.add, summed, tuple(grads[1:]))
        return (summed, (result, grads[0]))
    initial = jax.tree.map(jnp.zeros_like, params)
    summed, (outputs, d_tokens) = lax.scan(one_sequence, initial, (tokens, cotangent))
    d_gain_in, d_w_in, d_conv_w, d_conv_b, d_dt_b, d_alog, d_skip, d_gain_out, d_w_out = summed
    return (outputs, d_tokens, d_gain_in, d_w_in, d_conv_w, d_conv_b, d_dt_b, d_alog, d_skip, d_gain_out, d_w_out)
```

```python
import functools

import jax
import jax.numpy as jnp
from jax import lax
from jax.experimental import pallas as pl
from jax.experimental.pallas import tpu as pltpu
from jax.sharding import PartitionSpec as P

HEADS = 48
HEAD_DIM = 64
STATE = 128
KW = 4
INNER = 3072
D = 1536
CONV = INNER + 2 * STATE

EPSILON = 1e-05
CHUNK = 128
QUAD = 256
QUADS = INNER // QUAD
HALO = 16
VMEM_LIMIT = 56 * 1024 * 1024
F32 = jnp.float32
BF16 = jnp.bfloat16
HIGHEST = lax.Precision.HIGHEST
NT = (((1,), (1,)), ((), ()))
TN = (((0,), (0,)), ((), ()))


def iota(shape, axis):
    return lax.broadcasted_iota(jnp.int32, shape, axis)


def mm(a, b):
    return jnp.dot(a, b, preferred_element_type=F32)


def mm_nt(a, b):
    return lax.dot_general(a, b, NT, preferred_element_type=F32)


def sigmoid(v):
    return 0.5 * jnp.tanh(0.5 * v) + 0.5


def split3(v):
    high = v.astype(BF16)
    rest = v - high.astype(F32)
    mid = rest.astype(BF16)
    low = (rest - mid.astype(F32)).astype(BF16)
    return high, mid, low


def mm_exact(v, ones):
    high, mid, low = split3(v)
    return mm(high, ones) + mm(mid, ones) + mm(low, ones)


def head_ones():
    return jnp.where((iota((128, INNER), 1) >> 6) == iota((128, INNER), 0), 1.0, 0.0).astype(BF16)


def two_heads(first, second):
    return jnp.where(iota((CHUNK, 128), 1) < HEAD_DIM, first, second)


def spread(cols, start):
    wide = [jnp.broadcast_to(cols[:, start + i : start + i + 1], (CHUNK, 128)) for i in range(4)]
    return wide, jnp.concatenate([two_heads(wide[0], wide[1]), two_heads(wide[2], wide[3])], axis=1)


def columns_of(rows):
    count, length = rows.shape
    return jnp.concatenate([rows, jnp.zeros((128 - count, length), F32)], axis=0).T


def step_kernel(dt_ref, bias_ref, alog_ref, rows_ref, ecd_ref, total_ref):
    length = dt_ref.shape[0]
    raw = dt_ref[...].astype(F32) + bias_ref[...]
    step = jnp.maximum(raw, 0.0) + jnp.log1p(jnp.exp(-jnp.abs(raw)))
    sig = 1.0 / (1.0 + jnp.exp(-raw))
    rate = -jnp.exp(alog_ref[...])
    pace = step * rate
    lower = jnp.where(iota((CHUNK, CHUNK), 0) >= iota((CHUNK, CHUNK), 1), 1.0, 0.0).astype(F32)
    inside, along = [], []
    offset = jnp.zeros((1, 128), F32)
    for start in range(0, length, CHUNK):
        part = jnp.dot(lower, pace[start : start + CHUNK], precision=HIGHEST, preferred_element_type=F32)
        inside.append(part)
        along.append(part + offset)
        offset = offset + part[CHUNK - 1 : CHUNK]
    cum = jnp.concatenate(inside, axis=0)
    along = jnp.concatenate(along, axis=0)
    ecd_ref[...] = jnp.exp(along)
    total_ref[...] = jnp.broadcast_to(jnp.exp(offset), (8, 128))
    left = jnp.exp(offset - along) * step
    for place, array in enumerate((cum, step, left, sig, jnp.broadcast_to(rate, (length, 128)))):
        turned = array.T
        for quad in range(QUADS):
            rows_ref[quad, 8 * place : 8 * place + 4, :] = turned[4 * quad : 4 * quad + 4, :]
            rows_ref[quad, 8 * place + 4 : 8 * place + 8, :] = jnp.zeros((4, length), F32)


def step_call(dt_raw, dt_bias, a_log):
    length = dt_raw.shape[0]
    return pl.pallas_call(
        step_kernel,
        out_shape=(
            jax.ShapeDtypeStruct((QUADS, 40, length), F32),
            jax.ShapeDtypeStruct((length, 128), F32),
            jax.ShapeDtypeStruct((8, 128), F32),
        ),
        compiler_params=pltpu.CompilerParams(vmem_limit_bytes=VMEM_LIMIT),
        name="steps",
    )(dt_raw, dt_bias, a_log)


def conv_kernel(ranks, me_ref, v_ref, cw_ref, cb_ref, rows_ref, total_ref, *rest):
    x_ref, slope_ref, b_ref, c_ref, bt_ref, ct_ref = rest[:6]
    out_refs = rest[6 : 6 + ranks]
    ext, weighted, state = rest[6 + ranks :]
    length = v_ref.shape[0] - HALO
    share = STATE // ranks
    grid = pl.program_id(0)
    ext[...] = v_ref[...].astype(F32)

    def act(start):
        total = cb_ref[...] + cw_ref[0:1, :] * ext[HALO - 3 + start : HALO - 3 + start + CHUNK, :]
        for tap in range(1, KW):
            at = HALO - 3 + tap + start
            total = total + cw_ref[tap : tap + 1, :] * ext[at : at + CHUNK, :]
        sig = sigmoid(total)
        slope_ref[start : start + CHUNK, :] = (sig * (1.0 + total * (1.0 - sig))).astype(BF16)
        return total * sig

    @pl.when(grid == 0)
    def _():
        for start in range(0, length, CHUNK):
            both = act(start)
            b_part, c_part = both[:, :STATE], both[:, STATE:]
            b_ref[start : start + CHUNK, :] = b_part.astype(BF16)
            c_ref[start : start + CHUNK, :] = c_part.astype(BF16)
            bt_ref[:, start : start + CHUNK] = b_part.T.astype(BF16)
            ct_ref[:, start : start + CHUNK] = c_part.T.astype(BF16)
        high, mid, low = split3(total_ref[0:1, :])
        row = iota((share, 128), 0)
        told = jnp.where(row == 0, high.astype(F32), jnp.where(row == 1, mid.astype(F32), jnp.where(row == 2, low.astype(F32), 0.0)))
        for out_ref in out_refs:
            out_ref[:, INNER : INNER + 128] = told.astype(BF16)

    @pl.when(grid > 0)
    def _():
        cols = columns_of(rows_ref[0])
        for start in range(0, length, CHUNK):
            x_part = act(start)
            x_ref[start : start + CHUNK, :] = x_part.astype(BF16)
            _, left = spread(cols[start : start + CHUNK], 16)
            weighted[start : start + CHUNK, :] = (x_part * left).astype(BF16)
        state[...] = mm(bt_ref[...], weighted[...])
        lanes = pl.ds(pl.multiple_of((grid - 1) * QUAD, QUAD), QUAD)
        for step, out_ref in enumerate(out_refs):
            other = me_ref[0] ^ step
            out_ref[:, lanes] = state[pl.ds(pl.multiple_of(other * share, share), share), :].astype(BF16)


def conv_call(ranks, me, v, conv_weight, conv_bias, rows, total):
    length = v.shape[0] - HALO
    share = STATE // ranks
    last = QUADS
    block = lambda g, *_: (0, (g + last) % (last + 1))
    quad = lambda g, *_: (0, jnp.maximum(g - 1, 0))
    whole = lambda g, *_: (0, 0)
    grid_spec = pltpu.PrefetchScalarGridSpec(
        num_scalar_prefetch=1,
        grid=(last + 1,),
        in_specs=[
            pl.BlockSpec((length + HALO, QUAD), block),
            pl.BlockSpec((KW, QUAD), block),
            pl.BlockSpec((1, QUAD), block),
            pl.BlockSpec((1, 40, length), lambda g, *_: (jnp.maximum(g - 1, 0), 0, 0)),
            pl.BlockSpec((8, 128), whole),
        ],
        out_specs=[
            pl.BlockSpec((length, QUAD), quad),
            pl.BlockSpec((length, QUAD), block),
            pl.BlockSpec((length, STATE), whole),
            pl.BlockSpec((length, STATE), whole),
            pl.BlockSpec((STATE, length), whole),
            pl.BlockSpec((STATE, length), whole),
        ]
        + [pl.BlockSpec((share, INNER + 128), whole)] * ranks,
        scratch_shapes=[
            pltpu.VMEM((length + HALO, QUAD), F32),
            pltpu.VMEM((length, QUAD), BF16),
            pltpu.VMEM((STATE, QUAD), F32),
        ],
    )
    return pl.pallas_call(
        functools.partial(conv_kernel, ranks),
        grid_spec=grid_spec,
        out_shape=[
            jax.ShapeDtypeStruct((length, INNER), BF16),
            jax.ShapeDtypeStruct((length, CONV), BF16),
            jax.ShapeDtypeStruct((length, STATE), BF16),
            jax.ShapeDtypeStruct((length, STATE), BF16),
            jax.ShapeDtypeStruct((STATE, length), BF16),
            jax.ShapeDtypeStruct((STATE, length), BF16),
        ]
        + [jax.ShapeDtypeStruct((share, INNER + 128), BF16)] * ranks,
        compiler_params=pltpu.CompilerParams(vmem_limit_bytes=VMEM_LIMIT),
        cost_estimate=pl.CostEstimate(flops=int(4e8), bytes_accessed=int(2e7), transcendentals=0),
        name="conv_states",
    )(me, v, conv_weight, conv_bias, rows, total)


def carry_kernel(ranks, backward, me_ref, *rest):
    share = STATE // ranks
    if backward:
        in_refs, total_ref, out_refs = rest[:ranks], rest[ranks], rest[ranks + 1 : 2 * ranks + 1]
        held, decays = rest[2 * ranks + 1 :], total_ref[...]
        (held,) = held
    else:
        in_refs, out_refs, total_ref = rest[:ranks], rest[ranks : 2 * ranks], rest[2 * ranks]
        (held,) = rest[2 * ranks + 1 :]
    for step, in_ref in enumerate(in_refs):
        other = me_ref[0] ^ step
        held[other] = in_ref[:, :INNER].astype(F32)
        if not backward:
            told = in_ref[:, INNER : INNER + 128].astype(F32)
            total_ref[pl.ds(other, 1), :] = told[0:1] + told[1:2] + told[2:3]
    if not backward:
        decays = total_ref[...]
    wide = mm_exact(decays, head_ones())
    carry = jnp.zeros((share, INNER), F32)
    for place in range(ranks - 1, -1, -1) if backward else range(ranks):
        fresh = held[place]
        held[place] = carry
        carry = wide[place : place + 1] * carry + fresh
    for step, out_ref in enumerate(out_refs):
        out_ref[...] = held[me_ref[0] ^ step].astype(BF16)


def carry_call(ranks, me, parts, totals=None):
    share = STATE // ranks
    backward = totals is not None
    smem = pl.BlockSpec(memory_space=pltpu.SMEM)
    vmem = pl.BlockSpec(memory_space=pltpu.VMEM)
    outs = [jax.ShapeDtypeStruct((share, INNER), BF16)] * ranks
    args = list(parts) + ([totals] if backward else [])
    if not backward:
        outs.append(jax.ShapeDtypeStruct((ranks, 128), F32))
    return pl.pallas_call(
        functools.partial(carry_kernel, ranks, backward),
        in_specs=[smem] + [vmem] * len(args),
        out_specs=[vmem] * len(outs),
        out_shape=outs,
        scratch_shapes=[pltpu.VMEM((ranks, share, INNER), F32)],
        compiler_params=pltpu.CompilerParams(vmem_limit_bytes=VMEM_LIMIT),
        name="carry_back" if backward else "carry",
    )(me, *args)


def inside_kernel(x_ref, b_ref, c_ref, bt_ref, rows_ref, skip_ref, y_ref, scores, state):
    length = x_ref.shape[0]
    grid = pl.program_id(0)

    @pl.when(grid == 0)
    def _():
        for start in range(0, length, CHUNK):
            part = slice(start, start + CHUNK)
            scores[part, :] = mm_nt(c_ref[part, :], b_ref[part, :])

    cols = columns_of(rows_ref[0])
    lower = iota((CHUNK, CHUNK), 0) >= iota((CHUNK, CHUNK), 1)
    first = iota((CHUNK, 128), 1) < HEAD_DIM
    for start in range(0, length, CHUNK):
        part = slice(start, start + CHUNK)
        x_f = x_ref[part, :].astype(F32)
        wide, cum = spread(cols[part], 0)
        _, step = spread(cols[part], 8)
        weights = []
        for head in range(4):
            cum_row = rows_ref[0, head : head + 1, part]
            step_row = rows_ref[0, 8 + head : 9 + head, part]
            fade = jnp.exp(jnp.where(lower, wide[head] - cum_row, -1e30))
            weights.append((scores[part, :] * fade * step_row).astype(BF16))
        pieces = []
        for pair in range(2):
            x_pair = x_f[:, 128 * pair : 128 * pair + 128]
            both = jnp.concatenate([jnp.where(first, x_pair, 0.0), jnp.where(first, 0.0, x_pair)], axis=0)
            pieces.append(mm(jnp.concatenate(weights[2 * pair : 2 * pair + 2], axis=1), both.astype(BF16)))
        y_part = jnp.concatenate(pieces, axis=1) + skip_ref[...] * x_f
        if start > 0:
            y_part = y_part + jnp.exp(cum) * mm(c_ref[part, :], state[...].astype(BF16))
        y_ref[part, :] = y_part
        if start + CHUNK < length:
            end = cum[CHUNK - 1 : CHUNK]
            fresh = mm(bt_ref[:, part], (x_f * (jnp.exp(end - cum) * step)).astype(BF16))
            state[...] = fresh if start == 0 else jnp.exp(end) * state[...] + fresh


def inside_call(x_act, b_act, c_act, b_turned, rows, skip_wide):
    length = x_act.shape[0]
    whole = lambda g: (0, 0)
    quad = lambda g: (0, g)
    return pl.pallas_call(
        inside_kernel,
        grid=(QUADS,),
        in_specs=[
            pl.BlockSpec((length, QUAD), quad),
            pl.BlockSpec((length, STATE), whole),
            pl.BlockSpec((length, STATE), whole),
            pl.BlockSpec((STATE, length), whole),
            pl.BlockSpec((1, 40, length), lambda g: (g, 0, 0)),
            pl.BlockSpec((1, QUAD), quad),
        ],
        out_specs=pl.BlockSpec((length, QUAD), quad),
        out_shape=jax.ShapeDtypeStruct((length, INNER), F32),
        scratch_shapes=[pltpu.VMEM((length, CHUNK), F32), pltpu.VMEM((STATE, QUAD), F32)],
        compiler_params=pltpu.CompilerParams(vmem_limit_bytes=VMEM_LIMIT),
        cost_estimate=pl.CostEstimate(flops=int(8e9), bytes_accessed=int(2e7), transcendentals=0),
        name="ssd_inside",
    )(x_act, b_act, c_act, b_turned, rows, skip_wide)


def gate_kernel(ranks, me_ref, y_ref, gate_ref, dn_ref, c_ref, ct_ref, ecd_ref, gain_ref, *rest):
    in_refs = rest[:ranks]
    normed_ref, dgate_ref, dm_ref, dgain_ref, sin_ref = rest[ranks : ranks + 5]
    out_refs = rest[ranks + 5 : 2 * ranks + 5]
    sin, ones, ecd, gated, silu, slope, back = rest[2 * ranks + 5 :]
    share = STATE // ranks
    grid = pl.program_id(0)

    @pl.when(grid == 0)
    def _():
        for step, in_ref in enumerate(in_refs):
            other = me_ref[0] ^ step
            sin[pl.ds(pl.multiple_of(other * share, share), share), :] = in_ref[...].astype(F32)
        sin_ref[...] = sin[...].astype(BF16)
        ones[...] = head_ones()
        back[...] = jnp.zeros_like(back)
        dgain_ref[...] = jnp.zeros_like(dgain_ref)

    high, mid, _ = split3(ecd_ref[...])
    squares = jnp.zeros((CHUNK, QUAD), F32)
    product = jnp.zeros((CHUNK, QUAD), F32)
    for at in range(0, INNER, QUAD):
        lanes = slice(at, at + QUAD)
        grown = mm(high, ones[:, lanes]) + mm(mid, ones[:, lanes])
        ecd[:, lanes] = grown
        mixed = y_ref[:, lanes] + grown * mm(c_ref[...], sin_ref[:, lanes])
        mixed = mixed.astype(BF16).astype(F32)
        gate = gate_ref[:, lanes].astype(F32)
        sig = sigmoid(gate)
        open_part = gate * sig
        value = mixed * open_part
        silu[:, lanes] = open_part
        slope[:, lanes] = mixed * (sig * (1.0 + gate * (1.0 - sig)))
        gated[:, lanes] = value
        squares = squares + value * value
        product = product + dn_ref[:, lanes] * gain_ref[:, lanes] * value
    inverse = lax.rsqrt(jnp.sum(squares, axis=1, keepdims=True) * (1.0 / INNER) + EPSILON)
    shift = inverse * inverse * inverse * (jnp.sum(product, axis=1, keepdims=True) * (1.0 / INNER))
    inverse = jnp.broadcast_to(inverse, (CHUNK, QUAD))
    shift = jnp.broadcast_to(shift, (CHUNK, QUAD))
    for at in range(0, INNER, QUAD):
        lanes = slice(at, at + QUAD)
        value = gated[:, lanes]
        scaled = value * inverse
        gain = gain_ref[:, lanes]
        dn = dn_ref[:, lanes]
        normed_ref[:, lanes] = (scaled * gain).astype(BF16)
        dgain_ref[:, lanes] += jnp.sum(dn * scaled, axis=0, keepdims=True)
        d_gated = inverse * (dn * gain) - value * shift
        dgate_ref[:, lanes] = (d_gated * slope[:, lanes]).astype(BF16)
        d_mixed = (d_gated * silu[:, lanes]).astype(BF16)
        dm_ref[:, lanes] = d_mixed
        back[:, lanes] += mm(ct_ref[...], (d_mixed.astype(F32) * ecd[:, lanes]).astype(BF16))

    @pl.when(grid == pl.num_programs(0) - 1)
    def _():
        for step, out_ref in enumerate(out_refs):
            other = me_ref[0] ^ step
            out_ref[...] = back[pl.ds(pl.multiple_of(other * share, share), share), :].astype(BF16)


def gate_call(ranks, me, y_inside, gate_in, d_normed, c_act, c_turned, ecd, out_gain, parts):
    length = y_inside.shape[0]
    share = STATE // ranks
    whole = lambda g, *_: (0, 0)
    down = lambda g, *_: (g, 0)
    wide = pl.BlockSpec((CHUNK, INNER), down)
    grid_spec = pltpu.PrefetchScalarGridSpec(
        num_scalar_prefetch=1,
        grid=(length // CHUNK,),
        in_specs=[
            wide,
            wide,
            wide,
            pl.BlockSpec((CHUNK, STATE), down),
            pl.BlockSpec((STATE, CHUNK), lambda g, *_: (0, g)),
            pl.BlockSpec((CHUNK, 128), down),
            pl.BlockSpec((1, INNER), whole),
        ]
        + [pl.BlockSpec((share, INNER), whole)] * ranks,
        out_specs=[wide, wide, wide, pl.BlockSpec((1, INNER), whole), pl.BlockSpec((STATE, INNER), whole)]
        + [pl.BlockSpec((share, INNER), whole)] * ranks,
        scratch_shapes=[
            pltpu.VMEM((STATE, INNER), F32),
            pltpu.VMEM((128, INNER), BF16),
            pltpu.VMEM((CHUNK, INNER), F32),
            pltpu.VMEM((CHUNK, INNER), F32),
            pltpu.VMEM((CHUNK, INNER), F32),
            pltpu.VMEM((CHUNK, INNER), F32),
            pltpu.VMEM((STATE, INNER), F32),
        ],
    )
    rows = jax.ShapeDtypeStruct((length, INNER), BF16)
    return pl.pallas_call(
        functools.partial(gate_kernel, ranks),
        grid_spec=grid_spec,
        out_shape=[rows, rows, rows, jax.ShapeDtypeStruct((1, INNER), F32), jax.ShapeDtypeStruct((STATE, INNER), BF16)]
        + [jax.ShapeDtypeStruct((share, INNER), BF16)] * ranks,
        compiler_params=pltpu.CompilerParams(vmem_limit_bytes=VMEM_LIMIT),
        cost_estimate=pl.CostEstimate(flops=int(2e9), bytes_accessed=int(3e7), transcendentals=0),
        name="gated_norm",
    )(me, y_inside, gate_in, d_normed, c_act, c_turned, ecd, out_gain, *parts)


def back_kernel(ranks, me_ref, x_ref, dm_ref, slope_ref, v_ref, cw_ref, b_ref, c_ref, bt_ref, ct_ref, rows_ref, skip_ref, sin_ref, *rest):
    in_refs = rest[:ranks]
    dv_ref, sums_ref, heads_ref = rest[ranks : ranks + 3]
    scores, d_scores, d_b, d_c, states, back, grads, ext, d_step = rest[ranks + 3 :]
    length = x_ref.shape[0]
    share = STATE // ranks
    chunks = length // CHUNK
    grid = pl.program_id(0)

    @pl.when(grid == 0)
    def _():
        for start in range(0, length, CHUNK):
            part = slice(start, start + CHUNK)
            scores[part, :] = mm_nt(b_ref[part, :], c_ref[part, :])
        d_scores[...] = jnp.zeros_like(d_scores)
        d_b[...] = jnp.zeros_like(d_b)
        d_c[...] = jnp.zeros_like(d_c)
        d_step[...] = jnp.zeros_like(d_step)
        grads[0:HALO, :] = jnp.zeros((HALO, QUAD), F32)
        grads[HALO + length :, :] = jnp.zeros((HALO, QUAD), F32)

    def finish(extra):
        ext[...] = v_ref[...].astype(F32)
        total = [jnp.zeros((1, QUAD), F32)] * (KW + 1)
        for start in range(0, length, CHUNK):
            here = grads[HALO + start : HALO + start + CHUNK, :]
            for tap in range(KW):
                at = HALO - 3 + tap + start
                total[tap] = total[tap] + jnp.sum(here * ext[at : at + CHUNK, :], axis=0, keepdims=True)
            total[KW] = total[KW] + jnp.sum(here, axis=0, keepdims=True)
        for at, row in enumerate(total + [extra]):
            sums_ref[at : at + 1, :] = row
        sums_ref[KW + 2 : 8, :] = jnp.zeros((8 - KW - 2, QUAD), F32)
        for start in [0] + list(range(HALO, HALO + length, CHUNK)):
            count = HALO if start == 0 else CHUNK
            value = cw_ref[KW - 1 : KW, :] * grads[start : start + count, :]
            for tap in range(KW - 1):
                at = start + KW - 1 - tap
                value = value + cw_ref[tap : tap + 1, :] * grads[at : at + count, :]
            dv_ref[start : start + count, :] = value.astype(BF16)

    @pl.when(grid < QUADS)
    def _():
        cols = columns_of(rows_ref[0])
        upper = iota((CHUNK, CHUNK), 0) <= iota((CHUNK, CHUNK), 1)
        first = iota((CHUNK, 128), 1) < HEAD_DIM
        lane = iota((CHUNK, 128), 1)
        line = iota((8, 128), 0)
        head_of = iota((QUAD, 128), 0) >> 6
        ones_v = jnp.where(iota((QUAD, 128), 1) == head_of + 8, 1.0, 0.0).astype(BF16)
        ones_u = jnp.where(iota((QUAD, 128), 1) == head_of + 16, 1.0, 0.0).astype(BF16)
        square = (CHUNK, CHUNK)
        later = jnp.where(iota(square, 0) >= iota(square, 1), 1.0, 0.0).astype(BF16)
        before = jnp.where(iota(square, 0) < iota(square, 1), 1.0, 0.0).astype(BF16)
        skip = skip_ref[...]
        for step, in_ref in enumerate(in_refs):
            other = me_ref[0] ^ step
            back[pl.ds(pl.multiple_of(other * share, share), share), :] = in_ref[...].astype(F32)
        state = sin_ref[...].astype(F32)
        for chunk in range(chunks):
            part = slice(chunk * CHUNK, chunk * CHUNK + CHUNK)
            states[chunk] = state
            if chunk + 1 < chunks:
                _, cum = spread(cols[part], 0)
                _, step = spread(cols[part], 8)
                end = cum[CHUNK - 1 : CHUNK]
                fed = (x_ref[part, :].astype(F32) * (jnp.exp(end - cum) * step)).astype(BF16)
                state = jnp.exp(end) * state + mm(bt_ref[:, part], fed)
        skip_sum = jnp.zeros((1, QUAD), F32)
        bias_sum = jnp.zeros((8, 1), F32)
        rate_sum = jnp.zeros((8, 1), F32)
        for chunk in range(chunks - 1, -1, -1):
            part = slice(chunk * CHUNK, chunk * CHUNK + CHUNK)
            x_f = x_ref[part, :].astype(F32)
            dm = dm_ref[part, :]
            dm_f = dm.astype(F32)
            cum_wide, cum = spread(cols[part], 0)
            step_wide, step = spread(cols[part], 8)
            end = cum[CHUNK - 1 : CHUNK]
            after = back[...]
            after_low = after.astype(BF16)
            state = states[chunk]
            left = jnp.exp(end - cum)
            grown = dm_f * jnp.exp(cum)
            grown_low = grown.astype(BF16)
            faded = x_f * left
            from_after = mm(b_ref[part, :], after_low)
            from_state = mm(c_ref[part, :], state.astype(BF16))
            d_b[part, :] += mm_nt((faded * step).astype(BF16), after_low)
            d_c[part, :] += mm_nt(grown_low, state.astype(BF16))
            marks = mm((grown * from_state).astype(BF16), ones_v) + mm((faded * from_after).astype(BF16), ones_u)
            pair_sum = jnp.zeros((8, CHUNK), F32)
            crossing = jnp.zeros((8, 1), F32)
            cross = jnp.sum(state * after, axis=0, keepdims=True) * jnp.exp(end)
            pieces = []
            for pair in range(2):
                x_pair = x_f[:, 128 * pair : 128 * pair + 128]
                dm_pair = dm_f[:, 128 * pair : 128 * pair + 128]
                x_both = jnp.concatenate([jnp.where(first, x_pair, 0.0), jnp.where(first, 0.0, x_pair)], axis=0)
                dm_both = jnp.concatenate([jnp.where(first, dm_pair, 0.0), jnp.where(first, 0.0, dm_pair)], axis=0)
                d_weights = mm_nt(x_both.astype(BF16), dm[:, 128 * pair : 128 * pair + 128])
                kept = []
                for half in range(2):
                    head = 2 * pair + half
                    cum_row = rows_ref[0, head : head + 1, part]
                    fade = jnp.exp(jnp.where(upper, cum_row - cum_wide[head], -1e30))
                    faded_grad = d_weights[half * CHUNK : half * CHUNK + CHUNK] * fade
                    d_scores[part, :] += faded_grad * step_wide[head]
                    joint = faded_grad * scores[part, :]
                    marks = marks + jnp.where(lane == head, jnp.sum(joint, axis=1, keepdims=True), 0.0)
                    row = jnp.sum(joint * step_wide[head], axis=0, keepdims=True)
                    pair_sum = pair_sum + jnp.where(line == head, row, 0.0)
                    kept.append((scores[part, :] * fade).astype(BF16))
                    low, high = 64 * head, 64 * head + 64
                    here = (iota((1, QUAD), 1) >= low) & (iota((1, QUAD), 1) < high)
                    amount = jnp.sum(jnp.where(here, cross, 0.0), axis=1, keepdims=True)
                    crossing = crossing + jnp.where(iota((8, 1), 0) == head, amount, 0.0)
                pieces.append(mm(jnp.concatenate(kept, axis=1), dm_both.astype(BF16)))
            direct = jnp.concatenate(pieces, axis=1) + left * from_after
            d_x = step * direct + skip * dm_f
            grads[HALO + chunk * CHUNK : HALO + chunk * CHUNK + CHUNK, :] = d_x * slope_ref[part, :].astype(F32)
            skip_sum = skip_sum + jnp.sum(x_f * dm_f, axis=0, keepdims=True)
            back[...] = jnp.exp(end) * after + mm(ct_ref[:, part], grown_low)
            marks = marks.T
            within, carried, outward = marks[0:8], marks[8:16], marks[16:24]
            step_rows = rows_ref[0, 8:16, part]
            change = pair_sum - step_rows * within + carried
            decay = mm_exact(change, later) + mm_exact(step_rows * outward, before) + crossing
            d_raw = (within + outward + rows_ref[0, 32:40, part] * decay) * rows_ref[0, 24:32, part]
            d_step[pl.ds(pl.multiple_of(grid * 8, 8), 8), part] = d_raw
            bias_sum = bias_sum + jnp.sum(d_raw, axis=1, keepdims=True)
            rate_sum = rate_sum + jnp.sum(step_rows * decay, axis=1, keepdims=True)
        heads_ref[0, 0:8, :] = jnp.broadcast_to(bias_sum, (8, 128))
        heads_ref[0, 8:16, :] = jnp.broadcast_to(rate_sum, (8, 128))
        finish(skip_sum)

    @pl.when(grid == QUADS)
    def _():
        for start in range(0, length, CHUNK):
            part = slice(start, start + CHUNK)
            low = d_scores[part, :].astype(BF16)
            into_b = d_b[part, :] + mm(low, c_ref[part, :])
            into_c = d_c[part, :] + mm(d_scores[part, :].T.astype(BF16), b_ref[part, :])
            both = jnp.concatenate([into_b, into_c], axis=1)
            grads[HALO + start : HALO + start + CHUNK, :] = both * slope_ref[part, :].astype(F32)
        finish(jnp.zeros((1, QUAD), F32))

    @pl.when(grid == QUADS + 1)
    def _():
        row, column = iota((128, QUAD), 0), iota((128, QUAD), 1)
        pick = (column < HEADS) & (row == 8 * (column >> 2) + (column & 3))
        turned = d_step[...].T.astype(BF16)
        dv_ref[0:HALO, :] = jnp.zeros((HALO, QUAD), BF16)
        dv_ref[HALO:, :] = mm(turned, jnp.where(pick, 1.0, 0.0).astype(BF16)).astype(BF16)


def back_call(ranks, me, x_act, d_mixed, slope, v, conv_weight, b_act, c_act, b_turned, c_turned, rows, skip_wide, s_in, parts):
    length = x_act.shape[0]
    share = STATE // ranks
    whole = lambda g, *_: (0, 0)
    quad = lambda g, *_: (0, jnp.minimum(g, QUADS - 1))
    block = lambda g, *_: (0, jnp.minimum(g, QUADS))
    lead = lambda g, *_: (jnp.minimum(g, QUADS - 1), 0, 0)
    grid_spec = pltpu.PrefetchScalarGridSpec(
        num_scalar_prefetch=1,
        grid=(QUADS + 2,),
        in_specs=[
            pl.BlockSpec((length, QUAD), quad),
            pl.BlockSpec((length, QUAD), quad),
            pl.BlockSpec((length, QUAD), block),
            pl.BlockSpec((length + HALO, QUAD), block),
            pl.BlockSpec((KW, QUAD), block),
            pl.BlockSpec((length, STATE), whole),
            pl.BlockSpec((length, STATE), whole),
            pl.BlockSpec((STATE, length), whole),
            pl.BlockSpec((STATE, length), whole),
            pl.BlockSpec((1, 40, length), lead),
            pl.BlockSpec((1, QUAD), quad),
            pl.BlockSpec((STATE, QUAD), quad),
        ]
        + [pl.BlockSpec((share, QUAD), quad)] * ranks,
        out_specs=[
            pl.BlockSpec((length + HALO, QUAD), lambda g, *_: (0, g)),
            pl.BlockSpec((8, QUAD), block),
            pl.BlockSpec((1, 16, 128), lead),
        ],
        scratch_shapes=[
            pltpu.VMEM((length, CHUNK), F32),
            pltpu.VMEM((length, CHUNK), F32),
            pltpu.VMEM((length, STATE), F32),
            pltpu.VMEM((length, STATE), F32),
            pltpu.VMEM((length // CHUNK, STATE, QUAD), F32),
            pltpu.VMEM((STATE, QUAD), F32),
            pltpu.VMEM((length + 2 * HALO, QUAD), F32),
            pltpu.VMEM((length + HALO, QUAD), F32),
            pltpu.VMEM((128, length), F32),
        ],
    )
    return pl.pallas_call(
        functools.partial(back_kernel, ranks),
        grid_spec=grid_spec,
        out_shape=[
            jax.ShapeDtypeStruct((length + HALO, CONV + QUAD), BF16),
            jax.ShapeDtypeStruct((8, CONV), F32),
            jax.ShapeDtypeStruct((QUADS, 16, 128), F32),
        ],
        compiler_params=pltpu.CompilerParams(vmem_limit_bytes=VMEM_LIMIT),
        cost_estimate=pl.CostEstimate(flops=int(2e10), bytes_accessed=int(4e7), transcendentals=0),
        name="ssd_back",
    )(me, x_act, d_mixed, slope, v, conv_weight, b_act, c_act, b_turned, c_turned, rows, skip_wide, s_in, *parts)


def on_device(
    ranks,
    shards,
    tokens,
    norm_gain,
    w_in,
    conv_weight,
    conv_bias,
    dt_bias,
    a_log,
    skip_gain,
    out_gain,
    w_out,
    cotangent,
):
    both = ("seq", "fsdp")
    rank = lax.axis_index("seq")
    shard = lax.axis_index("fsdp")
    me = rank.astype(jnp.int32).reshape(1)

    def move(value, target):
        pairs = []
        for s in range(ranks):
            for f in range(shards):
                goal = target(s, f)
                if goal is not None:
                    pairs.append((s * shards + f, goal[0] * shards + goal[1]))
        return lax.ppermute(value, both, pairs)

    def gather(value):
        got = [value]
        for step in range(2, shards, 2):
            got.append(move(value, lambda s, f: (s, f ^ step)))
        pieces = []
        for piece in got:
            pieces += [piece, move(piece, lambda s, f: (s, f ^ 1))]
        return pieces

    def exchange(parts):
        return [part if step == 0 else move(part, lambda s, f: (s ^ step, f)) for step, part in enumerate(parts)]

    def total(value):
        step = 1
        while step < shards:
            value = value + move(value, lambda s, f: (s, f ^ step))
            step *= 2
        step = 1
        while step < ranks:
            value = value + move(value, lambda s, f: (s ^ step, f))
            step *= 2
        return value

    def ordered(pieces):
        stack = jnp.stack(pieces)
        return stack[jnp.arange(shards) ^ shard].reshape((-1,) + pieces[0].shape[1:])

    halo = move(tokens[0, -HALO:], lambda s, f: (s + 1, f) if s + 1 < ranks else None)
    values = tokens[0].astype(F32)
    longer = jnp.concatenate([halo, tokens[0]], axis=0).astype(F32)
    inverse = lax.rsqrt(jnp.mean(longer * longer, axis=-1, keepdims=True) + EPSILON)
    normed_long = (longer * inverse * norm_gain).astype(BF16)
    inverse = inverse[HALO:]
    normed = normed_long[HALO:]

    w_v = ordered(gather(w_in[:, INNER:]))
    w_g = ordered(gather(w_in[:, :INNER]))
    w_o = ordered(gather(w_out))

    projected = mm(normed_long, w_v).astype(BF16)
    dt_raw = jnp.pad(projected[HALO:, CONV:], ((0, 0), (0, 128 - HEADS)))
    lanes = lambda vec: jnp.pad(vec, (0, 128 - HEADS)).reshape(1, 128)
    rows, ecd, decay_all = step_call(dt_raw, lanes(dt_bias), lanes(a_log))
    v = projected[:, :CONV]
    made = conv_call(ranks, me, v, conv_weight, conv_bias.reshape(1, CONV), rows, decay_all)
    x_act, slope, b_act, c_act, b_turned, c_turned = made[:6]
    carried = carry_call(ranks, me, exchange(made[6:]))
    parts, totals = exchange(carried[:ranks]), carried[ranks]
    skip_wide = jnp.repeat(skip_gain, HEAD_DIM).reshape(1, INNER)
    y_inside = inside_call(x_act, b_act, c_act, b_turned, rows, skip_wide)
    gate_in = mm(normed, w_g).astype(BF16)
    cotan = cotangent[0]
    d_normed_out = mm_nt(cotan, w_o)
    made = gate_call(ranks, me, y_inside, gate_in, d_normed_out, c_act, c_turned, ecd, out_gain.reshape(1, INNER), parts)
    normed_out, d_gate, d_mixed, d_gain_out, s_in = made[:5]
    parts = exchange(carry_call(ranks, me, exchange(made[5:]), totals))
    block_out = values + mm(normed_out, w_o)

    def scattered(left, right):
        partial = lax.dot_general(left, right, TN, preferred_element_type=F32).astype(BF16)
        return lax.psum_scatter(partial, both, scatter_dimension=0, tiled=True).astype(F32)

    d_w_out = scattered(normed_out, cotan)
    d_w_gate = scattered(normed, d_gate)
    d_v_long, sums, heads = back_call(
        ranks, me, x_act, d_mixed, slope, v, conv_weight, b_act, c_act, b_turned, c_turned, rows, skip_wide, s_in, parts
    )
    d_w_rest = scattered(normed_long, d_v_long[:, : CONV + HEADS])
    d_w_in = jnp.concatenate([d_w_gate, d_w_rest], axis=1)

    spill = move(d_v_long[:HALO], lambda s, f: (s - 1, f) if s > 0 else None)
    ends = (d_v_long[-HALO:].astype(F32) + spill.astype(F32)).astype(BF16)
    d_v = lax.dynamic_update_slice(d_v_long, ends, (d_v_long.shape[0] - HALO, 0))[HALO:, : CONV + HEADS]
    d_normed = mm_nt(d_gate, w_g) + mm_nt(d_v, w_v)
    d_norm_gain = jnp.sum(d_normed * values * inverse, axis=0)
    scaled = d_normed * norm_gain
    shift = inverse * inverse * inverse * jnp.mean(scaled * values, axis=-1, keepdims=True)
    d_tokens = cotan.astype(F32) + inverse * scaled - values * shift

    d_skip = sums[KW + 1, :INNER].reshape(HEADS, HEAD_DIM).sum(axis=1)
    pieces = [
        d_norm_gain,
        sums[:KW].reshape(-1),
        sums[KW],
        heads[:, 0:4, 0].reshape(-1),
        heads[:, 8:12, 0].reshape(-1) * -jnp.exp(a_log),
        d_skip,
        d_gain_out.reshape(-1),
    ]
    flat = jnp.concatenate(pieces)
    width = flat.shape[0]
    flat = total(jnp.pad(flat, (0, -width % 1024)).reshape(-1, 128)).reshape(-1)
    small, at = [], 0
    for piece in pieces:
        small.append(flat[at : at + piece.shape[0]])
        at += piece.shape[0]
    d_norm_gain, d_conv_weight, d_conv_bias, d_dt_bias, d_a_log, d_skip, d_gain_out = small
    return (
        block_out[None],
        d_tokens[None],
        d_norm_gain,
        d_w_in,
        d_conv_weight.reshape(KW, CONV),
        d_conv_bias,
        d_dt_bias,
        d_a_log,
        d_skip,
        d_gain_out,
        d_w_out,
    )


def solution(mesh):
    split = P("fsdp", "seq", None)
    rows = P("fsdp", None)
    last = P(("seq", "fsdp"), None)
    return jax.shard_map(
        functools.partial(on_device, mesh.shape["seq"], mesh.shape["fsdp"]),
        mesh=mesh,
        in_specs=(split, P(), rows, P(), P(), P(), P(), P(), P(), rows, split),
        out_specs=(split, split, P(), last, P(), P(), P(), P(), P(), P(), last),
        check_vma=False,
    )
```

```python
import functools

import jax
import jax.numpy as jnp
from jax import lax
from jax.experimental import pallas as pl
from jax.experimental.pallas import tpu as pltpu
from jax.sharding import PartitionSpec as P

HEADS = 48
HEAD_DIM = 64
STATE = 128
KW = 4
INNER = 3072
D = 1536
CONV = INNER + 2 * STATE

EPSILON = 1e-05
CHUNK = 128
QUAD = 256
QUADS = INNER // QUAD
HALO = 16
VMEM_LIMIT = 56 * 1024 * 1024
COST = pl.CostEstimate(flops=1000000, bytes_accessed=1000000, transcendentals=0)
F32 = jnp.float32
BF16 = jnp.bfloat16
HIGHEST = lax.Precision.HIGHEST
NT = (((1,), (1,)), ((), ()))
TN = (((0,), (0,)), ((), ()))


def iota(shape, axis):
    return lax.broadcasted_iota(jnp.int32, shape, axis)


def mm(a, b):
    return jnp.dot(a, b, preferred_element_type=F32)


def mm_nt(a, b):
    return lax.dot_general(a, b, NT, preferred_element_type=F32)


def sigmoid(v):
    return 0.5 * jnp.tanh(0.5 * v) + 0.5


def split3(v):
    high = v.astype(BF16)
    rest = v - high.astype(F32)
    mid = rest.astype(BF16)
    low = (rest - mid.astype(F32)).astype(BF16)
    return high, mid, low


def mm_exact(v, ones):
    high, mid, low = split3(v)
    return mm(high, ones) + mm(mid, ones) + mm(low, ones)


def head_ones():
    return jnp.where((iota((128, INNER), 1) >> 6) == iota((128, INNER), 0), 1.0, 0.0).astype(BF16)


def two_heads(first, second):
    return jnp.where(iota((CHUNK, 128), 1) < HEAD_DIM, first, second)


def spread(cols, start):
    wide = [jnp.broadcast_to(cols[:, start + i : start + i + 1], (CHUNK, 128)) for i in range(4)]
    return wide, jnp.concatenate([two_heads(wide[0], wide[1]), two_heads(wide[2], wide[3])], axis=1)


def fold_rows(value):
    return jnp.sum(value.reshape(-1, 8, value.shape[1]), axis=0)


def columns_of(rows):
    count, length = rows.shape
    return jnp.concatenate([rows, jnp.zeros((128 - count, length), F32)], axis=0).T


def step_kernel(dt_ref, bias_ref, alog_ref, rows_ref, ecd_ref, total_ref):
    length = dt_ref.shape[0] - HALO
    raw = dt_ref[HALO:, :].astype(F32) + bias_ref[...]
    step = jnp.maximum(raw, 0.0) + jnp.log1p(jnp.exp(-jnp.abs(raw)))
    sig = 1.0 / (1.0 + jnp.exp(-raw))
    rate = -jnp.exp(alog_ref[...])
    pace = step * rate
    lower = jnp.where(iota((CHUNK, CHUNK), 0) >= iota((CHUNK, CHUNK), 1), 1.0, 0.0).astype(F32)
    inside, along = [], []
    offset = jnp.zeros((1, 128), F32)
    for start in range(0, length, CHUNK):
        part = jnp.dot(lower, pace[start : start + CHUNK], precision=HIGHEST, preferred_element_type=F32)
        inside.append(part)
        along.append(part + offset)
        offset = offset + part[CHUNK - 1 : CHUNK]
    cum = jnp.concatenate(inside, axis=0)
    along = jnp.concatenate(along, axis=0)
    ecd_ref[...] = jnp.exp(along)
    total_ref[...] = jnp.broadcast_to(jnp.exp(offset), (8, 128))
    left = jnp.exp(offset - along) * step
    for place, array in enumerate((cum, step, left, sig, jnp.broadcast_to(rate, (length, 128)))):
        turned = array.T
        for quad in range(QUADS):
            rows_ref[quad, 8 * place : 8 * place + 4, :] = turned[4 * quad : 4 * quad + 4, :]
            rows_ref[quad, 8 * place + 4 : 8 * place + 8, :] = jnp.zeros((4, length), F32)


def step_call(projected, dt_bias, a_log):
    length = projected.shape[0] - HALO
    line = pl.BlockSpec((1, 128), lambda g: (0, 0))
    return pl.pallas_call(
        step_kernel,
        grid=(1,),
        in_specs=[pl.BlockSpec((length + HALO, 128), lambda g: (0, CONV // 128)), line, line],
        out_specs=(
            pl.BlockSpec((QUADS, 40, length), lambda g: (0, 0, 0)),
            pl.BlockSpec((length, 128), lambda g: (0, 0)),
            pl.BlockSpec((8, 128), lambda g: (0, 0)),
        ),
        out_shape=(
            jax.ShapeDtypeStruct((QUADS, 40, length), F32),
            jax.ShapeDtypeStruct((length, 128), F32),
            jax.ShapeDtypeStruct((8, 128), F32),
        ),
        compiler_params=pltpu.CompilerParams(vmem_limit_bytes=VMEM_LIMIT),
        cost_estimate=COST,
        name="steps",
    )(projected, dt_bias, a_log)


def conv_kernel(
    share, v_ref, cw_ref, cb_ref, rows_ref, total_ref, *rest
):
    x_ref, slope_ref, b_ref, c_ref, bt_ref, ct_ref, state_ref, ext, weighted = rest[-9:]
    length = v_ref.shape[0] - HALO
    grid = pl.program_id(0)
    for plane in range(2):
        ext[plane] = v_ref[:, 128 * plane : 128 * plane + 128].astype(F32)

    def act(start):
        made = []
        for plane in range(2):
            lanes = slice(128 * plane, 128 * plane + 128)
            total = cb_ref[:, lanes] + cw_ref[0:1, lanes] * ext[plane, HALO - 3 + start : HALO - 3 + start + CHUNK, :]
            for tap in range(1, KW):
                at = HALO - 3 + tap + start
                total = total + cw_ref[tap : tap + 1, lanes] * ext[plane, at : at + CHUNK, :]
            sig = sigmoid(total)
            slope_ref[start : start + CHUNK, lanes] = (sig * (1.0 + total * (1.0 - sig))).astype(BF16)
            made.append(total * sig)
        return jnp.concatenate(made, axis=1)

    @pl.when(grid == 0)
    def _():
        for start in range(0, length, CHUNK):
            both = act(start)
            b_part, c_part = both[:, :STATE], both[:, STATE:]
            b_ref[start : start + CHUNK, :] = b_part.astype(BF16)
            c_ref[start : start + CHUNK, :] = c_part.astype(BF16)
            bt_ref[:, start : start + CHUNK] = b_part.T.astype(BF16)
            ct_ref[:, start : start + CHUNK] = c_part.T.astype(BF16)
        high, mid, low = split3(total_ref[0:1, :])
        row = iota((STATE, 128), 0) % share
        told = jnp.where(row == 0, high.astype(F32), jnp.where(row == 1, mid.astype(F32), jnp.where(row == 2, low.astype(F32), 0.0)))
        state_ref[:, :128] = told.astype(BF16)
        state_ref[:, 128:] = jnp.zeros((STATE, QUAD - 128), BF16)

    @pl.when(grid > 0)
    def _():
        cols = columns_of(rows_ref[0])
        for start in range(0, length, CHUNK):
            x_part = act(start)
            x_ref[start : start + CHUNK, :] = x_part.astype(BF16)
            _, left = spread(cols[start : start + CHUNK], 16)
            weighted[start : start + CHUNK, :] = (x_part * left).astype(BF16)
        state_ref[...] = mm(bt_ref[...], weighted[...]).astype(BF16)


def conv_call(ranks, v, conv_weight, conv_bias, rows, total, after):
    length = v.shape[0] - HALO
    last = QUADS
    block = lambda g: (0, (g + last) % (last + 1))
    quad = lambda g: (0, jnp.maximum(g - 1, 0))
    whole = lambda g: (0, 0)
    return pl.pallas_call(
        functools.partial(conv_kernel, STATE // ranks),
        grid=(last + 1,),
        in_specs=[
            pl.BlockSpec((length + HALO, QUAD), block),
            pl.BlockSpec((KW, QUAD), block),
            pl.BlockSpec((1, QUAD), block),
            pl.BlockSpec((1, 40, length), lambda g: (jnp.maximum(g - 1, 0), 0, 0)),
            pl.BlockSpec((8, 128), whole),
        ]
        + [pl.BlockSpec(memory_space=pl.ANY)] * len(after),
        out_specs=[
            pl.BlockSpec((length, QUAD), quad),
            pl.BlockSpec((length, QUAD), block),
            pl.BlockSpec((length, STATE), whole),
            pl.BlockSpec((length, STATE), whole),
            pl.BlockSpec((STATE, length), whole),
            pl.BlockSpec((STATE, length), whole),
            pl.BlockSpec((STATE, QUAD), block),
        ],
        scratch_shapes=[pltpu.VMEM((2, length + HALO, 128), F32), pltpu.VMEM((length, QUAD), BF16)],
        out_shape=[
            jax.ShapeDtypeStruct((length, INNER), BF16),
            jax.ShapeDtypeStruct((length, CONV), BF16),
            jax.ShapeDtypeStruct((length, STATE), BF16),
            jax.ShapeDtypeStruct((length, STATE), BF16),
            jax.ShapeDtypeStruct((STATE, length), BF16),
            jax.ShapeDtypeStruct((STATE, length), BF16),
            jax.ShapeDtypeStruct((STATE, CONV), BF16),
        ],
        compiler_params=pltpu.CompilerParams(vmem_limit_bytes=VMEM_LIMIT),
        cost_estimate=COST,
        name="conv_states",
    )(v, conv_weight, conv_bias, rows, total, *after)


def carry_kernel(ranks, backward, in_ref, *rest):
    share = STATE // ranks
    if backward:
        total_ref, out_ref = rest[0], rest[-1]
        decays = total_ref[...]
    else:
        out_ref, total_ref = rest[-2:]
        for place in range(ranks):
            told = in_ref[place * share : (place + 1) * share, INNER : INNER + 128].astype(F32)
            total_ref[place : place + 1, :] = told[0:1] + told[1:2] + told[2:3]
        decays = total_ref[...]
    wide = mm_exact(decays, head_ones())
    carry = jnp.zeros((share, INNER), F32)
    for place in range(ranks - 1, -1, -1) if backward else range(ranks):
        part = slice(place * share, (place + 1) * share)
        out_ref[part, :] = carry.astype(BF16)
        carry = wide[place : place + 1] * carry + in_ref[part, :INNER].astype(F32)


def carry_call(ranks, states, totals=None, after=()):
    backward = totals is not None
    vmem = pl.BlockSpec(memory_space=pltpu.VMEM)
    outs = [jax.ShapeDtypeStruct((STATE, INNER), BF16)]
    args = [states] + ([totals] if backward else [])
    if not backward:
        outs.append(jax.ShapeDtypeStruct((ranks, 128), F32))
    return pl.pallas_call(
        functools.partial(carry_kernel, ranks, backward),
        in_specs=[vmem] * len(args) + [pl.BlockSpec(memory_space=pl.ANY)] * len(after),
        out_specs=[vmem] * len(outs),
        out_shape=outs,
        compiler_params=pltpu.CompilerParams(vmem_limit_bytes=VMEM_LIMIT),
        cost_estimate=COST,
        name="carry_back" if backward else "carry",
    )(*args, *after)


def inside_kernel(x_ref, b_ref, c_ref, bt_ref, rows_ref, skip_ref, y_ref, scores, state):
    length = x_ref.shape[0]
    grid = pl.program_id(0)

    @pl.when(grid == 0)
    def _():
        for start in range(0, length, CHUNK):
            part = slice(start, start + CHUNK)
            scores[part, :] = mm_nt(c_ref[part, :], b_ref[part, :])

    cols = columns_of(rows_ref[0])
    lower = iota((CHUNK, CHUNK), 0) >= iota((CHUNK, CHUNK), 1)
    first = iota((CHUNK, 128), 1) < HEAD_DIM
    for start in range(0, length, CHUNK):
        part = slice(start, start + CHUNK)
        x_f = x_ref[part, :].astype(F32)
        wide, cum = spread(cols[part], 0)
        _, step = spread(cols[part], 8)
        weights = []
        for head in range(4):
            cum_row = rows_ref[0, head : head + 1, part]
            step_row = rows_ref[0, 8 + head : 9 + head, part]
            fade = jnp.exp(jnp.where(lower, wide[head] - cum_row, -1e30))
            weights.append((scores[part, :] * fade * step_row).astype(BF16))
        pieces = []
        for pair in range(2):
            x_pair = x_f[:, 128 * pair : 128 * pair + 128]
            both = jnp.concatenate([jnp.where(first, x_pair, 0.0), jnp.where(first, 0.0, x_pair)], axis=0)
            pieces.append(mm(jnp.concatenate(weights[2 * pair : 2 * pair + 2], axis=1), both.astype(BF16)))
        y_part = jnp.concatenate(pieces, axis=1) + skip_ref[...] * x_f
        if start > 0:
            y_part = y_part + jnp.exp(cum) * mm(c_ref[part, :], state[...].astype(BF16))
        y_ref[part, :] = y_part
        if start + CHUNK < length:
            end = cum[CHUNK - 1 : CHUNK]
            fresh = mm(bt_ref[:, part], (x_f * (jnp.exp(end - cum) * step)).astype(BF16))
            state[...] = fresh if start == 0 else jnp.exp(end) * state[...] + fresh


def inside_call(x_act, b_act, c_act, b_turned, rows, skip_wide):
    length = x_act.shape[0]
    whole = lambda g: (0, 0)
    quad = lambda g: (0, g)
    return pl.pallas_call(
        inside_kernel,
        grid=(QUADS,),
        in_specs=[
            pl.BlockSpec((length, QUAD), quad),
            pl.BlockSpec((length, STATE), whole),
            pl.BlockSpec((length, STATE), whole),
            pl.BlockSpec((STATE, length), whole),
            pl.BlockSpec((1, 40, length), lambda g: (g, 0, 0)),
            pl.BlockSpec((1, QUAD), quad),
        ],
        out_specs=pl.BlockSpec((length, QUAD), quad),
        out_shape=jax.ShapeDtypeStruct((length, INNER), F32),
        scratch_shapes=[pltpu.VMEM((length, CHUNK), F32), pltpu.VMEM((STATE, QUAD), F32)],
        compiler_params=pltpu.CompilerParams(vmem_limit_bytes=VMEM_LIMIT),
        cost_estimate=COST,
        name="ssd_inside",
    )(x_act, b_act, c_act, b_turned, rows, skip_wide)


def gate_kernel(
    y_ref, gate_ref, dn_ref, c_ref, ct_ref, ecd_ref, gain_ref, sin_ref,
    normed_ref, dgate_ref, dm_ref, dgain_ref, out_ref, ones, ecd, gated, silu, slope, back,
):
    grid = pl.program_id(0)

    @pl.when(grid == 0)
    def _():
        ones[...] = head_ones()
        back[...] = jnp.zeros_like(back)
        dgain_ref[...] = jnp.zeros_like(dgain_ref)

    high, mid, _ = split3(ecd_ref[...])
    squares = jnp.zeros((CHUNK, QUAD), F32)
    product = jnp.zeros((CHUNK, QUAD), F32)
    for at in range(0, INNER, QUAD):
        lanes = slice(at, at + QUAD)
        grown = mm(high, ones[:, lanes]) + mm(mid, ones[:, lanes])
        ecd[:, lanes] = grown
        mixed = y_ref[:, lanes] + grown * mm(c_ref[...], sin_ref[:, lanes])
        mixed = mixed.astype(BF16).astype(F32)
        gate = gate_ref[:, lanes].astype(F32)
        sig = sigmoid(gate)
        open_part = gate * sig
        value = mixed * open_part
        silu[:, lanes] = open_part
        slope[:, lanes] = mixed * (sig * (1.0 + gate * (1.0 - sig)))
        gated[:, lanes] = value
        squares = squares + value * value
        product = product + dn_ref[:, lanes] * gain_ref[:, lanes] * value
    inverse = lax.rsqrt(jnp.sum(squares, axis=1, keepdims=True) * (1.0 / INNER) + EPSILON)
    shift = inverse * inverse * inverse * (jnp.sum(product, axis=1, keepdims=True) * (1.0 / INNER))
    inverse = jnp.broadcast_to(inverse, (CHUNK, QUAD))
    shift = jnp.broadcast_to(shift, (CHUNK, QUAD))
    for at in range(0, INNER, QUAD):
        lanes = slice(at, at + QUAD)
        value = gated[:, lanes]
        scaled = value * inverse
        gain = gain_ref[:, lanes]
        dn = dn_ref[:, lanes]
        normed_ref[:, lanes] = (scaled * gain).astype(BF16)
        dgain_ref[:, lanes] += jnp.sum(dn * scaled, axis=0, keepdims=True)
        d_gated = inverse * (dn * gain) - value * shift
        dgate_ref[:, lanes] = (d_gated * slope[:, lanes]).astype(BF16)
        d_mixed = (d_gated * silu[:, lanes]).astype(BF16)
        dm_ref[:, lanes] = d_mixed
        back[:, lanes] += mm(ct_ref[...], (d_mixed.astype(F32) * ecd[:, lanes]).astype(BF16))

    @pl.when(grid == pl.num_programs(0) - 1)
    def _():
        out_ref[...] = back[...].astype(BF16)


def gate_call(y_inside, gate_in, d_normed, c_act, c_turned, ecd, out_gain, s_in):
    length = y_inside.shape[0]
    whole = lambda g: (0, 0)
    down = lambda g: (g, 0)
    wide = pl.BlockSpec((CHUNK, INNER), down)
    rows = jax.ShapeDtypeStruct((length, INNER), BF16)
    state = pl.BlockSpec((STATE, INNER), whole)
    line = pl.BlockSpec((1, INNER), whole)
    return pl.pallas_call(
        gate_kernel,
        grid=(length // CHUNK,),
        in_specs=[
            wide,
            wide,
            wide,
            pl.BlockSpec((CHUNK, STATE), down),
            pl.BlockSpec((STATE, CHUNK), lambda g: (0, g)),
            pl.BlockSpec((CHUNK, 128), down),
            line,
            state,
        ],
        out_specs=[wide, wide, wide, line, state],
        out_shape=[rows, rows, rows, jax.ShapeDtypeStruct((1, INNER), F32), jax.ShapeDtypeStruct((STATE, INNER), BF16)],
        scratch_shapes=[pltpu.VMEM((128, INNER), BF16)]
        + [pltpu.VMEM((CHUNK, INNER), F32)] * 4
        + [pltpu.VMEM((STATE, INNER), F32)],
        compiler_params=pltpu.CompilerParams(vmem_limit_bytes=VMEM_LIMIT),
        cost_estimate=COST,
        name="gated_norm",
    )(y_inside, gate_in, d_normed, c_act, c_turned, ecd, out_gain, s_in)


def back_kernel(x_ref, dm_ref, slope_ref, v_ref, cw_ref, b_ref, c_ref, bt_ref, ct_ref, rows_ref, skip_ref, sin_ref, rin_ref, *rest):
    dv_ref, sums_ref, heads_ref, scores, d_scores, d_b, d_c, states, back, grads, ext, d_step = rest[-12:]
    length = x_ref.shape[0]
    chunks = length // CHUNK
    grid = pl.program_id(0)

    @pl.when(grid == 0)
    def _():
        for start in range(0, length, CHUNK):
            part = slice(start, start + CHUNK)
            scores[part, :] = mm_nt(b_ref[part, :], c_ref[part, :])
        d_scores[...] = jnp.zeros_like(d_scores)
        d_b[...] = jnp.zeros_like(d_b)
        d_c[...] = jnp.zeros_like(d_c)
        d_step[...] = jnp.zeros_like(d_step)
        grads[:, 0:HALO, :] = jnp.zeros((2, HALO, 128), F32)
        grads[:, HALO + length :, :] = jnp.zeros((2, HALO, 128), F32)

    def finish(extra):
        for plane in range(2):
            lanes = slice(128 * plane, 128 * plane + 128)
            ext[plane] = v_ref[:, lanes].astype(F32)
            total = [jnp.zeros((8, 128), F32)] * (KW + 1)
            for start in range(0, length, CHUNK):
                here = grads[plane, HALO + start : HALO + start + CHUNK, :]
                for tap in range(KW):
                    at = HALO - 3 + tap + start
                    total[tap] = total[tap] + fold_rows(here * ext[plane, at : at + CHUNK, :])
                total[KW] = total[KW] + fold_rows(here)
            for at, rows in enumerate(total):
                sums_ref[at : at + 1, lanes] = jnp.sum(rows, axis=0, keepdims=True)
            for start in [0] + list(range(HALO, HALO + length, CHUNK)):
                count = HALO if start == 0 else CHUNK
                value = cw_ref[KW - 1 : KW, lanes] * grads[plane, start : start + count, :]
                for tap in range(KW - 1):
                    at = start + KW - 1 - tap
                    value = value + cw_ref[tap : tap + 1, lanes] * grads[plane, at : at + count, :]
                place = length if start == 0 else start - HALO
                dv_ref[place : place + count, lanes] = value.astype(BF16)
        sums_ref[KW + 1 : KW + 2, :] = extra
        sums_ref[KW + 2 : 8, :] = jnp.zeros((8 - KW - 2, QUAD), F32)

    def keep(start, value):
        for plane in range(2):
            grads[plane, HALO + start : HALO + start + CHUNK, :] = value[:, 128 * plane : 128 * plane + 128]

    @pl.when(grid < QUADS)
    def _():
        cols = columns_of(rows_ref[0])
        upper = iota((CHUNK, CHUNK), 0) <= iota((CHUNK, CHUNK), 1)
        first = iota((CHUNK, 128), 1) < HEAD_DIM
        lane = iota((CHUNK, 128), 1)
        line = iota((8, 128), 0)
        head_of = iota((QUAD, 128), 0) >> 6
        ones_v = jnp.where(iota((QUAD, 128), 1) == head_of + 8, 1.0, 0.0).astype(BF16)
        ones_u = jnp.where(iota((QUAD, 128), 1) == head_of + 16, 1.0, 0.0).astype(BF16)
        square = (CHUNK, CHUNK)
        later = jnp.where(iota(square, 0) >= iota(square, 1), 1.0, 0.0).astype(BF16)
        before = jnp.where(iota(square, 0) < iota(square, 1), 1.0, 0.0).astype(BF16)
        skip = skip_ref[...]
        back[...] = rin_ref[...].astype(F32)
        state = sin_ref[...].astype(F32)
        for chunk in range(chunks):
            part = slice(chunk * CHUNK, chunk * CHUNK + CHUNK)
            states[chunk] = state
            if chunk + 1 < chunks:
                _, cum = spread(cols[part], 0)
                _, step = spread(cols[part], 8)
                end = cum[CHUNK - 1 : CHUNK]
                fed = (x_ref[part, :].astype(F32) * (jnp.exp(end - cum) * step)).astype(BF16)
                state = jnp.exp(end) * state + mm(bt_ref[:, part], fed)
        skip_sum = jnp.zeros((1, QUAD), F32)
        bias_sum = jnp.zeros((8, 1), F32)
        rate_sum = jnp.zeros((8, 1), F32)
        for chunk in range(chunks - 1, -1, -1):
            part = slice(chunk * CHUNK, chunk * CHUNK + CHUNK)
            x_f = x_ref[part, :].astype(F32)
            dm = dm_ref[part, :]
            dm_f = dm.astype(F32)
            cum_wide, cum = spread(cols[part], 0)
            step_wide, step = spread(cols[part], 8)
            end = cum[CHUNK - 1 : CHUNK]
            after = back[...]
            after_low = after.astype(BF16)
            state = states[chunk]
            left = jnp.exp(end - cum)
            grown = dm_f * jnp.exp(cum)
            grown_low = grown.astype(BF16)
            faded = x_f * left
            from_after = mm(b_ref[part, :], after_low)
            from_state = mm(c_ref[part, :], state.astype(BF16))
            d_b[part, :] += mm_nt((faded * step).astype(BF16), after_low)
            d_c[part, :] += mm_nt(grown_low, state.astype(BF16))
            marks = mm((grown * from_state).astype(BF16), ones_v) + mm((faded * from_after).astype(BF16), ones_u)
            pair_sum = jnp.zeros((8, CHUNK), F32)
            crossing = jnp.zeros((8, 1), F32)
            cross = jnp.sum(state * after, axis=0, keepdims=True) * jnp.exp(end)
            pieces = []
            for pair in range(2):
                x_pair = x_f[:, 128 * pair : 128 * pair + 128]
                dm_pair = dm_f[:, 128 * pair : 128 * pair + 128]
                x_both = jnp.concatenate([jnp.where(first, x_pair, 0.0), jnp.where(first, 0.0, x_pair)], axis=0)
                dm_both = jnp.concatenate([jnp.where(first, dm_pair, 0.0), jnp.where(first, 0.0, dm_pair)], axis=0)
                d_weights = mm_nt(x_both.astype(BF16), dm[:, 128 * pair : 128 * pair + 128])
                kept = []
                for half in range(2):
                    head = 2 * pair + half
                    cum_row = rows_ref[0, head : head + 1, part]
                    fade = jnp.exp(jnp.where(upper, cum_row - cum_wide[head], -1e30))
                    faded_grad = d_weights[half * CHUNK : half * CHUNK + CHUNK] * fade
                    d_scores[part, :] += faded_grad * step_wide[head]
                    joint = faded_grad * scores[part, :]
                    marks = marks + jnp.where(lane == head, jnp.sum(joint, axis=1, keepdims=True), 0.0)
                    row = jnp.sum(joint * step_wide[head], axis=0, keepdims=True)
                    pair_sum = pair_sum + jnp.where(line == head, row, 0.0)
                    kept.append((scores[part, :] * fade).astype(BF16))
                    low, high = 64 * head, 64 * head + 64
                    here = (iota((1, QUAD), 1) >= low) & (iota((1, QUAD), 1) < high)
                    amount = jnp.sum(jnp.where(here, cross, 0.0), axis=1, keepdims=True)
                    crossing = crossing + jnp.where(iota((8, 1), 0) == head, amount, 0.0)
                pieces.append(mm(jnp.concatenate(kept, axis=1), dm_both.astype(BF16)))
            direct = jnp.concatenate(pieces, axis=1) + left * from_after
            d_x = step * direct + skip * dm_f
            keep(chunk * CHUNK, d_x * slope_ref[part, :].astype(F32))
            skip_sum = skip_sum + jnp.sum(x_f * dm_f, axis=0, keepdims=True)
            back[...] = jnp.exp(end) * after + mm(ct_ref[:, part], grown_low)
            marks = marks.T
            within, carried, outward = marks[0:8], marks[8:16], marks[16:24]
            step_rows = rows_ref[0, 8:16, part]
            change = pair_sum - step_rows * within + carried
            decay = mm_exact(change, later) + mm_exact(step_rows * outward, before) + crossing
            d_raw = (within + outward + rows_ref[0, 32:40, part] * decay) * rows_ref[0, 24:32, part]
            d_step[pl.ds(pl.multiple_of(grid * 8, 8), 8), part] = d_raw
            bias_sum = bias_sum + jnp.sum(d_raw, axis=1, keepdims=True)
            rate_sum = rate_sum + jnp.sum(step_rows * decay, axis=1, keepdims=True)
        heads_ref[0, 0:8, :] = jnp.broadcast_to(bias_sum, (8, 128))
        heads_ref[0, 8:16, :] = jnp.broadcast_to(rate_sum, (8, 128))
        finish(skip_sum)

    @pl.when(grid == QUADS)
    def _():
        for start in range(0, length, CHUNK):
            part = slice(start, start + CHUNK)
            low = d_scores[part, :].astype(BF16)
            into_b = d_b[part, :] + mm(low, c_ref[part, :])
            into_c = d_c[part, :] + mm(d_scores[part, :].T.astype(BF16), b_ref[part, :])
            both = jnp.concatenate([into_b, into_c], axis=1)
            keep(start, both * slope_ref[part, :].astype(F32))
        finish(jnp.zeros((1, QUAD), F32))

    @pl.when(grid == QUADS + 1)
    def _():
        row, column = iota((128, QUAD), 0), iota((128, QUAD), 1)
        pick = (column < HEADS) & (row == 8 * (column >> 2) + (column & 3))
        turned = d_step[...].T.astype(BF16)
        dv_ref[length:, :] = jnp.zeros((HALO, QUAD), BF16)
        dv_ref[0:length, :] = mm(turned, jnp.where(pick, 1.0, 0.0).astype(BF16)).astype(BF16)


def back_call(x_act, d_mixed, slope, v, conv_weight, b_act, c_act, b_turned, c_turned, rows, skip_wide, s_in, r_in, after):
    length = x_act.shape[0]
    whole = lambda g: (0, 0)
    quad = lambda g: (0, jnp.minimum(g, QUADS - 1))
    block = lambda g: (0, jnp.minimum(g, QUADS))
    lead = lambda g: (jnp.minimum(g, QUADS - 1), 0, 0)
    return pl.pallas_call(
        back_kernel,
        grid=(QUADS + 2,),
        in_specs=[
            pl.BlockSpec((length, QUAD), quad),
            pl.BlockSpec((length, QUAD), quad),
            pl.BlockSpec((length, QUAD), block),
            pl.BlockSpec((length + HALO, QUAD), block),
            pl.BlockSpec((KW, QUAD), block),
            pl.BlockSpec((length, STATE), whole),
            pl.BlockSpec((length, STATE), whole),
            pl.BlockSpec((STATE, length), whole),
            pl.BlockSpec((STATE, length), whole),
            pl.BlockSpec((1, 40, length), lead),
            pl.BlockSpec((1, QUAD), quad),
            pl.BlockSpec((STATE, QUAD), quad),
            pl.BlockSpec((STATE, QUAD), quad),
        ]
        + [pl.BlockSpec(memory_space=pl.ANY)] * len(after),
        out_specs=[
            pl.BlockSpec((length + HALO, QUAD), lambda g: (0, g)),
            pl.BlockSpec((8, QUAD), block),
            pl.BlockSpec((1, 16, 128), lead),
        ],
        scratch_shapes=[
            pltpu.VMEM((length, CHUNK), F32),
            pltpu.VMEM((length, CHUNK), F32),
            pltpu.VMEM((length, STATE), F32),
            pltpu.VMEM((length, STATE), F32),
            pltpu.VMEM((length // CHUNK, STATE, QUAD), F32),
            pltpu.VMEM((STATE, QUAD), F32),
            pltpu.VMEM((2, length + 2 * HALO, 128), F32),
            pltpu.VMEM((2, length + HALO, 128), F32),
            pltpu.VMEM((128, length), F32),
        ],
        out_shape=[
            jax.ShapeDtypeStruct((length + HALO, CONV + QUAD), BF16),
            jax.ShapeDtypeStruct((8, CONV), F32),
            jax.ShapeDtypeStruct((QUADS, 16, 128), F32),
        ],
        compiler_params=pltpu.CompilerParams(vmem_limit_bytes=VMEM_LIMIT),
        cost_estimate=COST,
        name="ssd_back",
    )(x_act, d_mixed, slope, v, conv_weight, b_act, c_act, b_turned, c_turned, rows, skip_wide, s_in, r_in, *after)


def weight_kernel(height, halves, place_ref, x_ref, *rest):
    piece_refs, (out_ref, w_ref) = rest[:-2], rest[-2:]
    block = w_ref.shape[0]
    if halves:
        grid = pl.program_id(0)
        lower = grid < pl.num_programs(0) // 2

        @pl.when(lower == (place_ref[len(piece_refs)] == 0))
        def _():
            for at, piece_ref in enumerate(piece_refs):
                if at < 2 or at % 2 == 0:
                    w_ref[:, pl.ds(pl.multiple_of(place_ref[at] * height, 128), height)] = piece_ref[...]

        @pl.when(lower != (place_ref[len(piece_refs)] == 0))
        def _():
            for at, piece_ref in enumerate(piece_refs):
                if at < 2 or at % 2 == 1:
                    w_ref[:, pl.ds(pl.multiple_of(place_ref[at] * height, 128), height)] = piece_ref[...]
    else:
        for at, piece_ref in enumerate(piece_refs):
            w_ref[:, pl.ds(pl.multiple_of(place_ref[at] * height, 128), height)] = piece_ref[...]
    out_ref[...] = mm_nt(x_ref[...], w_ref[...]).astype(BF16)


def weight_call(x, pieces, places, width, block, halves, name):
    rows, depth = x.shape
    height = pieces[0].shape[1]
    steps = width // block
    half = steps // 2

    def spec(at):
        if not halves or at < 2:
            return pl.BlockSpec((block, height), lambda g, place: (g, 0))
        return pl.BlockSpec((block, height), lambda g, place: (g % half, 0))

    grid_spec = pltpu.PrefetchScalarGridSpec(
        num_scalar_prefetch=1,
        grid=(steps,),
        in_specs=[pl.BlockSpec((rows, depth), lambda g, place: (0, 0))] + [spec(at) for at in range(len(pieces))],
        out_specs=[
            pl.BlockSpec((rows, block), lambda g, place: (0, g)),
            pl.BlockSpec((block, depth), lambda g, place: (g, 0)),
        ],
    )
    return pl.pallas_call(
        functools.partial(weight_kernel, height, halves),
        grid_spec=grid_spec,
        out_shape=[jax.ShapeDtypeStruct((rows, width), BF16), jax.ShapeDtypeStruct((width, depth), BF16)],
        compiler_params=pltpu.CompilerParams(vmem_limit_bytes=VMEM_LIMIT),
        cost_estimate=COST,
        name=name,
    )(places, x, *pieces)


def weight_back_kernel(per, place_ref, g_ref, *rest):
    piece_refs, (out_ref, w_ref) = rest[:-2], rest[-2:]
    for at, piece_ref in enumerate(piece_refs):

        @pl.when(pl.program_id(0) // per == at)
        def _():
            w_ref[...] = piece_ref[...]
            out_ref[...] = mm_nt(g_ref[...], piece_ref[...])


def weight_back_call(g, pieces, places):
    rows, width = g.shape
    block = 384
    per = pieces[0].shape[0] // block
    steps = per * len(pieces)
    total = steps * block
    step_of = lambda at: lambda k, place: (jnp.clip(k - at * per, 0, per - 1), 0)
    target = lambda k, place: place[k // per] * per + k % per
    grid_spec = pltpu.PrefetchScalarGridSpec(
        num_scalar_prefetch=1,
        grid=(steps,),
        in_specs=[pl.BlockSpec((rows, width), lambda k, place: (0, 0))]
        + [pl.BlockSpec((block, width), step_of(at)) for at in range(len(pieces))],
        out_specs=[
            pl.BlockSpec((rows, block), lambda k, place: (0, target(k, place))),
            pl.BlockSpec((block, width), lambda k, place: (target(k, place), 0)),
        ],
    )
    return pl.pallas_call(
        functools.partial(weight_back_kernel, per),
        grid_spec=grid_spec,
        out_shape=[jax.ShapeDtypeStruct((rows, total), F32), jax.ShapeDtypeStruct((total, width), BF16)],
        compiler_params=pltpu.CompilerParams(vmem_limit_bytes=VMEM_LIMIT),
        cost_estimate=COST,
        name="d_normed_out",
    )(places, g, *pieces)


def pick_kernel(parts, table_ref, *rest):
    ins, outs = rest[: 4 * parts], rest[-3 * parts :]
    for part in range(parts):
        own, other, own_halo, other_halo = ins[4 * part : 4 * part + 4]
        own_out, other_out, halo_out = outs[3 * part : 3 * part + 3]
        own_out[...] = own[...]
        other_out[...] = other[...]
        halo_out[:, :, :HALO] = own_halo[...]
        halo_out[:, :, HALO:] = other_halo[...]


def pick_call(table, own, other, own_halo, other_halo, after):
    parts, blocks = table.shape
    _, height, length = own.shape
    in_specs, out_specs, shapes = [], [], []
    for part in range(parts):
        pick = functools.partial(lambda part, g, table_ref: (table_ref[part, g], 0, 0), part)
        here = lambda g, *_: (g, 0, 0)
        in_specs += [pl.BlockSpec((1, height, length), pick)] * 2 + [pl.BlockSpec((1, height, HALO), pick)] * 2
        out_specs += [pl.BlockSpec((1, height, length), here)] * 2 + [pl.BlockSpec((1, height, 2 * HALO), here)]
        shapes += [jax.ShapeDtypeStruct((blocks, height, length), BF16)] * 2
        shapes += [jax.ShapeDtypeStruct((blocks, height, 2 * HALO), BF16)]
    in_specs += [pl.BlockSpec(memory_space=pl.ANY)] * len(after)
    made = pl.pallas_call(
        functools.partial(pick_kernel, parts),
        grid_spec=pltpu.PrefetchScalarGridSpec(num_scalar_prefetch=1, grid=(blocks,), in_specs=in_specs, out_specs=out_specs),
        out_shape=shapes,
        compiler_params=pltpu.CompilerParams(vmem_limit_bytes=VMEM_LIMIT),
        cost_estimate=COST,
        name="pick_rows",
    )(table, *([own, other, own_halo, other_halo] * parts), *after)
    return [[array.reshape(blocks * height, -1) for array in made[3 * part : 3 * part + 3]] for part in range(parts)]


def grad_kernel(halo, *refs):
    kept_ref, sent_ref = refs[-2:]
    if halo:
        own, other, edge, right, right_other, edge_right, edge_other = refs[:7]
    else:
        own, other, right, right_other = refs[:4]
    total = mm(own[...], right[...]) + mm(other[...], right_other[...])
    if halo:
        total = total + mm(edge[...], jnp.concatenate([edge_right[...], edge_other[...]], axis=0))
    half = total.shape[0] // 2
    kept_ref[...] = total[:half].astype(BF16)
    sent_ref[...] = total[half:].astype(BF16)


def grad_call(left, right, right_other, first, width, block, halo, name, after):
    own, other, edge = left
    rows, length = own.shape
    whole = lambda g: (0, 0)
    column = lambda g: (0, first // block + g)
    below = lambda g: (length // HALO, first // block + g)
    specs = [pl.BlockSpec((rows, length), whole)] * 2
    args = [own, other]
    if halo:
        specs.append(pl.BlockSpec((rows, 2 * HALO), whole))
        args.append(edge)
    specs += [pl.BlockSpec((length, block), column)] * 2
    args += [right, right_other]
    if halo:
        specs += [pl.BlockSpec((HALO, block), below)] * 2
        args += [right, right_other]
    specs += [pl.BlockSpec(memory_space=pl.ANY)] * len(after)
    args += list(after)
    return pl.pallas_call(
        functools.partial(grad_kernel, halo),
        grid=(width // block,),
        in_specs=specs,
        out_specs=[pl.BlockSpec((rows // 2, block), lambda g: (0, g))] * 2,
        out_shape=[jax.ShapeDtypeStruct((rows // 2, width), BF16)] * 2,
        compiler_params=pltpu.CompilerParams(vmem_limit_bytes=VMEM_LIMIT),
        cost_estimate=COST,
        name=name,
    )(*args)


def fold_kernel(parts, groups, last, *refs):
    ins, outs = refs[: 2 * parts * groups], refs[-(1 if last else 2 * parts) :]
    for part in range(parts):
        at = 0
        for group in range(groups):
            kept, got = ins[2 * (part * groups + group)], ins[2 * (part * groups + group) + 1]
            width = kept.shape[1]
            total = kept[...].astype(F32) + got[...].astype(F32)
            if last:
                gate = INNER // parts
                other = width - gate
                outs[0][:, part * gate : (part + 1) * gate] = total[:, :gate]
                begin = INNER + part * other
                end = min(begin + other, outs[0].shape[1])
                outs[0][:, begin:end] = total[:, gate : gate + end - begin]
            else:
                half = total.shape[0] // 2
                outs[2 * part][:, at : at + width] = total[:half].astype(BF16)
                outs[2 * part + 1][:, at : at + width] = total[half:].astype(BF16)
            at += width


def fold_call(pairs, width, after=()):
    parts, groups = len(pairs), len(pairs[0])
    arrays = [array for part in pairs for pair in part for array in pair]
    vmem = pl.BlockSpec(memory_space=pltpu.VMEM)
    rows = arrays[0].shape[0]
    if width:
        shapes = [jax.ShapeDtypeStruct((rows, width), F32)]
    else:
        shapes = []
        for part in pairs:
            total = sum(kept.shape[1] for kept, _ in part)
            shapes += [jax.ShapeDtypeStruct((rows // 2, total), BF16)] * 2
    made = pl.pallas_call(
        functools.partial(fold_kernel, parts, groups, bool(width)),
        in_specs=[vmem] * len(arrays) + [pl.BlockSpec(memory_space=pl.ANY)] * len(after),
        out_specs=[vmem] * len(shapes),
        out_shape=shapes,
        compiler_params=pltpu.CompilerParams(vmem_limit_bytes=VMEM_LIMIT),
        cost_estimate=COST,
        name="fold",
    )(*arrays, *after)
    return made[0] if width else [(made[2 * part], made[2 * part + 1]) for part in range(parts)]


def residual_kernel(x_ref, w_ref, tokens_ref, *rest):
    out_ref = rest[-1]
    out_ref[0] = tokens_ref[0].astype(F32) + mm(x_ref[...], w_ref[...])


def residual_call(x, w, tokens, after=()):
    rows, depth = x.shape
    width = w.shape[1]
    block = 256
    whole = pl.BlockSpec((1, rows, block), lambda g: (0, 0, g))
    return pl.pallas_call(
        residual_kernel,
        grid=(width // block,),
        in_specs=[pl.BlockSpec((rows, depth), lambda g: (0, 0)), pl.BlockSpec((depth, block), lambda g: (0, g)), whole]
        + [pl.BlockSpec(memory_space=pl.ANY)] * len(after),
        out_specs=whole,
        out_shape=jax.ShapeDtypeStruct((1, rows, width), F32),
        compiler_params=pltpu.CompilerParams(vmem_limit_bytes=VMEM_LIMIT),
        cost_estimate=COST,
        name="block_out",
    )(x, w, tokens, *after)


def tokens_kernel(dg_ref, dv_ref, spill_ref, wg_ref, wv_ref, tokens_ref, cotan_ref, gain_ref, *rest):
    out_ref, dgain_ref, fixed, d_normed, inverse = rest[-5:]
    length = dg_ref.shape[0]
    block = wg_ref.shape[1]
    grid = pl.program_id(0)

    @pl.when(grid == 0)
    def _():
        fixed[...] = dv_ref[...]
        ends = dv_ref[length - HALO :, :].astype(F32) + spill_ref[...].astype(F32)
        fixed[length - HALO :, :] = ends.astype(BF16)
        for start in range(0, length, CHUNK):
            part = slice(start, start + CHUNK)
            values = tokens_ref[0, part, :].astype(F32)
            mean = jnp.sum(values * values, axis=1, keepdims=True) * (1.0 / D)
            inverse[part, :] = jnp.broadcast_to(lax.rsqrt(mean + EPSILON), (CHUNK, 128))

    lanes = pl.ds(pl.multiple_of(grid * block, block), block)
    total = mm(dg_ref[...], wg_ref[...]) + mm(fixed[...], wv_ref[...])
    d_normed[:, lanes] = total
    scaled = jnp.concatenate([inverse[...]] * (block // 128), axis=1) * tokens_ref[0, :, lanes].astype(F32)
    dgain_ref[...] = jnp.sum(total * scaled, axis=0, keepdims=True)

    @pl.when(grid == pl.num_programs(0) - 1)
    def _():
        for start in range(0, length, CHUNK):
            part = slice(start, start + CHUNK)
            values = tokens_ref[0, part, :].astype(F32)
            a = d_normed[part, :] * gain_ref[...]
            inv = inverse[part, 0:1]
            shift = inv * inv * inv * (jnp.sum(a * values, axis=1, keepdims=True) * (1.0 / D))
            out_ref[0, part, :] = cotan_ref[0, part, :].astype(F32) + inv * a - values * shift


def tokens_call(d_gate, d_v, spill, w_g, w_v, tokens, cotangent, gain, after):
    length = d_gate.shape[0]
    block = 256
    wide = w_v.shape[0]
    whole = lambda g: (0, 0)
    all_rows = pl.BlockSpec((1, length, D), lambda g: (0, 0, 0))
    return pl.pallas_call(
        tokens_kernel,
        grid=(D // block,),
        in_specs=[
            pl.BlockSpec((length, INNER), whole),
            pl.BlockSpec((length, wide), whole),
            pl.BlockSpec((HALO, wide), whole),
            pl.BlockSpec((INNER, block), lambda g: (0, g)),
            pl.BlockSpec((wide, block), lambda g: (0, g)),
            all_rows,
            all_rows,
            pl.BlockSpec((1, D), whole),
        ]
        + [pl.BlockSpec(memory_space=pl.ANY)] * len(after),
        out_specs=[all_rows, pl.BlockSpec((1, block), lambda g: (0, g))],
        out_shape=[jax.ShapeDtypeStruct((1, length, D), F32), jax.ShapeDtypeStruct((1, D), F32)],
        scratch_shapes=[pltpu.VMEM((length, wide), BF16), pltpu.VMEM((length, D), F32), pltpu.VMEM((length, 128), F32)],
        compiler_params=pltpu.CompilerParams(vmem_limit_bytes=VMEM_LIMIT),
        cost_estimate=COST,
        name="d_tokens",
    )(d_gate, d_v, spill, w_g, w_v, tokens, cotangent, gain, *after)


def on_device(
    ranks,
    shards,
    tokens,
    norm_gain,
    w_in,
    conv_weight,
    conv_bias,
    dt_bias,
    a_log,
    skip_gain,
    out_gain,
    w_out,
    cotangent,
):
    both = ("seq", "fsdp")
    rank = lax.axis_index("seq")
    shard = lax.axis_index("fsdp")

    def move(value, target):
        pairs = []
        for s in range(ranks):
            for f in range(shards):
                goal = target(s, f)
                if goal is not None:
                    pairs.append((s * shards + f, goal[0] * shards + goal[1]))
        return lax.ppermute(value, both, pairs)

    def across(value):
        return move(value, lambda s, f: (s, f ^ 1))

    def tie(value, *others):
        if others:
            value = lax.optimization_barrier((value,) + others)[0]
        return value

    def gather(value, crossed, middle, near):
        pieces = [(value, 0), (crossed, 1)] + near
        pieces += [(across(tie(piece, middle)), step ^ 1) for piece, step in near]
        return [piece for piece, _ in pieces], jnp.stack([shard ^ step for _, step in pieces]).astype(jnp.int32)

    def send_near(value):
        return [(move(value, lambda s, f: (s, f ^ step)), step) for step in range(2, shards, 2)]

    def gather_halves(value, crossed, middle):
        height = value.shape[0]
        side = rank & 1
        half = lax.dynamic_slice_in_dim(value, side * (height // 2), height // 2, 0)
        pairs = []
        for step in range(2, shards, 2):
            near = move(half, lambda s, f: (s, f ^ step))
            far = move(tie(near, *middle), lambda s, f: (s ^ 1, f))
            pairs += [(near, step), (far, step)]
        pieces = [(value, 0), (crossed, 1)] + pairs + [(across(piece), step ^ 1) for piece, step in pairs]
        places = [shard ^ step for _, step in pieces] + [side]
        return [piece for piece, _ in pieces], jnp.stack(places).astype(jnp.int32)

    def in_order(pieces, places, halves):
        height = pieces[0].shape[1]
        whole = jnp.zeros((pieces[0].shape[0], height * shards), pieces[0].dtype)
        for at, piece in enumerate(pieces):
            first = 0
            if halves and at >= 2:
                first = (places[-1] if at % 2 == 0 else 1 - places[-1]) * piece.shape[0]
            whole = lax.dynamic_update_slice(whole, piece, (first, places[at] * height))
        return [whole], jnp.zeros((1,), jnp.int32)

    def exchange(states):
        return lax.all_to_all(states, "seq", split_axis=0, concat_axis=0, tiled=True)

    halo = move(tokens[0, -HALO:], lambda s, f: (s + 1, f) if s + 1 < ranks else None)
    longer = jnp.concatenate([halo, tokens[0]], axis=0).astype(F32)
    inverse = lax.rsqrt(jnp.mean(longer * longer, axis=-1, keepdims=True) + EPSILON)
    normed_long = (longer * inverse * norm_gain).astype(BF16)
    normed = normed_long[HALO:]

    cotan = cotangent[0]
    turned = w_in.T
    width_v = CONV + QUAD
    own_v = jnp.pad(turned[INNER:], ((0, width_v - (turned.shape[0] - INNER)), (0, 0)))
    chip_bits = [("fsdp", bit) for bit in (2, 4, 8) if bit < shards]
    seq_bits = [("seq", bit) for bit in (1, 2, 4, 8) if bit < ranks]
    first_bits = [seq_bits[0], chip_bits[0], seq_bits[1]] if chip_bits else [seq_bits[0], seq_bits[1], seq_bits[0]]
    orders = []
    for part in range(3):
        lead = list(dict.fromkeys(first_bits[part:] + first_bits[:part]))
        orders.append(lead + [bit for bit in chip_bits + seq_bits if bit not in lead])
    chips = ranks * (shards // 2)
    table = []
    for order in orders:
        line = []
        for place in range(chips):
            s, f = rank, shard
            for at, (axis, bit) in enumerate(order):
                if place >> (len(order) - 1 - at) & 1:
                    s, f = (s ^ bit, f) if axis == "seq" else (s, f ^ bit)
            line.append(s * (shards // 2) + (f >> 1))
        table.append(jnp.stack(line))
    table = jnp.stack(table).astype(jnp.int32)

    def halves(turned):
        blocks = turned.reshape(chips, 2, -1, turned.shape[1])
        core = shard & 1
        return lax.dynamic_index_in_dim(blocks, core, 1, False), lax.dynamic_index_in_dim(blocks, 1 - core, 1, False)

    own, other = halves(normed.T)
    own_halo, other_halo = halves(normed_long[:HALO].T)
    lefts = pick_call(table, own, across(other), own_halo, across(other_halo), [])
    own_g = turned[:INNER]
    crossed_v, crossed_g, crossed_o = across(own_v), across(own_g), across(w_out)
    pieces_v, places_v = gather_halves(own_v, crossed_v, (lefts[0][0], crossed_v, crossed_g, crossed_o))

    def flip(axis, bit):
        return lambda s, f: (s ^ bit, f) if axis == "seq" else (s, f ^ bit)

    def first_terms(right, width, block, halo, name, *ahead):
        right_other = tie(across(right), *ahead)
        return [grad_call(lefts[part], right, right_other, part * width, width, block, halo, name, ()) for part in range(3)]

    def first_step(terms, *ahead):
        return [(kept, move(tie(sent, *ahead), flip(*orders[part][0]))) for part, (kept, sent) in enumerate(terms)]

    lanes_whole = w_in.shape[0] % 128 == 0
    if lanes_whole:
        projected, w_v = weight_call(normed_long, pieces_v, places_v, width_v, width_v // 4, True, "project_v")
    else:
        projected, w_v = weight_call(normed_long, *in_order(pieces_v, places_v, True), width_v, width_v // 4, False, "project_v")
    near_g = send_near(tie(own_g, pieces_v[2]))
    pieces_g, places = gather(own_g, crossed_g, projected, near_g)
    near_o = send_near(tie(w_out, near_g[0][0], projected))
    lanes = lambda vec: jnp.pad(vec, (0, 128 - HEADS)).reshape(1, 128)
    rows, ecd, decay_all = step_call(projected, lanes(dt_bias), lanes(a_log))
    v = projected
    made = conv_call(ranks, v, conv_weight, conv_bias.reshape(1, CONV), rows, decay_all, ())
    x_act, slope, b_act, c_act, b_turned, c_turned, states = made
    skip_wide = jnp.repeat(skip_gain, HEAD_DIM).reshape(1, INNER)
    y_inside = inside_call(x_act, b_act, c_act, b_turned, rows, skip_wide)
    carried, totals = carry_call(ranks, exchange(states), None, [y_inside])
    s_in = exchange(carried)
    pieces_o, _ = gather(w_out, crossed_o, carried, near_o)
    gate_pieces = (pieces_g, places) if lanes_whole else in_order(pieces_g, places, False)
    gate_in, w_g = weight_call(normed, *gate_pieces, INNER, 768, False, "project_gate")
    d_normed_out, w_o = weight_back_call(cotan, pieces_o, places)
    made = gate_call(y_inside, gate_in, d_normed_out, c_act, c_turned, ecd, out_gain.reshape(1, INNER), s_in)
    normed_out, d_gate, d_mixed, d_gain_out, states = made
    d_w_out = lax.dot_general(normed_out, cotan, TN, preferred_element_type=F32).astype(BF16)
    d_w_out_sum = lax.psum_scatter(d_w_out, both, scatter_dimension=0, tiled=True).astype(F32)
    block_out = residual_call(normed_out, w_o, tokens, [states])
    gate_terms = first_terms(d_gate, INNER // 3, 512, False, "d_w_gate")
    (carried,) = carry_call(ranks, exchange(states), totals, [d_w_out, block_out])
    r_in = exchange(carried)
    gate_parts = first_step(gate_terms, r_in)
    d_v_long, sums, heads = back_call(
        x_act, d_mixed, slope, v, conv_weight, b_act, c_act, b_turned, c_turned, rows, skip_wide, s_in, r_in, ()
    )
    d_v_long = tie(d_v_long, *[got for _, got in gate_parts])
    spill = move(d_v_long[tokens.shape[1] :], lambda s, f: (s - 1, f) if s > 0 else None)
    rest_parts = first_step(first_terms(d_v_long, (CONV + 128) // 3, 384, True, "d_w_rest", spill))
    d_tokens, d_norm_gain = tokens_call(
        d_gate, d_v_long, spill, w_g, w_v, tokens, cotangent, norm_gain.reshape(1, D), [kept for kept, _ in rest_parts]
    )

    d_skip = sums[KW + 1, :INNER].reshape(HEADS, HEAD_DIM).sum(axis=1)
    pieces = [
        d_norm_gain.reshape(-1),
        sums[:KW].reshape(-1),
        sums[KW],
        heads[:, 0:4, 0].reshape(-1),
        heads[:, 8:12, 0].reshape(-1) * -jnp.exp(a_log),
        d_skip,
        d_gain_out.reshape(-1),
    ]
    flat = jnp.concatenate(pieces)
    width = flat.shape[0]
    flat = jnp.pad(flat, (0, -width % 1024)).reshape(-1, 128)
    flat = flat + across(flat)
    small_bits = seq_bits[:1] + chip_bits + seq_bits[1:]
    flat = flat + move(flat, flip(*small_bits[0]))

    pairs = [[gate_parts[part], rest_parts[part]] for part in range(3)]
    for at in range(1, len(orders[0])):
        halves_now = fold_call(pairs, 0, [flat])
        pairs = [[(kept, move(sent, flip(*orders[part][at])))] for part, (kept, sent) in enumerate(halves_now)]
        flat = flat + move(tie(flat, halves_now[0][0]), flip(*small_bits[at]))
    d_w_in = fold_call(pairs, w_in.shape[1], [flat])
    flat = flat.reshape(-1)
    small, at = [], 0
    for piece in pieces:
        small.append(flat[at : at + piece.shape[0]])
        at += piece.shape[0]
    d_norm_gain, d_conv_weight, d_conv_bias, d_dt_bias, d_a_log, d_skip, d_gain_out = small
    return (
        block_out,
        d_tokens,
        d_norm_gain,
        d_w_in,
        d_conv_weight.reshape(KW, CONV),
        d_conv_bias,
        d_dt_bias,
        d_a_log,
        d_skip,
        d_gain_out,
        d_w_out_sum,
    )


def solution(mesh):
    split = P("fsdp", "seq", None)
    rows = P("fsdp", None)
    last = P(("seq", "fsdp"), None)
    return jax.shard_map(
        functools.partial(on_device, mesh.shape["seq"], mesh.shape["fsdp"]),
        mesh=mesh,
        in_specs=(split, P(), rows, P(), P(), P(), P(), P(), P(), rows, split),
        out_specs=(split, split, P(), last, P(), P(), P(), P(), P(), P(), last),
        check_vma=False,
    )
```

```python
import functools

import jax
import jax.numpy as jnp
from jax import lax
from jax.experimental import pallas as pl
from jax.experimental.pallas import tpu as pltpu
from jax.sharding import PartitionSpec as P

HEADS = 48
HEAD_DIM = 64
STATE = 128
KW = 4
INNER = 3072
D = 1536
CONV = INNER + 2 * STATE

EPSILON = 1e-05
CHUNK = 128
QUAD = 256
QUADS = INNER // QUAD
HALO = 16
VMEM_LIMIT = 56 * 1024 * 1024
LONG = pl.CostEstimate(flops=200000000000, bytes_accessed=1000000, transcendentals=0)
COST = pl.CostEstimate(flops=1000000, bytes_accessed=1000000, transcendentals=0)
F32 = jnp.float32
BF16 = jnp.bfloat16
HIGHEST = lax.Precision.HIGHEST
NT = (((1,), (1,)), ((), ()))
TN = (((0,), (0,)), ((), ()))


def iota(shape, axis):
    return lax.broadcasted_iota(jnp.int32, shape, axis)


def tie(value, *others):
    return lax.optimization_barrier((value,) + others)[0] if others else value


def mm(a, b):
    return jnp.dot(a, b, preferred_element_type=F32)


def mm_nt(a, b):
    return lax.dot_general(a, b, NT, preferred_element_type=F32)


def sigmoid(v):
    return 0.5 * jnp.tanh(0.5 * v) + 0.5


def split3(v):
    high = v.astype(BF16)
    rest = v - high.astype(F32)
    mid = rest.astype(BF16)
    low = (rest - mid.astype(F32)).astype(BF16)
    return high, mid, low


def mm_exact(v, ones):
    high, mid, low = split3(v)
    return mm(high, ones) + mm(mid, ones) + mm(low, ones)


def head_ones():
    return jnp.where((iota((128, INNER), 1) >> 6) == iota((128, INNER), 0), 1.0, 0.0).astype(BF16)


def two_heads(first, second):
    return jnp.where(iota((CHUNK, 128), 1) < HEAD_DIM, first, second)


def spread(cols, start):
    wide = [jnp.broadcast_to(cols[:, start + i : start + i + 1], (CHUNK, 128)) for i in range(4)]
    return wide, jnp.concatenate([two_heads(wide[0], wide[1]), two_heads(wide[2], wide[3])], axis=1)


def fold_rows(value):
    return jnp.sum(value.reshape(-1, 8, value.shape[1]), axis=0)


def columns_of(rows):
    count, length = rows.shape
    return jnp.concatenate([rows, jnp.zeros((128 - count, length), F32)], axis=0).T


def step_kernel(dt_ref, bias_ref, alog_ref, rows_ref, ecd_ref, total_ref):
    length = dt_ref.shape[0] - HALO
    raw = dt_ref[HALO:, :].astype(F32) + bias_ref[...]
    step = jnp.maximum(raw, 0.0) + jnp.log1p(jnp.exp(-jnp.abs(raw)))
    sig = 1.0 / (1.0 + jnp.exp(-raw))
    rate = -jnp.exp(alog_ref[...])
    pace = step * rate
    lower = jnp.where(iota((CHUNK, CHUNK), 0) >= iota((CHUNK, CHUNK), 1), 1.0, 0.0).astype(F32)
    inside, along = [], []
    offset = jnp.zeros((1, 128), F32)
    for start in range(0, length, CHUNK):
        part = jnp.dot(lower, pace[start : start + CHUNK], precision=HIGHEST, preferred_element_type=F32)
        inside.append(part)
        along.append(part + offset)
        offset = offset + part[CHUNK - 1 : CHUNK]
    cum = jnp.concatenate(inside, axis=0)
    along = jnp.concatenate(along, axis=0)
    ecd_ref[...] = jnp.exp(along)
    total_ref[...] = jnp.broadcast_to(jnp.exp(offset), (8, 128))
    left = jnp.exp(offset - along) * step
    for place, array in enumerate((cum, step, left, sig, jnp.broadcast_to(rate, (length, 128)))):
        turned = array.T
        for quad in range(QUADS):
            rows_ref[quad, 8 * place : 8 * place + 4, :] = turned[4 * quad : 4 * quad + 4, :]
            rows_ref[quad, 8 * place + 4 : 8 * place + 8, :] = jnp.zeros((4, length), F32)


def step_call(projected, dt_bias, a_log):
    length = projected.shape[0] - HALO
    line = pl.BlockSpec((1, 128), lambda g: (0, 0))
    return pl.pallas_call(
        step_kernel,
        grid=(1,),
        in_specs=[pl.BlockSpec((length + HALO, 128), lambda g: (0, CONV // 128)), line, line],
        out_specs=(
            pl.BlockSpec((QUADS, 40, length), lambda g: (0, 0, 0)),
            pl.BlockSpec((length, 128), lambda g: (0, 0)),
            pl.BlockSpec((8, 128), lambda g: (0, 0)),
        ),
        out_shape=(
            jax.ShapeDtypeStruct((QUADS, 40, length), F32),
            jax.ShapeDtypeStruct((length, 128), F32),
            jax.ShapeDtypeStruct((8, 128), F32),
        ),
        compiler_params=pltpu.CompilerParams(vmem_limit_bytes=VMEM_LIMIT),
        cost_estimate=COST,
        name="steps",
    )(projected, dt_bias, a_log)


def conv_kernel(
    share, v_ref, cw_ref, cb_ref, rows_ref, total_ref, *rest
):
    x_ref, slope_ref, b_ref, c_ref, bt_ref, ct_ref, state_ref, ext, weighted = rest[-9:]
    length = v_ref.shape[0] - HALO
    grid = pl.program_id(0)
    for plane in range(2):
        ext[plane] = v_ref[:, 128 * plane : 128 * plane + 128].astype(F32)

    def act(start):
        made = []
        for plane in range(2):
            lanes = slice(128 * plane, 128 * plane + 128)
            total = cb_ref[:, lanes] + cw_ref[0:1, lanes] * ext[plane, HALO - 3 + start : HALO - 3 + start + CHUNK, :]
            for tap in range(1, KW):
                at = HALO - 3 + tap + start
                total = total + cw_ref[tap : tap + 1, lanes] * ext[plane, at : at + CHUNK, :]
            sig = sigmoid(total)
            slope_ref[start : start + CHUNK, lanes] = (sig * (1.0 + total * (1.0 - sig))).astype(BF16)
            made.append(total * sig)
        return jnp.concatenate(made, axis=1)

    @pl.when(grid == 0)
    def _():
        for start in range(0, length, CHUNK):
            both = act(start)
            b_part, c_part = both[:, :STATE], both[:, STATE:]
            b_ref[start : start + CHUNK, :] = b_part.astype(BF16)
            c_ref[start : start + CHUNK, :] = c_part.astype(BF16)
            bt_ref[:, start : start + CHUNK] = b_part.T.astype(BF16)
            ct_ref[:, start : start + CHUNK] = c_part.T.astype(BF16)
        high, mid, low = split3(total_ref[0:1, :])
        row = iota((STATE, 128), 0) % share
        told = jnp.where(row == 0, high.astype(F32), jnp.where(row == 1, mid.astype(F32), jnp.where(row == 2, low.astype(F32), 0.0)))
        state_ref[:, :128] = told.astype(BF16)
        state_ref[:, 128:] = jnp.zeros((STATE, QUAD - 128), BF16)

    @pl.when(grid > 0)
    def _():
        cols = columns_of(rows_ref[0])
        for start in range(0, length, CHUNK):
            x_part = act(start)
            x_ref[start : start + CHUNK, :] = x_part.astype(BF16)
            _, left = spread(cols[start : start + CHUNK], 16)
            weighted[start : start + CHUNK, :] = (x_part * left).astype(BF16)
        state_ref[...] = mm(bt_ref[...], weighted[...]).astype(BF16)


def conv_call(ranks, v, conv_weight, conv_bias, rows, total, after):
    length = v.shape[0] - HALO
    last = QUADS
    block = lambda g: (0, (g + last) % (last + 1))
    quad = lambda g: (0, jnp.maximum(g - 1, 0))
    whole = lambda g: (0, 0)
    return pl.pallas_call(
        functools.partial(conv_kernel, STATE // ranks),
        grid=(last + 1,),
        in_specs=[
            pl.BlockSpec((length + HALO, QUAD), block),
            pl.BlockSpec((KW, QUAD), block),
            pl.BlockSpec((1, QUAD), block),
            pl.BlockSpec((1, 40, length), lambda g: (jnp.maximum(g - 1, 0), 0, 0)),
            pl.BlockSpec((8, 128), whole),
        ]
        + [pl.BlockSpec(memory_space=pl.ANY)] * len(after),
        out_specs=[
            pl.BlockSpec((length, QUAD), quad),
            pl.BlockSpec((length, QUAD), block),
            pl.BlockSpec((length, STATE), whole),
            pl.BlockSpec((length, STATE), whole),
            pl.BlockSpec((STATE, length), whole),
            pl.BlockSpec((STATE, length), whole),
            pl.BlockSpec((STATE, QUAD), block),
        ],
        scratch_shapes=[pltpu.VMEM((2, length + HALO, 128), F32), pltpu.VMEM((length, QUAD), BF16)],
        out_shape=[
            jax.ShapeDtypeStruct((length, INNER), BF16),
            jax.ShapeDtypeStruct((length, CONV), BF16),
            jax.ShapeDtypeStruct((length, STATE), BF16),
            jax.ShapeDtypeStruct((length, STATE), BF16),
            jax.ShapeDtypeStruct((STATE, length), BF16),
            jax.ShapeDtypeStruct((STATE, length), BF16),
            jax.ShapeDtypeStruct((STATE, CONV), BF16),
        ],
        compiler_params=pltpu.CompilerParams(vmem_limit_bytes=VMEM_LIMIT),
        cost_estimate=COST,
        name="conv_states",
    )(v, conv_weight, conv_bias, rows, total, *after)


def carry_kernel(ranks, backward, in_ref, *rest):
    share = STATE // ranks
    if backward:
        total_ref, out_ref = rest[0], rest[-1]
        decays = total_ref[...]
    else:
        out_ref, total_ref = rest[-2:]
        for place in range(ranks):
            told = in_ref[place * share : (place + 1) * share, INNER : INNER + 128].astype(F32)
            total_ref[place : place + 1, :] = told[0:1] + told[1:2] + told[2:3]
        decays = total_ref[...]
    wide = mm_exact(decays, head_ones())
    carry = jnp.zeros((share, INNER), F32)
    for place in range(ranks - 1, -1, -1) if backward else range(ranks):
        part = slice(place * share, (place + 1) * share)
        out_ref[part, :] = carry.astype(BF16)
        carry = wide[place : place + 1] * carry + in_ref[part, :INNER].astype(F32)


def carry_call(ranks, states, totals=None, after=()):
    backward = totals is not None
    vmem = pl.BlockSpec(memory_space=pltpu.VMEM)
    outs = [jax.ShapeDtypeStruct((STATE, INNER), BF16)]
    args = [states] + ([totals] if backward else [])
    if not backward:
        outs.append(jax.ShapeDtypeStruct((ranks, 128), F32))
    return pl.pallas_call(
        functools.partial(carry_kernel, ranks, backward),
        in_specs=[vmem] * len(args) + [pl.BlockSpec(memory_space=pl.ANY)] * len(after),
        out_specs=[vmem] * len(outs),
        out_shape=outs,
        compiler_params=pltpu.CompilerParams(vmem_limit_bytes=VMEM_LIMIT),
        cost_estimate=COST,
        name="carry_back" if backward else "carry",
    )(*args, *after)


def inside_kernel(x_ref, b_ref, c_ref, bt_ref, rows_ref, skip_ref, y_ref, scores, state):
    length = x_ref.shape[0]
    grid = pl.program_id(0)

    @pl.when(grid == 0)
    def _():
        for start in range(0, length, CHUNK):
            part = slice(start, start + CHUNK)
            scores[part, :] = mm_nt(c_ref[part, :], b_ref[part, :])

    cols = columns_of(rows_ref[0])
    lower = iota((CHUNK, CHUNK), 0) >= iota((CHUNK, CHUNK), 1)
    first = iota((CHUNK, 128), 1) < HEAD_DIM
    for start in range(0, length, CHUNK):
        part = slice(start, start + CHUNK)
        x_f = x_ref[part, :].astype(F32)
        wide, cum = spread(cols[part], 0)
        _, step = spread(cols[part], 8)
        weights = []
        for head in range(4):
            cum_row = rows_ref[0, head : head + 1, part]
            step_row = rows_ref[0, 8 + head : 9 + head, part]
            fade = jnp.exp(jnp.where(lower, wide[head] - cum_row, -1e30))
            weights.append((scores[part, :] * fade * step_row).astype(BF16))
        pieces = []
        for pair in range(2):
            x_pair = x_f[:, 128 * pair : 128 * pair + 128]
            both = jnp.concatenate([jnp.where(first, x_pair, 0.0), jnp.where(first, 0.0, x_pair)], axis=0)
            pieces.append(mm(jnp.concatenate(weights[2 * pair : 2 * pair + 2], axis=1), both.astype(BF16)))
        y_part = jnp.concatenate(pieces, axis=1) + skip_ref[...] * x_f
        if start > 0:
            y_part = y_part + jnp.exp(cum) * mm(c_ref[part, :], state[...].astype(BF16))
        y_ref[part, :] = y_part
        if start + CHUNK < length:
            end = cum[CHUNK - 1 : CHUNK]
            fresh = mm(bt_ref[:, part], (x_f * (jnp.exp(end - cum) * step)).astype(BF16))
            state[...] = fresh if start == 0 else jnp.exp(end) * state[...] + fresh


def inside_call(x_act, b_act, c_act, b_turned, rows, skip_wide):
    length = x_act.shape[0]
    whole = lambda g: (0, 0)
    quad = lambda g: (0, g)
    return pl.pallas_call(
        inside_kernel,
        grid=(QUADS,),
        in_specs=[
            pl.BlockSpec((length, QUAD), quad),
            pl.BlockSpec((length, STATE), whole),
            pl.BlockSpec((length, STATE), whole),
            pl.BlockSpec((STATE, length), whole),
            pl.BlockSpec((1, 40, length), lambda g: (g, 0, 0)),
            pl.BlockSpec((1, QUAD), quad),
        ],
        out_specs=pl.BlockSpec((length, QUAD), quad),
        out_shape=jax.ShapeDtypeStruct((length, INNER), F32),
        scratch_shapes=[pltpu.VMEM((length, CHUNK), F32), pltpu.VMEM((STATE, QUAD), F32)],
        compiler_params=pltpu.CompilerParams(vmem_limit_bytes=VMEM_LIMIT),
        cost_estimate=COST,
        name="ssd_inside",
    )(x_act, b_act, c_act, b_turned, rows, skip_wide)


def gate_kernel(
    y_ref, gate_ref, dn_ref, c_ref, ct_ref, ecd_ref, gain_ref, sin_ref,
    normed_ref, dgate_ref, dm_ref, dgain_ref, out_ref, ones, ecd, gated, silu, slope, back,
):
    grid = pl.program_id(0)

    @pl.when(grid == 0)
    def _():
        ones[...] = head_ones()
        back[...] = jnp.zeros_like(back)
        dgain_ref[...] = jnp.zeros_like(dgain_ref)

    high, mid, _ = split3(ecd_ref[...])
    squares = jnp.zeros((CHUNK, QUAD), F32)
    product = jnp.zeros((CHUNK, QUAD), F32)
    for at in range(0, INNER, QUAD):
        lanes = slice(at, at + QUAD)
        grown = mm(high, ones[:, lanes]) + mm(mid, ones[:, lanes])
        ecd[:, lanes] = grown
        mixed = y_ref[:, lanes] + grown * mm(c_ref[...], sin_ref[:, lanes])
        mixed = mixed.astype(BF16).astype(F32)
        gate = gate_ref[:, lanes].astype(F32)
        sig = sigmoid(gate)
        open_part = gate * sig
        value = mixed * open_part
        silu[:, lanes] = open_part
        slope[:, lanes] = mixed * (sig * (1.0 + gate * (1.0 - sig)))
        gated[:, lanes] = value
        squares = squares + value * value
        product = product + dn_ref[:, lanes] * gain_ref[:, lanes] * value
    inverse = lax.rsqrt(jnp.sum(squares, axis=1, keepdims=True) * (1.0 / INNER) + EPSILON)
    shift = inverse * inverse * inverse * (jnp.sum(product, axis=1, keepdims=True) * (1.0 / INNER))
    inverse = jnp.broadcast_to(inverse, (CHUNK, QUAD))
    shift = jnp.broadcast_to(shift, (CHUNK, QUAD))
    for at in range(0, INNER, QUAD):
        lanes = slice(at, at + QUAD)
        value = gated[:, lanes]
        scaled = value * inverse
        gain = gain_ref[:, lanes]
        dn = dn_ref[:, lanes]
        normed_ref[:, lanes] = (scaled * gain).astype(BF16)
        dgain_ref[:, lanes] += jnp.sum(dn * scaled, axis=0, keepdims=True)
        d_gated = inverse * (dn * gain) - value * shift
        dgate_ref[:, lanes] = (d_gated * slope[:, lanes]).astype(BF16)
        d_mixed = (d_gated * silu[:, lanes]).astype(BF16)
        dm_ref[:, lanes] = d_mixed
        back[:, lanes] += mm(ct_ref[...], (d_mixed.astype(F32) * ecd[:, lanes]).astype(BF16))

    @pl.when(grid == pl.num_programs(0) - 1)
    def _():
        out_ref[...] = back[...].astype(BF16)


def gate_call(y_inside, gate_in, d_normed, c_act, c_turned, ecd, out_gain, s_in):
    length = y_inside.shape[0]
    whole = lambda g: (0, 0)
    down = lambda g: (g, 0)
    wide = pl.BlockSpec((CHUNK, INNER), down)
    rows = jax.ShapeDtypeStruct((length, INNER), BF16)
    state = pl.BlockSpec((STATE, INNER), whole)
    line = pl.BlockSpec((1, INNER), whole)
    return pl.pallas_call(
        gate_kernel,
        grid=(length // CHUNK,),
        in_specs=[
            wide,
            wide,
            wide,
            pl.BlockSpec((CHUNK, STATE), down),
            pl.BlockSpec((STATE, CHUNK), lambda g: (0, g)),
            pl.BlockSpec((CHUNK, 128), down),
            line,
            state,
        ],
        out_specs=[wide, wide, wide, line, state],
        out_shape=[rows, rows, rows, jax.ShapeDtypeStruct((1, INNER), F32), jax.ShapeDtypeStruct((STATE, INNER), BF16)],
        scratch_shapes=[pltpu.VMEM((128, INNER), BF16)]
        + [pltpu.VMEM((CHUNK, INNER), F32)] * 4
        + [pltpu.VMEM((STATE, INNER), F32)],
        compiler_params=pltpu.CompilerParams(vmem_limit_bytes=VMEM_LIMIT),
        cost_estimate=COST,
        name="gated_norm",
    )(y_inside, gate_in, d_normed, c_act, c_turned, ecd, out_gain, s_in)


def back_kernel(x_ref, dm_ref, slope_ref, v_ref, cw_ref, b_ref, c_ref, bt_ref, ct_ref, rows_ref, skip_ref, sin_ref, rin_ref, *rest):
    dv_ref, sums_ref, heads_ref, scores, d_scores, d_b, d_c, states, back, grads, ext, d_step = rest[-12:]
    length = x_ref.shape[0]
    chunks = length // CHUNK
    grid = pl.program_id(0)

    @pl.when(grid == 0)
    def _():
        for start in range(0, length, CHUNK):
            part = slice(start, start + CHUNK)
            scores[part, :] = mm_nt(b_ref[part, :], c_ref[part, :])
        d_scores[...] = jnp.zeros_like(d_scores)
        d_b[...] = jnp.zeros_like(d_b)
        d_c[...] = jnp.zeros_like(d_c)
        d_step[...] = jnp.zeros_like(d_step)
        grads[:, 0:HALO, :] = jnp.zeros((2, HALO, 128), F32)
        grads[:, HALO + length :, :] = jnp.zeros((2, HALO, 128), F32)

    def finish(extra):
        for plane in range(2):
            lanes = slice(128 * plane, 128 * plane + 128)
            ext[plane] = v_ref[:, lanes].astype(F32)
            total = [jnp.zeros((8, 128), F32)] * (KW + 1)
            for start in range(0, length, CHUNK):
                here = grads[plane, HALO + start : HALO + start + CHUNK, :]
                for tap in range(KW):
                    at = HALO - 3 + tap + start
                    total[tap] = total[tap] + fold_rows(here * ext[plane, at : at + CHUNK, :])
                total[KW] = total[KW] + fold_rows(here)
            for at, rows in enumerate(total):
                sums_ref[at : at + 1, lanes] = jnp.sum(rows, axis=0, keepdims=True)
            for start in [0] + list(range(HALO, HALO + length, CHUNK)):
                count = HALO if start == 0 else CHUNK
                value = cw_ref[KW - 1 : KW, lanes] * grads[plane, start : start + count, :]
                for tap in range(KW - 1):
                    at = start + KW - 1 - tap
                    value = value + cw_ref[tap : tap + 1, lanes] * grads[plane, at : at + count, :]
                place = length if start == 0 else start - HALO
                dv_ref[place : place + count, lanes] = value.astype(BF16)
        sums_ref[KW + 1 : KW + 2, :] = extra
        sums_ref[KW + 2 : 8, :] = jnp.zeros((8 - KW - 2, QUAD), F32)

    def keep(start, value):
        for plane in range(2):
            grads[plane, HALO + start : HALO + start + CHUNK, :] = value[:, 128 * plane : 128 * plane + 128]

    @pl.when(grid < QUADS)
    def _():
        cols = columns_of(rows_ref[0])
        upper = iota((CHUNK, CHUNK), 0) <= iota((CHUNK, CHUNK), 1)
        first = iota((CHUNK, 128), 1) < HEAD_DIM
        lane = iota((CHUNK, 128), 1)
        line = iota((8, 128), 0)
        head_of = iota((QUAD, 128), 0) >> 6
        ones_v = jnp.where(iota((QUAD, 128), 1) == head_of + 8, 1.0, 0.0).astype(BF16)
        ones_u = jnp.where(iota((QUAD, 128), 1) == head_of + 16, 1.0, 0.0).astype(BF16)
        square = (CHUNK, CHUNK)
        later = jnp.where(iota(square, 0) >= iota(square, 1), 1.0, 0.0).astype(BF16)
        before = jnp.where(iota(square, 0) < iota(square, 1), 1.0, 0.0).astype(BF16)
        skip = skip_ref[...]
        back[...] = rin_ref[...].astype(F32)
        state = sin_ref[...].astype(F32)
        for chunk in range(chunks):
            part = slice(chunk * CHUNK, chunk * CHUNK + CHUNK)
            states[chunk] = state
            if chunk + 1 < chunks:
                _, cum = spread(cols[part], 0)
                _, step = spread(cols[part], 8)
                end = cum[CHUNK - 1 : CHUNK]
                fed = (x_ref[part, :].astype(F32) * (jnp.exp(end - cum) * step)).astype(BF16)
                state = jnp.exp(end) * state + mm(bt_ref[:, part], fed)
        skip_sum = jnp.zeros((1, QUAD), F32)
        bias_sum = jnp.zeros((8, 1), F32)
        rate_sum = jnp.zeros((8, 1), F32)
        for chunk in range(chunks - 1, -1, -1):
            part = slice(chunk * CHUNK, chunk * CHUNK + CHUNK)
            x_f = x_ref[part, :].astype(F32)
            dm = dm_ref[part, :]
            dm_f = dm.astype(F32)
            cum_wide, cum = spread(cols[part], 0)
            step_wide, step = spread(cols[part], 8)
            end = cum[CHUNK - 1 : CHUNK]
            after = back[...]
            after_low = after.astype(BF16)
            state = states[chunk]
            left = jnp.exp(end - cum)
            grown = dm_f * jnp.exp(cum)
            grown_low = grown.astype(BF16)
            faded = x_f * left
            from_after = mm(b_ref[part, :], after_low)
            from_state = mm(c_ref[part, :], state.astype(BF16))
            d_b[part, :] += mm_nt((faded * step).astype(BF16), after_low)
            d_c[part, :] += mm_nt(grown_low, state.astype(BF16))
            marks = mm((grown * from_state).astype(BF16), ones_v) + mm((faded * from_after).astype(BF16), ones_u)
            pair_sum = jnp.zeros((8, CHUNK), F32)
            crossing = jnp.zeros((8, 1), F32)
            cross = jnp.sum(state * after, axis=0, keepdims=True) * jnp.exp(end)
            pieces = []
            for pair in range(2):
                x_pair = x_f[:, 128 * pair : 128 * pair + 128]
                dm_pair = dm_f[:, 128 * pair : 128 * pair + 128]
                x_both = jnp.concatenate([jnp.where(first, x_pair, 0.0), jnp.where(first, 0.0, x_pair)], axis=0)
                dm_both = jnp.concatenate([jnp.where(first, dm_pair, 0.0), jnp.where(first, 0.0, dm_pair)], axis=0)
                d_weights = mm_nt(x_both.astype(BF16), dm[:, 128 * pair : 128 * pair + 128])
                kept = []
                for half in range(2):
                    head = 2 * pair + half
                    cum_row = rows_ref[0, head : head + 1, part]
                    fade = jnp.exp(jnp.where(upper, cum_row - cum_wide[head], -1e30))
                    faded_grad = d_weights[half * CHUNK : half * CHUNK + CHUNK] * fade
                    d_scores[part, :] += faded_grad * step_wide[head]
                    joint = faded_grad * scores[part, :]
                    marks = marks + jnp.where(lane == head, jnp.sum(joint, axis=1, keepdims=True), 0.0)
                    row = jnp.sum(joint * step_wide[head], axis=0, keepdims=True)
                    pair_sum = pair_sum + jnp.where(line == head, row, 0.0)
                    kept.append((scores[part, :] * fade).astype(BF16))
                    low, high = 64 * head, 64 * head + 64
                    here = (iota((1, QUAD), 1) >= low) & (iota((1, QUAD), 1) < high)
                    amount = jnp.sum(jnp.where(here, cross, 0.0), axis=1, keepdims=True)
                    crossing = crossing + jnp.where(iota((8, 1), 0) == head, amount, 0.0)
                pieces.append(mm(jnp.concatenate(kept, axis=1), dm_both.astype(BF16)))
            direct = jnp.concatenate(pieces, axis=1) + left * from_after
            d_x = step * direct + skip * dm_f
            keep(chunk * CHUNK, d_x * slope_ref[part, :].astype(F32))
            skip_sum = skip_sum + jnp.sum(x_f * dm_f, axis=0, keepdims=True)
            back[...] = jnp.exp(end) * after + mm(ct_ref[:, part], grown_low)
            marks = marks.T
            within, carried, outward = marks[0:8], marks[8:16], marks[16:24]
            step_rows = rows_ref[0, 8:16, part]
            change = pair_sum - step_rows * within + carried
            decay = mm_exact(change, later) + mm_exact(step_rows * outward, before) + crossing
            d_raw = (within + outward + rows_ref[0, 32:40, part] * decay) * rows_ref[0, 24:32, part]
            d_step[pl.ds(pl.multiple_of(grid * 8, 8), 8), part] = d_raw
            bias_sum = bias_sum + jnp.sum(d_raw, axis=1, keepdims=True)
            rate_sum = rate_sum + jnp.sum(step_rows * decay, axis=1, keepdims=True)
        heads_ref[0, 0:8, :] = jnp.broadcast_to(bias_sum, (8, 128))
        heads_ref[0, 8:16, :] = jnp.broadcast_to(rate_sum, (8, 128))
        finish(skip_sum)

    @pl.when(grid == QUADS)
    def _():
        for start in range(0, length, CHUNK):
            part = slice(start, start + CHUNK)
            low = d_scores[part, :].astype(BF16)
            into_b = d_b[part, :] + mm(low, c_ref[part, :])
            into_c = d_c[part, :] + mm(d_scores[part, :].T.astype(BF16), b_ref[part, :])
            both = jnp.concatenate([into_b, into_c], axis=1)
            keep(start, both * slope_ref[part, :].astype(F32))
        finish(jnp.zeros((1, QUAD), F32))

    @pl.when(grid == QUADS + 1)
    def _():
        row, column = iota((128, QUAD), 0), iota((128, QUAD), 1)
        pick = (column < HEADS) & (row == 8 * (column >> 2) + (column & 3))
        turned = d_step[...].T.astype(BF16)
        dv_ref[length:, :] = jnp.zeros((HALO, QUAD), BF16)
        dv_ref[0:length, :] = mm(turned, jnp.where(pick, 1.0, 0.0).astype(BF16)).astype(BF16)


def back_call(x_act, d_mixed, slope, v, conv_weight, b_act, c_act, b_turned, c_turned, rows, skip_wide, s_in, r_in, after):
    length = x_act.shape[0]
    whole = lambda g: (0, 0)
    quad = lambda g: (0, jnp.minimum(g, QUADS - 1))
    block = lambda g: (0, jnp.minimum(g, QUADS))
    lead = lambda g: (jnp.minimum(g, QUADS - 1), 0, 0)
    return pl.pallas_call(
        back_kernel,
        grid=(QUADS + 2,),
        in_specs=[
            pl.BlockSpec((length, QUAD), quad),
            pl.BlockSpec((length, QUAD), quad),
            pl.BlockSpec((length, QUAD), block),
            pl.BlockSpec((length + HALO, QUAD), block),
            pl.BlockSpec((KW, QUAD), block),
            pl.BlockSpec((length, STATE), whole),
            pl.BlockSpec((length, STATE), whole),
            pl.BlockSpec((STATE, length), whole),
            pl.BlockSpec((STATE, length), whole),
            pl.BlockSpec((1, 40, length), lead),
            pl.BlockSpec((1, QUAD), quad),
            pl.BlockSpec((STATE, QUAD), quad),
            pl.BlockSpec((STATE, QUAD), quad),
        ]
        + [pl.BlockSpec(memory_space=pl.ANY)] * len(after),
        out_specs=[
            pl.BlockSpec((length + HALO, QUAD), lambda g: (0, g)),
            pl.BlockSpec((8, QUAD), block),
            pl.BlockSpec((1, 16, 128), lead),
        ],
        scratch_shapes=[
            pltpu.VMEM((length, CHUNK), F32),
            pltpu.VMEM((length, CHUNK), F32),
            pltpu.VMEM((length, STATE), F32),
            pltpu.VMEM((length, STATE), F32),
            pltpu.VMEM((length // CHUNK, STATE, QUAD), F32),
            pltpu.VMEM((STATE, QUAD), F32),
            pltpu.VMEM((2, length + 2 * HALO, 128), F32),
            pltpu.VMEM((2, length + HALO, 128), F32),
            pltpu.VMEM((128, length), F32),
        ],
        out_shape=[
            jax.ShapeDtypeStruct((length + HALO, CONV + QUAD), BF16),
            jax.ShapeDtypeStruct((8, CONV), F32),
            jax.ShapeDtypeStruct((QUADS, 16, 128), F32),
        ],
        compiler_params=pltpu.CompilerParams(vmem_limit_bytes=VMEM_LIMIT),
        cost_estimate=LONG,
        name="ssd_back",
    )(x_act, d_mixed, slope, v, conv_weight, b_act, c_act, b_turned, c_turned, rows, skip_wide, s_in, r_in, *after)


def put_quarters(place_ref, count, step, refs, put):
    near = (step // 2) == place_ref[count]
    for at in range(2, count):
        for index in range(4):
            wanted = near if index < 2 else jnp.logical_not(near)

            @pl.when(wanted & (step % 2 == index % 2))
            def _():
                put(at, refs[2 + 4 * (at - 2) + index])


def weight_kernel(height, quarters, count, place_ref, x_ref, *rest):
    piece_refs, (out_ref, w_ref) = rest[:-2], rest[-2:]

    def put(at, ref):
        w_ref[:, pl.ds(pl.multiple_of(place_ref[at] * height, 128), height)] = ref[...]

    for at in range(2 if quarters else count):
        put(at, piece_refs[at])
    if quarters:
        put_quarters(place_ref, count, pl.program_id(0), piece_refs, put)
    out_ref[...] = mm_nt(x_ref[...], w_ref[...]).astype(BF16)


def weight_call(x, pieces, places, count, width, block, quarters, name):
    rows, depth = x.shape
    height = pieces[0].shape[1]

    def spec(at):
        if not quarters or at < 2:
            return pl.BlockSpec((block, height), lambda g, place: (g, 0))
        return pl.BlockSpec((block, height), lambda g, place: (0, 0))

    grid_spec = pltpu.PrefetchScalarGridSpec(
        num_scalar_prefetch=1,
        grid=(width // block,),
        in_specs=[pl.BlockSpec((rows, depth), lambda g, place: (0, 0))] + [spec(at) for at in range(len(pieces))],
        out_specs=pl.BlockSpec((rows, block), lambda g, place: (0, g)),
        scratch_shapes=[pltpu.VMEM((block, depth), BF16)],
    )
    return pl.pallas_call(
        functools.partial(weight_kernel, height, quarters, count),
        grid_spec=grid_spec,
        out_shape=jax.ShapeDtypeStruct((rows, width), BF16),
        compiler_params=pltpu.CompilerParams(vmem_limit_bytes=VMEM_LIMIT),
        cost_estimate=COST,
        name=name,
    )(places, x, *pieces)


def weight_back_kernel(place_ref, g_ref, *rest):
    piece_refs, out_ref = rest[:-1], rest[-1]
    for at, piece_ref in enumerate(piece_refs):

        @pl.when(pl.program_id(0) == at)
        def _():
            out_ref[...] = mm_nt(g_ref[...], piece_ref[...])


def weight_back_call(g, pieces, places):
    rows, width = g.shape
    block = pieces[0].shape[0]
    grid_spec = pltpu.PrefetchScalarGridSpec(
        num_scalar_prefetch=1,
        grid=(len(pieces),),
        in_specs=[pl.BlockSpec((rows, width), lambda k, place: (0, 0))]
        + [pl.BlockSpec((block, width), lambda k, place: (0, 0))] * len(pieces),
        out_specs=pl.BlockSpec((rows, block), lambda k, place: (0, place[k])),
    )
    return pl.pallas_call(
        weight_back_kernel,
        grid_spec=grid_spec,
        out_shape=jax.ShapeDtypeStruct((rows, block * len(pieces)), F32),
        compiler_params=pltpu.CompilerParams(vmem_limit_bytes=VMEM_LIMIT),
        cost_estimate=COST,
        name="d_normed_out",
    )(places, g, *pieces)


def pick_kernel(table_ref, own, other, own_halo, other_halo, own_out, other_out, halo_out):
    parts, blocks = own_out.shape[:2]
    for part in range(parts):

        @pl.loop(0, blocks)
        def _(at):
            block = table_ref[part, at]
            own_out[part, at] = own[block]
            other_out[part, at] = other[block]
            halo_out[part, at, :, :HALO] = own_halo[block]
            halo_out[part, at, :, HALO:] = other_halo[block]


def pick_call(table, own, other, own_halo, other_halo):
    parts, blocks = table.shape
    _, height, length = own.shape
    vmem = pl.BlockSpec(memory_space=pltpu.VMEM)
    made = pl.pallas_call(
        pick_kernel,
        in_specs=[pl.BlockSpec(memory_space=pltpu.SMEM)] + [vmem] * 4,
        out_specs=[vmem] * 3,
        out_shape=[jax.ShapeDtypeStruct((parts, blocks, height, length), BF16)] * 2
        + [jax.ShapeDtypeStruct((parts, blocks, height, 2 * HALO), BF16)],
        compiler_params=pltpu.CompilerParams(vmem_limit_bytes=VMEM_LIMIT),
        cost_estimate=COST,
        name="pick_rows",
    )(table, own, other, own_halo, other_halo)
    return [array.reshape(parts, blocks * height, -1) for array in made]


def grad_kernel(halo, *refs):
    outs = refs[-6:]
    own, other = refs[0][0], refs[1][0]
    if halo:
        edge, right, right_other, edge_right, edge_other = refs[2][0], refs[3], refs[4], refs[5], refs[6]
    else:
        right, right_other = refs[2], refs[3]
    total = mm(own, right[...]) + mm(other, right_other[...])
    if halo:
        total = total + mm(edge, jnp.concatenate([edge_right[...], edge_other[...]], axis=0))
    half = total.shape[0] // 2
    for part in range(3):

        @pl.when(pl.program_id(0) == part)
        def _():
            outs[2 * part][...] = total[:half].astype(BF16)
            outs[2 * part + 1][...] = total[half:].astype(BF16)


def grad_call(lefts, right, right_other, width, halo, name):
    own, other, edge = lefts
    _, rows, length = own.shape
    lead = lambda g: (g, 0, 0)
    column = lambda g: (0, g)
    below = lambda g: (length // HALO, g)
    specs = [pl.BlockSpec((1, rows, length), lead)] * 2
    args = [own, other]
    if halo:
        specs.append(pl.BlockSpec((1, rows, 2 * HALO), lead))
        args.append(edge)
    specs += [pl.BlockSpec((length, width), column)] * 2
    args += [right, right_other]
    if halo:
        specs += [pl.BlockSpec((HALO, width), below)] * 2
        args += [right, right_other]
    made = pl.pallas_call(
        functools.partial(grad_kernel, halo),
        grid=(3,),
        in_specs=specs,
        out_specs=[pl.BlockSpec((rows // 2, width), lambda g: (0, 0))] * 6,
        out_shape=[jax.ShapeDtypeStruct((rows // 2, width), BF16)] * 6,
        compiler_params=pltpu.CompilerParams(vmem_limit_bytes=VMEM_LIMIT),
        cost_estimate=COST,
        name=name,
    )(*args)
    return [(made[2 * part], made[2 * part + 1]) for part in range(3)]


def fold_kernel(parts, groups, which, *refs):
    ins, outs = refs[: 2 * parts * groups], refs[2 * parts * groups :]
    for part in range(parts):
        at = 0
        for group in range(groups):
            kept, got = ins[2 * (part * groups + group)], ins[2 * (part * groups + group) + 1]
            rows, width = kept.shape
            half = rows // 2
            lines = slice(0, rows) if which == "last" else slice(0, half) if which == "kept" else slice(half, rows)
            total = kept[lines, :].astype(F32) + got[lines, :].astype(F32)
            if which == "last":
                gate = INNER // parts
                other = width - gate
                outs[0][:, part * gate : (part + 1) * gate] = total[:, :gate]
                begin = INNER + part * other
                end = min(begin + other, outs[0].shape[1])
                outs[0][:, begin:end] = total[:, gate : gate + end - begin]
            else:
                outs[part][:, at : at + width] = total.astype(BF16)
            at += width


def fold_call(pairs, which, width=0):
    parts, groups = len(pairs), len(pairs[0])
    arrays = [array for part in pairs for pair in part for array in pair]
    rows = arrays[0].shape[0]
    half = rows // 2
    if which == "last":
        shapes = [jax.ShapeDtypeStruct((rows, width), F32)]
    else:
        shapes = [jax.ShapeDtypeStruct((half, sum(kept.shape[1] for kept, _ in part)), BF16) for part in pairs]
    vmem = pl.BlockSpec(memory_space=pltpu.VMEM)
    return pl.pallas_call(
        functools.partial(fold_kernel, parts, groups, which),
        in_specs=[vmem] * len(arrays),
        out_specs=[vmem] * len(shapes),
        out_shape=shapes,
        compiler_params=pltpu.CompilerParams(vmem_limit_bytes=VMEM_LIMIT),
        cost_estimate=COST,
        name="fold_" + which,
    )(*arrays)


def residual_kernel(place_ref, *refs):
    count = len(refs) // 2 - 1
    total = refs[2 * count][0].astype(F32)
    for at in range(count):
        total = total + mm(refs[at][...], refs[count + at][...])
    refs[-1][0] = total


def residual_call(x, pieces, places, tokens, after):
    rows = x.shape[0]
    height, width = pieces[0].shape
    block = 768
    part = lambda at: pl.BlockSpec((rows, height), lambda g, place: (0, place[at]))
    whole = pl.BlockSpec((1, rows, block), lambda g, place: (0, 0, g))
    grid_spec = pltpu.PrefetchScalarGridSpec(
        num_scalar_prefetch=1,
        grid=(width // block,),
        in_specs=[part(at) for at in range(len(pieces))]
        + [pl.BlockSpec((height, block), lambda g, place: (0, g))] * len(pieces)
        + [whole],
        out_specs=whole,
    )
    return pl.pallas_call(
        residual_kernel,
        grid_spec=grid_spec,
        out_shape=jax.ShapeDtypeStruct((1, rows, width), F32),
        compiler_params=pltpu.CompilerParams(vmem_limit_bytes=VMEM_LIMIT),
        cost_estimate=LONG,
        name="block_out",
    )(tie(places, after), *([x] * len(pieces)), *pieces, tokens)


def columns_kernel(count, place_ref, g_ref, *refs):
    w_refs, (out_ref, w) = refs[:count], refs[-2:]
    height = D // count
    for at in range(count):
        w[:, pl.ds(pl.multiple_of(place_ref[at] * height, 128), height)] = w_refs[at][...]
    product = mm(g_ref[...], w[...])

    @pl.when(pl.program_id(0) == 0)
    def _():
        out_ref[...] = product

    @pl.when(pl.program_id(0) > 0)
    def _():
        out_ref[...] += product


def columns_call(g, pieces, places):
    length, depth = g.shape
    height = pieces[0].shape[1]
    count = len(pieces)
    block = depth // 2
    down = lambda k, place: (k, 0)
    grid_spec = pltpu.PrefetchScalarGridSpec(
        num_scalar_prefetch=1,
        grid=(depth // block,),
        in_specs=[pl.BlockSpec((length, block), lambda k, place: (0, k))] + [pl.BlockSpec((block, height), down)] * count,
        out_specs=pl.BlockSpec((length, D), lambda k, place: (0, 0)),
        scratch_shapes=[pltpu.VMEM((block, D), BF16)],
    )
    return pl.pallas_call(
        functools.partial(columns_kernel, count),
        grid_spec=grid_spec,
        out_shape=jax.ShapeDtypeStruct((length, D), F32),
        compiler_params=pltpu.CompilerParams(vmem_limit_bytes=VMEM_LIMIT),
        cost_estimate=COST,
        name="d_normed_gate",
    )(places, g, *pieces)


def tokens_kernel(count, quarters, place_ref, *refs):
    part_ref, dv_ref, spill_ref, tokens_ref, cotan_ref, gain_ref = refs[:6]
    wv_refs = refs[6:-6]
    out_ref, dgain_ref, fixed, wv, total, inverse = refs[-6:]
    length = dv_ref.shape[0]
    height = D // count
    step, steps = pl.program_id(0), pl.num_programs(0)

    @pl.when(step == 0)
    def _():
        for start in range(0, length, CHUNK):
            part = slice(start, start + CHUNK)
            values = tokens_ref[0, part, :].astype(F32)
            mean = jnp.sum(values * values, axis=1, keepdims=True) * (1.0 / D)
            inverse[part, :] = jnp.broadcast_to(lax.rsqrt(mean + EPSILON), (CHUNK, 128))

    fixed[...] = dv_ref[...]
    ends = dv_ref[length - HALO :, :].astype(F32) + spill_ref[...].astype(F32)
    fixed[length - HALO :, :] = ends.astype(BF16)

    def put(at, ref):
        wv[:, pl.ds(pl.multiple_of(place_ref[at] * height, 128), height)] = ref[...]

    for at in range(2 if quarters else count):
        put(at, wv_refs[at])
    if quarters:
        put_quarters(place_ref, count, step, wv_refs, put)
    product = mm(fixed[...], wv[...])

    @pl.when(step == 0)
    def _():
        total[...] = part_ref[...] + product

    @pl.when(step > 0)
    def _():
        total[...] += product

    @pl.when(step == steps - 1)
    def _():
        sums = jnp.zeros((8, D), F32)
        for start in range(0, length, CHUNK):
            part = slice(start, start + CHUNK)
            values = tokens_ref[0, part, :].astype(F32)
            grad = total[part, :]
            a = grad * gain_ref[...]
            inv = inverse[part, 0:1]
            sums = sums + fold_rows(grad * values * inv)
            shift = inv * inv * inv * (jnp.sum(a * values, axis=1, keepdims=True) * (1.0 / D))
            out_ref[0, part, :] = cotan_ref[0, part, :].astype(F32) + inv * a - values * shift
        dgain_ref[...] = jnp.sum(sums, axis=0, keepdims=True)


def tokens_call(part, d_v, spill, pieces, places, quarters, tokens, cotangent, gain):
    length = part.shape[0]
    height = pieces[0].shape[1]
    wide = d_v.shape[1]
    steps = 4
    block = wide // steps
    count = D // height
    whole = lambda k, place: (0, 0)
    column = lambda k, place: (0, k)
    down = lambda k, place: (k, 0)
    all_rows = pl.BlockSpec((1, length, D), lambda k, place: (0, 0, 0))
    grid_spec = pltpu.PrefetchScalarGridSpec(
        num_scalar_prefetch=1,
        grid=(steps,),
        in_specs=[
            pl.BlockSpec((length, D), whole),
            pl.BlockSpec((length, block), column),
            pl.BlockSpec((HALO, block), column),
            all_rows,
            all_rows,
            pl.BlockSpec((1, D), whole),
        ]
        + [pl.BlockSpec((block, height), whole if quarters and at >= 2 else down) for at in range(len(pieces))],
        out_specs=[all_rows, pl.BlockSpec((1, D), whole)],
        scratch_shapes=[
            pltpu.VMEM((length, block), BF16),
            pltpu.VMEM((block, D), BF16),
            pltpu.VMEM((length, D), F32),
            pltpu.VMEM((length, 128), F32),
        ],
    )
    return pl.pallas_call(
        functools.partial(tokens_kernel, count, quarters),
        grid_spec=grid_spec,
        out_shape=[jax.ShapeDtypeStruct((1, length, D), F32), jax.ShapeDtypeStruct((1, D), F32)],
        compiler_params=pltpu.CompilerParams(vmem_limit_bytes=VMEM_LIMIT),
        cost_estimate=COST,
        name="d_tokens",
    )(places, part, d_v, spill, tokens, cotangent, gain, *pieces)


def on_device(
    ranks,
    shards,
    tokens,
    norm_gain,
    w_in,
    conv_weight,
    conv_bias,
    dt_bias,
    a_log,
    skip_gain,
    out_gain,
    w_out,
    cotangent,
):
    both = ("seq", "fsdp")
    rank = lax.axis_index("seq")
    shard = lax.axis_index("fsdp")

    def move(value, target):
        pairs = []
        for s in range(ranks):
            for f in range(shards):
                goal = target(s, f)
                if goal is not None:
                    pairs.append((s * shards + f, goal[0] * shards + goal[1]))
        return lax.ppermute(value, both, pairs)

    def across(value):
        return move(value, lambda s, f: (s, f ^ 1))

    def gather(value, crossed, middle, near):
        pieces = [(value, 0), (crossed, 1)] + near
        pieces += [(across(tie(piece, middle)), step ^ 1) for piece, step in near]
        return [piece for piece, _ in pieces], jnp.stack([shard ^ step for _, step in pieces]).astype(jnp.int32)

    def send_near(value):
        return [(move(value, lambda s, f: (s, f ^ step)), step) for step in range(2, shards, 2)]

    def gather_quarters(value, crossed, middle):
        quarter = value.shape[0] // 4
        side = rank & 1
        remote = []
        for step in range(2, shards, 2):
            near, far = [], []
            for part in range(2):
                sent = lax.dynamic_slice_in_dim(value, (2 * side + part) * quarter, quarter, 0)
                near.append(move(tie(sent, *near), lambda s, f: (s, f ^ step)))
                far.append(move(near[part], lambda s, f: (s ^ 1, f)))
            remote.append((near + far, step))
        remote += [([across(piece) for piece in pieces[:-1]] + [across(tie(pieces[-1], *middle))], step ^ 1) for pieces, step in remote]
        places = [shard, shard ^ 1] + [shard ^ step for _, step in remote] + [side]
        return [value, crossed] + sum([pieces for pieces, _ in remote], []), jnp.stack(places).astype(jnp.int32)

    def in_order(pieces, places, quarters):
        height = pieces[0].shape[1]
        whole = jnp.zeros((pieces[0].shape[0], height * shards), pieces[0].dtype)
        for at, piece in enumerate(pieces):
            first, place = 0, at
            if quarters and at >= 2:
                place, index = 2 + (at - 2) // 4, (at - 2) % 4
                side = places[shards] if index < 2 else 1 - places[shards]
                first = (2 * side + index % 2) * piece.shape[0]
            whole = lax.dynamic_update_slice(whole, piece, (first, places[place] * height))
        return [whole], jnp.zeros((1,), jnp.int32)

    def exchange(states):
        return lax.all_to_all(states, "seq", split_axis=0, concat_axis=0, tiled=True)

    halo = move(tokens[0, -HALO:], lambda s, f: (s + 1, f) if s + 1 < ranks else None)
    longer = jnp.concatenate([halo, tokens[0]], axis=0).astype(F32)
    inverse = lax.rsqrt(jnp.mean(longer * longer, axis=-1, keepdims=True) + EPSILON)
    normed_long = (longer * inverse * norm_gain).astype(BF16)
    normed = normed_long[HALO:]

    cotan = cotangent[0]
    turned = w_in.T
    width_v = CONV + QUAD
    own_v = jnp.pad(turned[INNER:], ((0, width_v - (turned.shape[0] - INNER)), (0, 0)))
    chip_bits = [("fsdp", bit) for bit in (2, 4, 8) if bit < shards]
    seq_bits = [("seq", bit) for bit in (1, 2, 4, 8) if bit < ranks]
    first_bits = [seq_bits[0], chip_bits[0], seq_bits[1]] if chip_bits else [seq_bits[0], seq_bits[1], seq_bits[0]]
    orders = []
    for part in range(3):
        lead = list(dict.fromkeys(first_bits[part:] + first_bits[:part]))
        orders.append(lead + [bit for bit in chip_bits + seq_bits if bit not in lead])
    chips = ranks * (shards // 2)
    table = []
    for order in orders:
        line = []
        for place in range(chips):
            s, f = rank, shard
            for at, (axis, bit) in enumerate(order):
                if place >> (len(order) - 1 - at) & 1:
                    s, f = (s ^ bit, f) if axis == "seq" else (s, f ^ bit)
            line.append(s * (shards // 2) + (f >> 1))
        table.append(jnp.stack(line))
    table = jnp.stack(table).astype(jnp.int32)

    def halves(turned):
        blocks = turned.reshape(chips, 2, -1, turned.shape[1])
        core = shard & 1
        return lax.dynamic_index_in_dim(blocks, core, 1, False), lax.dynamic_index_in_dim(blocks, 1 - core, 1, False)

    own, other = halves(normed.T)
    own_halo, other_halo = halves(normed_long[:HALO].T)
    lefts = pick_call(table, own, across(other), own_halo, across(other_halo))
    own_g = turned[:INNER]
    crossed_v, crossed_g, crossed_o = across(own_v), across(own_g), across(w_out)
    pieces_v, places_v = gather_quarters(own_v, crossed_v, (lefts[0], crossed_v, crossed_g, crossed_o))

    def flip(axis, bit):
        return lambda s, f: (s ^ bit, f) if axis == "seq" else (s, f ^ bit)

    def first_step(terms, *ahead):
        return [(kept, move(tie(sent, *ahead), flip(*orders[part][0]))) for part, (kept, sent) in enumerate(terms)]

    lanes_whole = w_in.shape[0] % 128 == 0
    last_near, first_far, count = pieces_v[3], pieces_v[4], shards
    if not lanes_whole:
        pieces_v, places_v = in_order(pieces_v, places_v, True)
        count = 1
    projected = weight_call(normed_long, pieces_v, places_v, count, width_v, width_v // 4, lanes_whole, "project_v")
    near_g = send_near(tie(own_g, last_near, first_far))
    pieces_g, places = gather(own_g, crossed_g, projected, near_g)
    near_o = send_near(tie(w_out, near_g[0][0], projected))
    lanes = lambda vec: jnp.pad(vec, (0, 128 - HEADS)).reshape(1, 128)
    rows, ecd, decay_all = step_call(projected, lanes(dt_bias), lanes(a_log))
    v = projected
    made = conv_call(ranks, v, conv_weight, conv_bias.reshape(1, CONV), rows, decay_all, ())
    x_act, slope, b_act, c_act, b_turned, c_turned, states = made
    skip_wide = jnp.repeat(skip_gain, HEAD_DIM).reshape(1, INNER)
    y_inside = inside_call(x_act, b_act, c_act, b_turned, rows, skip_wide)
    carried, totals = carry_call(ranks, exchange(states), None, [y_inside])
    s_in = exchange(carried)
    pieces_o, _ = gather(w_out, crossed_o, carried, near_o)
    places_o = places
    if not lanes_whole:
        pieces_g, places = in_order(pieces_g, places, False)
    gate_in = weight_call(normed, pieces_g, places, count, INNER, INNER // 3, False, "project_gate")
    d_normed_out = weight_back_call(cotan, pieces_o, places_o)
    made = gate_call(y_inside, gate_in, d_normed_out, c_act, c_turned, ecd, out_gain.reshape(1, INNER), s_in)
    normed_out, d_gate, d_mixed, d_gain_out, states = made
    d_w_out = lax.dot_general(normed_out, cotan, TN, preferred_element_type=F32).astype(BF16)
    d_w_out_sum = lax.psum_scatter(d_w_out, both, scatter_dimension=0, tiled=True).astype(F32)
    gate_terms = grad_call(lefts, d_gate, across(d_gate), INNER // 3, False, "d_w_gate")
    (carried,) = carry_call(ranks, exchange(states), totals, [d_w_out] + [kept for kept, _ in gate_terms])
    block_out = residual_call(normed_out, pieces_o, places_o, tokens, carried)
    r_in = exchange(carried)
    gate_parts = first_step(gate_terms, r_in)
    d_v_long, sums, heads = back_call(
        x_act, d_mixed, slope, v, conv_weight, b_act, c_act, b_turned, c_turned, rows, skip_wide, s_in, r_in, [block_out]
    )
    d_v_long = tie(d_v_long, *[got for _, got in gate_parts])
    spill = move(d_v_long[tokens.shape[1] :], lambda s, f: (s - 1, f) if s > 0 else None)
    part = columns_call(tie(d_gate, d_v_long), pieces_g, places)
    d_v_other = tie(across(d_v_long), spill, part)
    rest_terms = grad_call(lefts, d_v_long, d_v_other, (CONV + 128) // 3, True, "d_w_rest")
    rest_parts = first_step(rest_terms)
    d_tokens, d_norm_gain = tokens_call(
        part, tie(d_v_long, rest_terms[0][0]), spill, pieces_v, places_v, lanes_whole,
        tokens, cotangent, norm_gain.reshape(1, D),
    )
    rest_parts = [(kept, tie(got, d_tokens)) for kept, got in rest_parts]

    d_skip = sums[KW + 1, :INNER].reshape(HEADS, HEAD_DIM).sum(axis=1)
    pieces = [
        sums[:KW].reshape(-1),
        sums[KW],
        heads[:, 0:4, 0].reshape(-1),
        heads[:, 8:12, 0].reshape(-1) * -jnp.exp(a_log),
        d_skip,
        d_gain_out.reshape(-1),
    ]
    flat = jnp.concatenate(pieces)
    width = flat.shape[0]
    flat = jnp.pad(flat, (0, -width % 1024)).reshape(-1, 128)
    flat = flat + across(flat)
    small_bits = seq_bits[:1] + chip_bits + seq_bits[1:]
    flat = flat + move(flat, flip(*small_bits[0]))

    def four(value, first, second):
        parts = [move(value, flip(*first)), move(value, flip(*second))]
        corner = lambda s, f: flip(*first)(*flip(*second)(s, f))
        return (value + parts[0]) + (parts[1] + move(value, corner))

    all_bits = [("fsdp", 1)] + small_bits
    pairs = [[gate_parts[part], rest_parts[part]] for part in range(3)]
    for at in range(1, len(orders[0])):
        sent = fold_call(pairs, "sent")
        kept = fold_call(pairs, "kept")
        pairs = [[(kept[part], move(sent[part], flip(*orders[part][at])))] for part in range(3)]
        flat = flat + move(tie(flat, kept[0]), flip(*small_bits[at]))
        use = all_bits[2 * at - 2 : 2 * at]
        if len(use) == 2:
            d_norm_gain = four(tie(d_norm_gain, kept[0]), *use)
        elif use:
            d_norm_gain = d_norm_gain + move(tie(d_norm_gain, kept[0]), flip(*use[0]))
    (d_w_in,) = fold_call(pairs, "last", w_in.shape[1])
    flat = flat.reshape(-1)
    small, at = [], 0
    for piece in pieces:
        small.append(flat[at : at + piece.shape[0]])
        at += piece.shape[0]
    d_norm_gain = d_norm_gain.reshape(-1)
    d_conv_weight, d_conv_bias, d_dt_bias, d_a_log, d_skip, d_gain_out = small
    return (
        block_out,
        d_tokens,
        d_norm_gain,
        d_w_in,
        d_conv_weight.reshape(KW, CONV),
        d_conv_bias,
        d_dt_bias,
        d_a_log,
        d_skip,
        d_gain_out,
        d_w_out_sum,
    )


def solution(mesh):
    split = P("fsdp", "seq", None)
    rows = P("fsdp", None)
    last = P(("seq", "fsdp"), None)
    return jax.shard_map(
        functools.partial(on_device, mesh.shape["seq"], mesh.shape["fsdp"]),
        mesh=mesh,
        in_specs=(split, P(), rows, P(), P(), P(), P(), P(), P(), rows, split),
        out_specs=(split, split, P(), last, P(), P(), P(), P(), P(), P(), last),
        check_vma=False,
    )
```

```python
import functools

import jax
import jax.numpy as jnp
from jax import lax
from jax.experimental import pallas as pl
from jax.experimental.pallas import tpu as pltpu
from jax.sharding import PartitionSpec as P

HEADS = 48
HEAD_DIM = 64
STATE = 128
KW = 4
INNER = 3072
D = 1536
CONV = INNER + 2 * STATE

EPSILON = 1e-05
CHUNK = 128
QUAD = 256
QUADS = INNER // QUAD
HALO = 16
VMEM_LIMIT = 56 * 1024 * 1024
LONG = pl.CostEstimate(flops=40000000000, bytes_accessed=1000000, transcendentals=0)
COST = pl.CostEstimate(flops=1000000, bytes_accessed=1000000, transcendentals=0)
F32 = jnp.float32
BF16 = jnp.bfloat16
HIGHEST = lax.Precision.HIGHEST
NT = (((1,), (1,)), ((), ()))
TN = (((0,), (0,)), ((), ()))


def iota(shape, axis):
    return lax.broadcasted_iota(jnp.int32, shape, axis)


def tie(value, *others):
    return lax.optimization_barrier((value,) + others)[0] if others else value


def mm(a, b):
    return jnp.dot(a, b, preferred_element_type=F32)


def mm_nt(a, b):
    return lax.dot_general(a, b, NT, preferred_element_type=F32)


def sigmoid(v):
    return 0.5 * jnp.tanh(0.5 * v) + 0.5


def split3(v):
    high = v.astype(BF16)
    rest = v - high.astype(F32)
    mid = rest.astype(BF16)
    low = (rest - mid.astype(F32)).astype(BF16)
    return high, mid, low


def mm_exact(v, ones):
    high, mid, low = split3(v)
    return mm(high, ones) + mm(mid, ones) + mm(low, ones)


def head_ones():
    return jnp.where((iota((128, INNER), 1) >> 6) == iota((128, INNER), 0), 1.0, 0.0).astype(BF16)


def two_heads(first, second):
    return jnp.where(iota((CHUNK, 128), 1) < HEAD_DIM, first, second)


def spread(cols, start):
    wide = [jnp.broadcast_to(cols[:, start + i : start + i + 1], (CHUNK, 128)) for i in range(4)]
    return wide, jnp.concatenate([two_heads(wide[0], wide[1]), two_heads(wide[2], wide[3])], axis=1)


def fold_rows(value):
    return jnp.sum(value.reshape(-1, 8, value.shape[1]), axis=0)


def columns_of(rows):
    count, length = rows.shape
    return jnp.concatenate([rows, jnp.zeros((128 - count, length), F32)], axis=0).T


def step_kernel(dt_ref, bias_ref, alog_ref, rows_ref, heads_ref, ecd_ref, total_ref):
    length = dt_ref.shape[0] - HALO
    raw = dt_ref[HALO:, :].astype(F32) + bias_ref[...]
    step = jnp.maximum(raw, 0.0) + jnp.log1p(jnp.exp(-jnp.abs(raw)))
    sig = 1.0 / (1.0 + jnp.exp(-raw))
    rate = -jnp.exp(alog_ref[...])
    pace = step * rate
    lower = jnp.where(iota((CHUNK, CHUNK), 0) >= iota((CHUNK, CHUNK), 1), 1.0, 0.0).astype(F32)
    inside, along = [], []
    offset = jnp.zeros((1, 128), F32)
    for start in range(0, length, CHUNK):
        part = jnp.dot(lower, pace[start : start + CHUNK], precision=HIGHEST, preferred_element_type=F32)
        inside.append(part)
        along.append(part + offset)
        offset = offset + part[CHUNK - 1 : CHUNK]
    cum = jnp.concatenate(inside, axis=0)
    along = jnp.concatenate(along, axis=0)
    ecd_ref[...] = jnp.exp(along)
    total_ref[...] = jnp.broadcast_to(jnp.exp(offset), (8, 128))
    left = jnp.exp(offset - along) * step
    heads_ref[...] = jnp.zeros_like(heads_ref)
    rows_ref[...] = jnp.zeros_like(rows_ref)
    for place, array in enumerate((cum, step, left)):
        turned = array.T
        for quad in range(QUADS):
            rows_ref[quad, 8 * place : 8 * place + 4, :] = turned[4 * quad : 4 * quad + 4, :]
    for place, array in enumerate((step, sig, jnp.broadcast_to(rate, (length, 128)))):
        turned = array.T
        for quad in range(QUADS):
            heads_ref[place, 8 * quad : 8 * quad + 4, :] = turned[4 * quad : 4 * quad + 4, :]


def step_call(projected, dt_bias, a_log):
    length = projected.shape[0] - HALO
    line = pl.BlockSpec((1, 128), lambda g: (0, 0))
    return pl.pallas_call(
        step_kernel,
        grid=(1,),
        in_specs=[pl.BlockSpec((length + HALO, 128), lambda g: (0, CONV // 128)), line, line],
        out_specs=(
            pl.BlockSpec((QUADS, 24, length), lambda g: (0, 0, 0)),
            pl.BlockSpec((3, 8 * QUADS, length), lambda g: (0, 0, 0)),
            pl.BlockSpec((length, 128), lambda g: (0, 0)),
            pl.BlockSpec((8, 128), lambda g: (0, 0)),
        ),
        out_shape=(
            jax.ShapeDtypeStruct((QUADS, 24, length), F32),
            jax.ShapeDtypeStruct((3, 8 * QUADS, length), F32),
            jax.ShapeDtypeStruct((length, 128), F32),
            jax.ShapeDtypeStruct((8, 128), F32),
        ),
        compiler_params=pltpu.CompilerParams(vmem_limit_bytes=VMEM_LIMIT),
        cost_estimate=COST,
        name="steps",
    )(projected, dt_bias, a_log)


def conv_kernel(
    share, v_ref, cw_ref, cb_ref, rows_ref, total_ref, *rest
):
    x_ref, slope_ref, b_ref, c_ref, bt_ref, ct_ref, state_ref, ext, weighted = rest[-9:]
    length = v_ref.shape[0] - HALO
    grid = pl.program_id(0)
    for plane in range(2):
        ext[plane] = v_ref[:, 128 * plane : 128 * plane + 128].astype(F32)

    def act(start):
        made = []
        for plane in range(2):
            lanes = slice(128 * plane, 128 * plane + 128)
            total = cb_ref[:, lanes] + cw_ref[0:1, lanes] * ext[plane, HALO - 3 + start : HALO - 3 + start + CHUNK, :]
            for tap in range(1, KW):
                at = HALO - 3 + tap + start
                total = total + cw_ref[tap : tap + 1, lanes] * ext[plane, at : at + CHUNK, :]
            sig = sigmoid(total)
            slope_ref[start : start + CHUNK, lanes] = (sig * (1.0 + total * (1.0 - sig))).astype(BF16)
            made.append(total * sig)
        return jnp.concatenate(made, axis=1)

    @pl.when(grid == 0)
    def _():
        for start in range(0, length, CHUNK):
            both = act(start)
            b_part, c_part = both[:, :STATE], both[:, STATE:]
            b_ref[start : start + CHUNK, :] = b_part.astype(BF16)
            c_ref[start : start + CHUNK, :] = c_part.astype(BF16)
            bt_ref[:, start : start + CHUNK] = b_part.T.astype(BF16)
            ct_ref[:, start : start + CHUNK] = c_part.T.astype(BF16)
        high, mid, low = split3(total_ref[0:1, :])
        row = iota((STATE, 128), 0) % share
        told = jnp.where(row == 0, high.astype(F32), jnp.where(row == 1, mid.astype(F32), jnp.where(row == 2, low.astype(F32), 0.0)))
        state_ref[:, :128] = told.astype(BF16)
        state_ref[:, 128:] = jnp.zeros((STATE, QUAD - 128), BF16)

    @pl.when(grid > 0)
    def _():
        cols = columns_of(rows_ref[0])
        for start in range(0, length, CHUNK):
            x_part = act(start)
            x_ref[start : start + CHUNK, :] = x_part.astype(BF16)
            _, left = spread(cols[start : start + CHUNK], 16)
            weighted[start : start + CHUNK, :] = (x_part * left).astype(BF16)
        state_ref[...] = mm(bt_ref[...], weighted[...]).astype(BF16)


def conv_call(ranks, v, conv_weight, conv_bias, rows, total, after):
    length = v.shape[0] - HALO
    last = QUADS
    block = lambda g: (0, (g + last) % (last + 1))
    quad = lambda g: (0, jnp.maximum(g - 1, 0))
    whole = lambda g: (0, 0)
    return pl.pallas_call(
        functools.partial(conv_kernel, STATE // ranks),
        grid=(last + 1,),
        in_specs=[
            pl.BlockSpec((length + HALO, QUAD), block),
            pl.BlockSpec((KW, QUAD), block),
            pl.BlockSpec((1, QUAD), block),
            pl.BlockSpec((1, 24, length), lambda g: (jnp.maximum(g - 1, 0), 0, 0)),
            pl.BlockSpec((8, 128), whole),
        ]
        + [pl.BlockSpec(memory_space=pl.ANY)] * len(after),
        out_specs=[
            pl.BlockSpec((length, QUAD), quad),
            pl.BlockSpec((length, QUAD), block),
            pl.BlockSpec((length, STATE), whole),
            pl.BlockSpec((length, STATE), whole),
            pl.BlockSpec((STATE, length), whole),
            pl.BlockSpec((STATE, length), whole),
            pl.BlockSpec((STATE, QUAD), block),
        ],
        scratch_shapes=[pltpu.VMEM((2, length + HALO, 128), F32), pltpu.VMEM((length, QUAD), BF16)],
        out_shape=[
            jax.ShapeDtypeStruct((length, INNER), BF16),
            jax.ShapeDtypeStruct((length, CONV), BF16),
            jax.ShapeDtypeStruct((length, STATE), BF16),
            jax.ShapeDtypeStruct((length, STATE), BF16),
            jax.ShapeDtypeStruct((STATE, length), BF16),
            jax.ShapeDtypeStruct((STATE, length), BF16),
            jax.ShapeDtypeStruct((STATE, CONV), BF16),
        ],
        compiler_params=pltpu.CompilerParams(vmem_limit_bytes=VMEM_LIMIT),
        cost_estimate=COST,
        name="conv_states",
    )(v, conv_weight, conv_bias, rows, total, *after)


def carry_kernel(ranks, backward, in_ref, *rest):
    share = STATE // ranks
    if backward:
        total_ref, out_ref = rest[0], rest[-1]
        decays = total_ref[...]
    else:
        out_ref, total_ref = rest[-2:]
        for place in range(ranks):
            told = in_ref[place * share : (place + 1) * share, INNER : INNER + 128].astype(F32)
            total_ref[place : place + 1, :] = told[0:1] + told[1:2] + told[2:3]
        decays = total_ref[...]
    wide = mm_exact(decays, head_ones())
    carry = jnp.zeros((share, INNER), F32)
    for place in range(ranks - 1, -1, -1) if backward else range(ranks):
        part = slice(place * share, (place + 1) * share)
        out_ref[part, :] = carry.astype(BF16)
        carry = wide[place : place + 1] * carry + in_ref[part, :INNER].astype(F32)


def carry_call(ranks, states, totals=None, after=()):
    backward = totals is not None
    vmem = pl.BlockSpec(memory_space=pltpu.VMEM)
    outs = [jax.ShapeDtypeStruct((STATE, INNER), BF16)]
    args = [states] + ([totals] if backward else [])
    if not backward:
        outs.append(jax.ShapeDtypeStruct((ranks, 128), F32))
    return pl.pallas_call(
        functools.partial(carry_kernel, ranks, backward),
        in_specs=[vmem] * len(args) + [pl.BlockSpec(memory_space=pl.ANY)] * len(after),
        out_specs=[vmem] * len(outs),
        out_shape=outs,
        compiler_params=pltpu.CompilerParams(vmem_limit_bytes=VMEM_LIMIT),
        cost_estimate=COST,
        name="carry_back" if backward else "carry",
    )(*args, *after)


def inside_kernel(x_ref, b_ref, c_ref, bt_ref, rows_ref, skip_ref, y_ref, scores):
    length = x_ref.shape[0]
    grid = pl.program_id(0)

    @pl.when(grid == 0)
    def _():
        for start in range(0, length, CHUNK):
            part = slice(start, start + CHUNK)
            scores[part, :] = mm_nt(c_ref[part, :], b_ref[part, :])

    cols = columns_of(rows_ref[0])
    lower = iota((CHUNK, CHUNK), 0) >= iota((CHUNK, CHUNK), 1)
    first = iota((CHUNK, 128), 1) < HEAD_DIM
    for start in range(0, length, CHUNK):
        part = slice(start, start + CHUNK)
        x_f = x_ref[part, :].astype(F32)
        wide, cum = spread(cols[part], 0)
        _, step = spread(cols[part], 8)
        weights = []
        for head in range(4):
            cum_row = rows_ref[0, head : head + 1, part]
            step_row = rows_ref[0, 8 + head : 9 + head, part]
            fade = jnp.exp(jnp.where(lower, wide[head] - cum_row, -1e30))
            weights.append((scores[part, :] * fade * step_row).astype(BF16))
        pieces = []
        for pair in range(2):
            x_pair = x_f[:, 128 * pair : 128 * pair + 128]
            both = jnp.concatenate([jnp.where(first, x_pair, 0.0), jnp.where(first, 0.0, x_pair)], axis=0)
            pieces.append(mm(jnp.concatenate(weights[2 * pair : 2 * pair + 2], axis=1), both.astype(BF16)))
        y_part = jnp.concatenate(pieces, axis=1) + skip_ref[...] * x_f
        if start > 0:
            y_part = y_part + jnp.exp(cum) * mm(c_ref[part, :], state.astype(BF16))
        y_ref[part, :] = y_part
        if start + CHUNK < length:
            end = cum[CHUNK - 1 : CHUNK]
            fresh = mm(bt_ref[:, part], (x_f * (jnp.exp(end - cum) * step)).astype(BF16))
            state = fresh if start == 0 else jnp.exp(end) * state + fresh


def inside_call(x_act, b_act, c_act, b_turned, rows, skip_wide):
    length = x_act.shape[0]
    whole = lambda g: (0, 0)
    quad = lambda g: (0, g)
    return pl.pallas_call(
        inside_kernel,
        grid=(QUADS,),
        in_specs=[
            pl.BlockSpec((length, QUAD), quad),
            pl.BlockSpec((length, STATE), whole),
            pl.BlockSpec((length, STATE), whole),
            pl.BlockSpec((STATE, length), whole),
            pl.BlockSpec((1, 24, length), lambda g: (g, 0, 0)),
            pl.BlockSpec((1, QUAD), quad),
        ],
        out_specs=pl.BlockSpec((length, QUAD), quad),
        out_shape=jax.ShapeDtypeStruct((length, INNER), F32),
        scratch_shapes=[pltpu.VMEM((length, CHUNK), F32)],
        compiler_params=pltpu.CompilerParams(vmem_limit_bytes=VMEM_LIMIT),
        cost_estimate=COST,
        name="ssd_inside",
    )(x_act, b_act, c_act, b_turned, rows, skip_wide)


def gate_kernel(
    y_ref, gate_ref, dn_ref, c_ref, ct_ref, ecd_ref, gain_ref, sin_ref,
    normed_ref, dgate_ref, dm_ref, dgain_ref, out_ref, ones, ecd, gated, silu, slope, back,
):
    grid = pl.program_id(0)

    @pl.when(grid == 0)
    def _():
        ones[...] = head_ones()
        back[...] = jnp.zeros_like(back)
        dgain_ref[...] = jnp.zeros_like(dgain_ref)

    high, mid, _ = split3(ecd_ref[...])
    squares = jnp.zeros((CHUNK, QUAD), F32)
    product = jnp.zeros((CHUNK, QUAD), F32)
    for at in range(0, INNER, QUAD):
        lanes = slice(at, at + QUAD)
        grown = mm(high, ones[:, lanes]) + mm(mid, ones[:, lanes])
        ecd[:, lanes] = grown
        mixed = y_ref[:, lanes] + grown * mm(c_ref[...], sin_ref[:, lanes])
        mixed = mixed.astype(BF16).astype(F32)
        gate = gate_ref[:, lanes].astype(F32)
        sig = sigmoid(gate)
        open_part = gate * sig
        value = mixed * open_part
        silu[:, lanes] = open_part
        slope[:, lanes] = mixed * (sig * (1.0 + gate * (1.0 - sig)))
        gated[:, lanes] = value
        squares = squares + value * value
        product = product + dn_ref[:, lanes] * gain_ref[:, lanes] * value
    inverse = lax.rsqrt(jnp.sum(squares, axis=1, keepdims=True) * (1.0 / INNER) + EPSILON)
    shift = inverse * inverse * inverse * (jnp.sum(product, axis=1, keepdims=True) * (1.0 / INNER))
    inverse = jnp.broadcast_to(inverse, (CHUNK, QUAD))
    shift = jnp.broadcast_to(shift, (CHUNK, QUAD))
    for at in range(0, INNER, QUAD):
        lanes = slice(at, at + QUAD)
        value = gated[:, lanes]
        scaled = value * inverse
        gain = gain_ref[:, lanes]
        dn = dn_ref[:, lanes]
        normed_ref[:, lanes] = (scaled * gain).astype(BF16)
        dgain_ref[:, lanes] += jnp.sum(dn * scaled, axis=0, keepdims=True)
        d_gated = inverse * (dn * gain) - value * shift
        dgate_ref[:, lanes] = (d_gated * slope[:, lanes]).astype(BF16)
        d_mixed = (d_gated * silu[:, lanes]).astype(BF16)
        dm_ref[:, lanes] = d_mixed
        back[:, lanes] += mm(ct_ref[...], (d_mixed.astype(F32) * ecd[:, lanes]).astype(BF16))

    @pl.when(grid == pl.num_programs(0) - 1)
    def _():
        out_ref[...] = back[...].astype(BF16)


def gate_call(y_inside, gate_in, d_normed, c_act, c_turned, ecd, out_gain, s_in):
    length = y_inside.shape[0]
    whole = lambda g: (0, 0)
    down = lambda g: (g, 0)
    wide = pl.BlockSpec((CHUNK, INNER), down)
    rows = jax.ShapeDtypeStruct((length, INNER), BF16)
    state = pl.BlockSpec((STATE, INNER), whole)
    line = pl.BlockSpec((1, INNER), whole)
    return pl.pallas_call(
        gate_kernel,
        grid=(length // CHUNK,),
        in_specs=[
            wide,
            wide,
            wide,
            pl.BlockSpec((CHUNK, STATE), down),
            pl.BlockSpec((STATE, CHUNK), lambda g: (0, g)),
            pl.BlockSpec((CHUNK, 128), down),
            line,
            state,
        ],
        out_specs=[wide, wide, wide, line, state],
        out_shape=[rows, rows, rows, jax.ShapeDtypeStruct((1, INNER), F32), jax.ShapeDtypeStruct((STATE, INNER), BF16)],
        scratch_shapes=[pltpu.VMEM((128, INNER), BF16)]
        + [pltpu.VMEM((CHUNK, INNER), F32)] * 4
        + [pltpu.VMEM((STATE, INNER), F32)],
        compiler_params=pltpu.CompilerParams(vmem_limit_bytes=VMEM_LIMIT),
        cost_estimate=COST,
        name="gated_norm",
    )(y_inside, gate_in, d_normed, c_act, c_turned, ecd, out_gain, s_in)


def back_kernel(
    x_ref, dm_ref, slope_ref, v_ref, cw_ref, b_ref, c_ref, bt_ref, ct_ref, rows_ref, table_ref, skip_ref, sin_ref, rin_ref, *rest
):
    dv_ref, sums_ref, heads_ref = rest[-14:-11]
    scores, d_scores, d_b, d_c, states, products, grads, ext, marks, across, crossing = rest[-11:]
    length = x_ref.shape[0]
    chunks = length // CHUNK
    grid = pl.program_id(0)

    @pl.when(grid == 0)
    def _():
        for start in range(0, length, CHUNK):
            part = slice(start, start + CHUNK)
            scores[part, :] = mm_nt(b_ref[part, :], c_ref[part, :])
        d_scores[...] = jnp.zeros_like(d_scores)
        d_b[...] = jnp.zeros_like(d_b)
        d_c[...] = jnp.zeros_like(d_c)
        marks[...] = jnp.zeros_like(marks)
        grads[:, 0:HALO, :] = jnp.zeros((2, HALO, 128), F32)
        grads[:, HALO + length :, :] = jnp.zeros((2, HALO, 128), F32)

    def finish(extra):
        for plane in range(2):
            lanes = slice(128 * plane, 128 * plane + 128)
            ext[plane] = v_ref[:, lanes].astype(F32)
            total = [jnp.zeros((8, 128), F32)] * (KW + 1)
            for start in range(0, length, CHUNK):
                here = grads[plane, HALO + start : HALO + start + CHUNK, :]
                for tap in range(KW):
                    at = HALO - 3 + tap + start
                    total[tap] = total[tap] + fold_rows(here * ext[plane, at : at + CHUNK, :])
                total[KW] = total[KW] + fold_rows(here)
            for at, rows in enumerate(total):
                sums_ref[at : at + 1, lanes] = jnp.sum(rows, axis=0, keepdims=True)
            for start in [0] + list(range(HALO, HALO + length, CHUNK)):
                count = HALO if start == 0 else CHUNK
                value = cw_ref[KW - 1 : KW, lanes] * grads[plane, start : start + count, :]
                for tap in range(KW - 1):
                    at = start + KW - 1 - tap
                    value = value + cw_ref[tap : tap + 1, lanes] * grads[plane, at : at + count, :]
                place = length if start == 0 else start - HALO
                dv_ref[place : place + count, lanes] = value.astype(BF16)
        sums_ref[KW + 1 : KW + 2, :] = extra
        sums_ref[KW + 2 : 8, :] = jnp.zeros((8 - KW - 2, QUAD), F32)

    def keep(start, value):
        for plane in range(2):
            grads[plane, HALO + start : HALO + start + CHUNK, :] = value[:, 128 * plane : 128 * plane + 128]

    @pl.when(grid < QUADS)
    def _():
        cols = columns_of(rows_ref[0])
        upper = iota((CHUNK, CHUNK), 0) <= iota((CHUNK, CHUNK), 1)
        first = iota((CHUNK, 128), 1) < HEAD_DIM
        lane = iota((CHUNK, 128), 1) - 8 * grid
        line = iota((8, 128), 0)
        ones = jnp.where(iota((QUAD, 128), 1) - 8 * grid == iota((QUAD, 128), 0) >> 6, 1.0, 0.0).astype(BF16)
        mine = pl.ds(pl.multiple_of(grid * 8, 8), 8)
        skip = skip_ref[...]
        after = rin_ref[...].astype(F32)
        state = sin_ref[...].astype(F32)
        spreads = []
        for chunk in range(chunks):
            part = slice(chunk * CHUNK, chunk * CHUNK + CHUNK)
            states[chunk] = state
            spreads.append(spread(cols[part], 0) + spread(cols[part], 8))
            _, cum, _, step = spreads[chunk]
            if chunk + 1 < chunks:
                end = cum[CHUNK - 1 : CHUNK]
                fed = (x_ref[part, :].astype(F32) * (jnp.exp(end - cum) * step)).astype(BF16)
                state = jnp.exp(end) * state + mm(bt_ref[:, part], fed)
        skip_sum = jnp.zeros((8, QUAD), F32)
        for chunk in range(chunks - 1, -1, -1):
            part = slice(chunk * CHUNK, chunk * CHUNK + CHUNK)
            x_f = x_ref[part, :].astype(F32)
            dm = dm_ref[part, :]
            dm_f = dm.astype(F32)
            cum_wide, cum, _, step = spreads[chunk]
            end = cum[CHUNK - 1 : CHUNK]
            after_low = after.astype(BF16)
            state = states[chunk]
            left = jnp.exp(end - cum)
            grown = dm_f * jnp.exp(cum)
            grown_low = grown.astype(BF16)
            faded = x_f * left
            fed = x_f * step
            from_after = mm(b_ref[part, :], after_low)
            from_state = mm(c_ref[part, :], state.astype(BF16))
            d_b[part, :] += mm_nt((faded * step).astype(BF16), after_low)
            d_c[part, :] += mm_nt(grown_low, state.astype(BF16))
            products[0, part, :] = (grown * from_state).astype(BF16)
            products[1, part, :] = (faded * from_after).astype(BF16)
            within = jnp.zeros((CHUNK, 128), F32)
            pair_sum = jnp.zeros((8, CHUNK), F32)
            cross_sum = jnp.zeros((8, 128), F32)
            cross = jnp.sum(state * after, axis=0, keepdims=True) * jnp.exp(end)
            summed = None
            pieces = []
            for pair in range(2):
                lanes = slice(128 * pair, 128 * pair + 128)
                x_pair, dm_pair = fed[:, lanes], dm_f[:, lanes]
                x_both = jnp.concatenate([jnp.where(first, x_pair, 0.0), jnp.where(first, 0.0, x_pair)], axis=0)
                dm_both = jnp.concatenate([jnp.where(first, dm_pair, 0.0), jnp.where(first, 0.0, dm_pair)], axis=0)
                d_weights = mm_nt(x_both.astype(BF16), dm[:, lanes])
                kept = []
                for half in range(2):
                    head = 2 * pair + half
                    cum_row = rows_ref[0, head : head + 1, part]
                    fade = jnp.exp(jnp.where(upper, cum_row - cum_wide[head], -1e30))
                    faded_grad = d_weights[half * CHUNK : half * CHUNK + CHUNK] * fade
                    summed = faded_grad if summed is None else summed + faded_grad
                    joint = faded_grad * scores[part, :]
                    within = jnp.where(lane == head, jnp.sum(joint, axis=1, keepdims=True), within)
                    pair_sum = jnp.where(line == head, jnp.sum(joint, axis=0, keepdims=True), pair_sum)
                    kept.append((scores[part, :] * fade).astype(BF16))
                    here = (iota((1, QUAD), 1) >> 6) == head
                    amount = jnp.sum(jnp.where(here, cross, 0.0), axis=1, keepdims=True)
                    cross_sum = jnp.where(line == head, amount, cross_sum)
                pieces.append(mm(jnp.concatenate(kept, axis=1), dm_both.astype(BF16)))
            d_scores[part, :] += summed
            marks[0, part, :] += within
            across[mine, part] = pair_sum
            crossing[chunk, mine, :] = cross_sum
            direct = jnp.concatenate(pieces, axis=1) + left * from_after
            products[2, part, :] = (x_f * direct).astype(BF16)
            d_x = step * direct + skip * dm_f
            keep(chunk * CHUNK, d_x * slope_ref[part, :].astype(F32))
            skip_sum = skip_sum + fold_rows(x_f * dm_f)
            after = jnp.exp(end) * after + mm(ct_ref[:, part], grown_low)
        for at in range(3):
            marks[1 + at] += mm(products[at], ones)
        finish(jnp.sum(skip_sum, axis=0, keepdims=True))

    @pl.when(grid == QUADS)
    def _():
        for start in range(0, length, CHUNK):
            part = slice(start, start + CHUNK)
            low = d_scores[part, :].astype(BF16)
            into_b = d_b[part, :] + mm(low, c_ref[part, :])
            into_c = d_c[part, :] + mm(d_scores[part, :].T.astype(BF16), b_ref[part, :])
            both = jnp.concatenate([into_b, into_c], axis=1)
            keep(start, both * slope_ref[part, :].astype(F32))
        finish(jnp.zeros((1, QUAD), F32))

    @pl.when(grid == QUADS + 1)
    def _():
        square = (CHUNK, CHUNK)
        later = jnp.where(iota(square, 0) >= iota(square, 1), 1.0, 0.0).astype(BF16)
        before = jnp.where(iota(square, 0) < iota(square, 1), 1.0, 0.0).astype(BF16)
        row, column = iota((128, QUAD), 0), iota((128, QUAD), 1)
        pick = (column < HEADS) & (row == 8 * (column >> 2) + (column & 3))
        pick = jnp.where(pick, 1.0, 0.0).astype(BF16)
        used = 8 * QUADS
        bias_sum = jnp.zeros((used, 1), F32)
        rate_sum = jnp.zeros((used, 1), F32)
        dv_ref[length:, :] = jnp.zeros((HALO, QUAD), BF16)
        for chunk in range(chunks):
            part = slice(chunk * CHUNK, chunk * CHUNK + CHUNK)
            within, carried, outward, direct = [marks[at, part, :].T[:used] for at in range(4)]
            step, sig, rate = [table_ref[at, :, part] for at in range(3)]
            change = across[0:used, part] - within + carried
            decay = mm_exact(change, later) + mm_exact(step * outward, before) + crossing[chunk]
            d_raw = (direct + rate * decay) * sig
            bias_sum = bias_sum + jnp.sum(d_raw, axis=1, keepdims=True)
            rate_sum = rate_sum + jnp.sum(step * decay, axis=1, keepdims=True)
            turned = jnp.concatenate([d_raw, jnp.zeros((128 - used, CHUNK), F32)], axis=0).T.astype(BF16)
            dv_ref[part, :] = mm(turned, pick).astype(BF16)
        heads_ref[0] = jnp.broadcast_to(bias_sum, (used, 128))
        heads_ref[1] = jnp.broadcast_to(rate_sum, (used, 128))


def back_call(x_act, d_mixed, slope, v, conv_weight, b_act, c_act, b_turned, c_turned, rows, table, skip_wide, s_in, r_in, after):
    length = x_act.shape[0]
    whole = lambda g: (0, 0)
    quad = lambda g: (0, jnp.minimum(g, QUADS - 1))
    block = lambda g: (0, jnp.minimum(g, QUADS))
    lead = lambda g: (jnp.minimum(g, QUADS - 1), 0, 0)
    return pl.pallas_call(
        back_kernel,
        grid=(QUADS + 2,),
        in_specs=[
            pl.BlockSpec((length, QUAD), quad),
            pl.BlockSpec((length, QUAD), quad),
            pl.BlockSpec((length, QUAD), block),
            pl.BlockSpec((length + HALO, QUAD), block),
            pl.BlockSpec((KW, QUAD), block),
            pl.BlockSpec((length, STATE), whole),
            pl.BlockSpec((length, STATE), whole),
            pl.BlockSpec((STATE, length), whole),
            pl.BlockSpec((STATE, length), whole),
            pl.BlockSpec((1, 24, length), lead),
            pl.BlockSpec((3, 8 * QUADS, length), lambda g: (0, 0, 0)),
            pl.BlockSpec((1, QUAD), quad),
            pl.BlockSpec((STATE, QUAD), quad),
            pl.BlockSpec((STATE, QUAD), quad),
        ]
        + [pl.BlockSpec(memory_space=pl.ANY)] * len(after),
        out_specs=[
            pl.BlockSpec((length + HALO, QUAD), lambda g: (0, g)),
            pl.BlockSpec((8, QUAD), block),
            pl.BlockSpec((2, 8 * QUADS, 128), lambda g: (0, 0, 0)),
        ],
        scratch_shapes=[
            pltpu.VMEM((length, CHUNK), F32),
            pltpu.VMEM((length, CHUNK), F32),
            pltpu.VMEM((length, STATE), F32),
            pltpu.VMEM((length, STATE), F32),
            pltpu.VMEM((length // CHUNK, STATE, QUAD), F32),
            pltpu.VMEM((3, length, QUAD), BF16),
            pltpu.VMEM((2, length + 2 * HALO, 128), F32),
            pltpu.VMEM((2, length + HALO, 128), F32),
            pltpu.VMEM((4, length, 128), F32),
            pltpu.VMEM((128, length), F32),
            pltpu.VMEM((length // CHUNK, 8 * QUADS, 128), F32),
        ],
        out_shape=[
            jax.ShapeDtypeStruct((length + HALO, CONV + QUAD), BF16),
            jax.ShapeDtypeStruct((8, CONV), F32),
            jax.ShapeDtypeStruct((2, 8 * QUADS, 128), F32),
        ],
        compiler_params=pltpu.CompilerParams(vmem_limit_bytes=VMEM_LIMIT),
        cost_estimate=LONG,
        name="ssd_back",
    )(x_act, d_mixed, slope, v, conv_weight, b_act, c_act, b_turned, c_turned, rows, table, skip_wide, s_in, r_in, *after)


def put_quarters(place_ref, count, step, refs, put):
    near = (step // 2) == place_ref[count]
    for at in range(2, count):
        for index in range(4):
            wanted = near if index < 2 else jnp.logical_not(near)

            @pl.when(wanted & (step % 2 == index % 2))
            def _():
                put(at, refs[2 + 4 * (at - 2) + index])


def put_quarters(place_ref, count, step, refs, put):
    near = (step // 2) == place_ref[count]
    for at in range(2, count):
        for index in range(4):
            wanted = near if index < 2 else jnp.logical_not(near)

            @pl.when(wanted & (step % 2 == index % 2))
            def _():
                put(at, refs[2 + 4 * (at - 2) + index])


def weight_kernel(height, split, count, place_ref, x_ref, *rest):
    piece_refs, (out_ref, w_ref) = rest[:-2], rest[-2:]

    def put(at, ref):
        w_ref[:, pl.ds(pl.multiple_of(place_ref[at] * height, 128), height)] = ref[...]

    for at in range(2 if split else count):
        put(at, piece_refs[at])
    for at in range(2, count if split else 2):
        for index in range(2):

            @pl.when(pl.program_id(0) == index)
            def _():
                put(at, piece_refs[2 + 2 * (at - 2) + index])

    out_ref[...] = mm_nt(x_ref[...], w_ref[...]).astype(BF16)


def weight_call(x, pieces, places, count, width, block, name, split="", into=None):
    rows, depth = x.shape
    height = pieces[0].shape[1]

    def block_of(g, place):
        if not split:
            return g
        side = place[count]
        if split == "halves":
            return jnp.where(g == 0, side, 1 - side)
        return 2 * (1 - side if split == "far" else side) + g

    def spec(at):
        if split and at >= 2:
            return pl.BlockSpec((block, height), lambda g, place: (0, 0))
        return pl.BlockSpec((block, height), lambda g, place: (block_of(g, place), 0))

    extra = [] if into is None else [into]
    grid_spec = pltpu.PrefetchScalarGridSpec(
        num_scalar_prefetch=1,
        grid=(2 if split else width // block,),
        in_specs=[pl.BlockSpec((rows, depth), lambda g, place: (0, 0))]
        + [spec(at) for at in range(len(pieces))]
        + [pl.BlockSpec(memory_space=pl.ANY)] * len(extra),
        out_specs=pl.BlockSpec((rows, block), lambda g, place: (0, block_of(g, place))),
        scratch_shapes=[pltpu.VMEM((block, depth), BF16)],
    )
    return pl.pallas_call(
        functools.partial(weight_kernel, height, split, count),
        grid_spec=grid_spec,
        out_shape=jax.ShapeDtypeStruct((rows, width), BF16),
        input_output_aliases={2 + len(pieces): 0} if extra else {},
        compiler_params=pltpu.CompilerParams(vmem_limit_bytes=VMEM_LIMIT),
        cost_estimate=COST,
        name=name,
    )(places, x, *pieces, *extra)


def weight_back_kernel(place_ref, g_ref, *rest):
    out_ref = rest[-1]
    for at, piece_ref in enumerate(rest[: place_ref.shape[0]]):

        @pl.when(pl.program_id(0) == at)
        def _():
            out_ref[...] = mm_nt(g_ref[...], piece_ref[...])


def weight_back_call(g, pieces, places, width, into=None):
    rows, depth = g.shape
    block = pieces[0].shape[0]
    extra = [] if into is None else [into]
    grid_spec = pltpu.PrefetchScalarGridSpec(
        num_scalar_prefetch=1,
        grid=(len(pieces),),
        in_specs=[pl.BlockSpec((rows, depth), lambda k, place: (0, 0))]
        + [pl.BlockSpec((block, depth), lambda k, place: (0, 0))] * len(pieces)
        + [pl.BlockSpec(memory_space=pl.ANY)] * len(extra),
        out_specs=pl.BlockSpec((rows, block), lambda k, place: (0, place[k])),
    )
    return pl.pallas_call(
        weight_back_kernel,
        grid_spec=grid_spec,
        out_shape=jax.ShapeDtypeStruct((rows, width), F32),
        input_output_aliases={2 + len(pieces): 0} if extra else {},
        compiler_params=pltpu.CompilerParams(vmem_limit_bytes=VMEM_LIMIT),
        cost_estimate=COST,
        name="d_normed_out",
    )(places, g, *pieces, *extra)


def pick_kernel(table_ref, own, other, own_halo, other_halo, own_out, other_out, halo_out):
    parts, blocks = own_out.shape[:2]
    for part in range(parts):

        @pl.loop(0, blocks)
        def _(at):
            block = table_ref[part, at]
            own_out[part, at] = own[block]
            other_out[part, at] = other[block]
            halo_out[part, at, :, :HALO] = own_halo[block]
            halo_out[part, at, :, HALO:] = other_halo[block]


def pick_call(table, own, other, own_halo, other_halo):
    parts, blocks = table.shape
    _, height, length = own.shape
    vmem = pl.BlockSpec(memory_space=pltpu.VMEM)
    made = pl.pallas_call(
        pick_kernel,
        in_specs=[pl.BlockSpec(memory_space=pltpu.SMEM)] + [vmem] * 4,
        out_specs=[vmem] * 3,
        out_shape=[jax.ShapeDtypeStruct((parts, blocks, height, length), BF16)] * 2
        + [jax.ShapeDtypeStruct((parts, blocks, height, 2 * HALO), BF16)],
        compiler_params=pltpu.CompilerParams(vmem_limit_bytes=VMEM_LIMIT),
        cost_estimate=COST,
        name="pick_rows",
    )(table, own, other, own_halo, other_halo)
    return [array.reshape(parts, blocks * height, -1) for array in made]


def grad_kernel(halo, *refs):
    outs = refs[-6:]
    own, other = refs[0][0], refs[1][0]
    if halo:
        edge, right, right_other, edge_right, edge_other = refs[2][0], refs[3], refs[4], refs[5], refs[6]
    else:
        right, right_other = refs[2], refs[3]
    total = mm(own, right[...]) + mm(other, right_other[...])
    if halo:
        total = total + mm(edge, jnp.concatenate([edge_right[...], edge_other[...]], axis=0))
    half = total.shape[0] // 2
    for part in range(3):

        @pl.when(pl.program_id(0) == part)
        def _():
            outs[2 * part][...] = total[:half].astype(BF16)
            outs[2 * part + 1][...] = total[half:].astype(BF16)


def grad_call(lefts, right, right_other, first, width, halo, name):
    own, other, edge = lefts
    _, rows, length = own.shape
    lead = lambda g: (g, 0, 0)
    column = lambda g: (0, first + g)
    below = lambda g: (length // HALO, first + g)
    specs = [pl.BlockSpec((1, rows, length), lead)] * 2
    args = [own, other]
    if halo:
        specs.append(pl.BlockSpec((1, rows, 2 * HALO), lead))
        args.append(edge)
    specs += [pl.BlockSpec((length, width), column)] * 2
    args += [right, right_other]
    if halo:
        specs += [pl.BlockSpec((HALO, width), below)] * 2
        args += [right, right_other]
    made = pl.pallas_call(
        functools.partial(grad_kernel, halo),
        grid=(3,),
        in_specs=specs,
        out_specs=[pl.BlockSpec((rows // 2, width), lambda g: (0, 0))] * 6,
        out_shape=[jax.ShapeDtypeStruct((rows // 2, width), BF16)] * 6,
        compiler_params=pltpu.CompilerParams(vmem_limit_bytes=VMEM_LIMIT),
        cost_estimate=COST,
        name=name,
    )(*args)
    return [(made[2 * part], made[2 * part + 1]) for part in range(3)]


def fold_kernel(parts, groups, which, *refs):
    ins, outs = refs[: 2 * parts * groups], refs[2 * parts * groups :]
    for part in range(parts):
        at = 0
        for group in range(groups):
            kept, got = ins[2 * (part * groups + group)], ins[2 * (part * groups + group) + 1]
            rows, width = kept.shape
            half = rows // 2
            lines = slice(0, rows) if which == "last" else slice(0, half) if which == "kept" else slice(half, rows)
            total = kept[lines, :].astype(F32) + got[lines, :].astype(F32)
            if which == "last":
                gate = INNER // parts
                other = width - gate
                outs[0][:, part * gate : (part + 1) * gate] = total[:, :gate]
                begin = INNER + part * other
                end = min(begin + other, outs[0].shape[1])
                outs[0][:, begin:end] = total[:, gate : gate + end - begin]
            else:
                outs[part][:, at : at + width] = total.astype(BF16)
            at += width


def fold_call(pairs, which, width=0):
    parts, groups = len(pairs), len(pairs[0])
    arrays = [array for part in pairs for pair in part for array in pair]
    rows = arrays[0].shape[0]
    half = rows // 2
    if which == "last":
        shapes = [jax.ShapeDtypeStruct((rows, width), F32)]
    else:
        shapes = [jax.ShapeDtypeStruct((half, sum(kept.shape[1] for kept, _ in part)), BF16) for part in pairs]
    vmem = pl.BlockSpec(memory_space=pltpu.VMEM)
    return pl.pallas_call(
        functools.partial(fold_kernel, parts, groups, which),
        in_specs=[vmem] * len(arrays),
        out_specs=[vmem] * len(shapes),
        out_shape=shapes,
        compiler_params=pltpu.CompilerParams(vmem_limit_bytes=VMEM_LIMIT),
        cost_estimate=COST,
        name="fold_" + which,
    )(*arrays)


def residual_kernel(place_ref, *refs):
    count = len(refs) // 2 - 1
    total = refs[2 * count][0].astype(F32)
    for at in range(count):
        total = total + mm(refs[at][...], refs[count + at][...])
    refs[-1][0] = total


def residual_call(x, pieces, places, tokens, after):
    rows = x.shape[0]
    height, width = pieces[0].shape
    block = 768
    part = lambda at: pl.BlockSpec((rows, height), lambda g, place: (0, place[at]))
    whole = pl.BlockSpec((1, rows, block), lambda g, place: (0, 0, g))
    grid_spec = pltpu.PrefetchScalarGridSpec(
        num_scalar_prefetch=1,
        grid=(width // block,),
        in_specs=[part(at) for at in range(len(pieces))]
        + [pl.BlockSpec((height, block), lambda g, place: (0, g))] * len(pieces)
        + [whole],
        out_specs=whole,
    )
    return pl.pallas_call(
        residual_kernel,
        grid_spec=grid_spec,
        out_shape=jax.ShapeDtypeStruct((1, rows, width), F32),
        compiler_params=pltpu.CompilerParams(vmem_limit_bytes=VMEM_LIMIT),
        cost_estimate=LONG,
        name="block_out",
    )(tie(places, after), *([x] * len(pieces)), *pieces, tokens)


def columns_kernel(count, split, place_ref, g_ref, *refs):
    out_ref, w = refs[-2:]
    height = D // count
    step = pl.program_id(0)

    def put(at, ref):
        w[:, pl.ds(pl.multiple_of(place_ref[at] * height, 128), height)] = ref[...]

    for at in range(2 if split else count):
        put(at, refs[at])
    for at in range(2, count if split else 2):
        for index in range(2):
            side = place_ref[count]

            @pl.when(step == (side if index == 0 else 1 - side))
            def _():
                put(at, refs[2 + 2 * (at - 2) + index])

    product = mm(g_ref[...], w[...])

    @pl.when(step == 0)
    def _():
        out_ref[...] = product

    @pl.when(step > 0)
    def _():
        out_ref[...] += product


def columns_call(g, pieces, places, count, split):
    length, depth = g.shape
    height = pieces[0].shape[1]
    block = depth // 2
    down = lambda k, place: (k, 0)
    whole = lambda k, place: (0, 0)
    grid_spec = pltpu.PrefetchScalarGridSpec(
        num_scalar_prefetch=1,
        grid=(2,),
        in_specs=[pl.BlockSpec((length, block), lambda k, place: (0, k))]
        + [pl.BlockSpec((block, height), whole if split and at >= 2 else down) for at in range(len(pieces))],
        out_specs=pl.BlockSpec((length, D), whole),
        scratch_shapes=[pltpu.VMEM((block, D), BF16)],
    )
    return pl.pallas_call(
        functools.partial(columns_kernel, count, split),
        grid_spec=grid_spec,
        out_shape=jax.ShapeDtypeStruct((length, D), F32),
        compiler_params=pltpu.CompilerParams(vmem_limit_bytes=VMEM_LIMIT),
        cost_estimate=COST,
        name="d_normed_gate",
    )(places, g, *pieces)


def tokens_kernel(count, quarters, place_ref, *refs):
    part_ref, dv_ref, spill_ref, tokens_ref, cotan_ref, gain_ref = refs[:6]
    wv_refs = refs[6:-6]
    out_ref, dgain_ref, fixed, wv, total, inverse = refs[-6:]
    length = dv_ref.shape[0]
    height = D // count
    step, steps = pl.program_id(0), pl.num_programs(0)

    @pl.when(step == 0)
    def _():
        for start in range(0, length, CHUNK):
            part = slice(start, start + CHUNK)
            values = tokens_ref[0, part, :].astype(F32)
            mean = jnp.sum(values * values, axis=1, keepdims=True) * (1.0 / D)
            inverse[part, :] = jnp.broadcast_to(lax.rsqrt(mean + EPSILON), (CHUNK, 128))

    fixed[...] = dv_ref[...]
    ends = dv_ref[length - HALO :, :].astype(F32) + spill_ref[...].astype(F32)
    fixed[length - HALO :, :] = ends.astype(BF16)

    def put(at, ref):
        wv[:, pl.ds(pl.multiple_of(place_ref[at] * height, 128), height)] = ref[...]

    for at in range(2 if quarters else count):
        put(at, wv_refs[at])
    if quarters:
        put_quarters(place_ref, count, step, wv_refs, put)
    product = mm(fixed[...], wv[...])

    @pl.when(step == 0)
    def _():
        total[...] = part_ref[...] + product

    @pl.when(step > 0)
    def _():
        total[...] += product

    @pl.when(step == steps - 1)
    def _():
        sums = jnp.zeros((8, D), F32)
        for start in range(0, length, CHUNK):
            part = slice(start, start + CHUNK)
            values = tokens_ref[0, part, :].astype(F32)
            grad = total[part, :]
            a = grad * gain_ref[...]
            inv = inverse[part, 0:1]
            sums = sums + fold_rows(grad * values * inv)
            shift = inv * inv * inv * (jnp.sum(a * values, axis=1, keepdims=True) * (1.0 / D))
            out_ref[0, part, :] = cotan_ref[0, part, :].astype(F32) + inv * a - values * shift
        dgain_ref[...] = jnp.sum(sums, axis=0, keepdims=True)


def tokens_call(part, d_v, spill, pieces, places, quarters, tokens, cotangent, gain):
    length = part.shape[0]
    height = pieces[0].shape[1]
    wide = d_v.shape[1]
    steps = 4
    block = wide // steps
    count = D // height
    whole = lambda k, place: (0, 0)
    column = lambda k, place: (0, k)
    down = lambda k, place: (k, 0)
    all_rows = pl.BlockSpec((1, length, D), lambda k, place: (0, 0, 0))
    grid_spec = pltpu.PrefetchScalarGridSpec(
        num_scalar_prefetch=1,
        grid=(steps,),
        in_specs=[
            pl.BlockSpec((length, D), whole),
            pl.BlockSpec((length, block), column),
            pl.BlockSpec((HALO, block), column),
            all_rows,
            all_rows,
            pl.BlockSpec((1, D), whole),
        ]
        + [pl.BlockSpec((block, height), whole if quarters and at >= 2 else down) for at in range(len(pieces))],
        out_specs=[all_rows, pl.BlockSpec((1, D), whole)],
        scratch_shapes=[
            pltpu.VMEM((length, block), BF16),
            pltpu.VMEM((block, D), BF16),
            pltpu.VMEM((length, D), F32),
            pltpu.VMEM((length, 128), F32),
        ],
    )
    return pl.pallas_call(
        functools.partial(tokens_kernel, count, quarters),
        grid_spec=grid_spec,
        out_shape=[jax.ShapeDtypeStruct((1, length, D), F32), jax.ShapeDtypeStruct((1, D), F32)],
        compiler_params=pltpu.CompilerParams(vmem_limit_bytes=VMEM_LIMIT),
        cost_estimate=COST,
        name="d_tokens",
    )(places, part, d_v, spill, tokens, cotangent, gain, *pieces)


def on_device(
    ranks,
    shards,
    tokens,
    norm_gain,
    w_in,
    conv_weight,
    conv_bias,
    dt_bias,
    a_log,
    skip_gain,
    out_gain,
    w_out,
    cotangent,
):
    both = ("seq", "fsdp")
    rank = lax.axis_index("seq")
    shard = lax.axis_index("fsdp")

    def move(value, target):
        pairs = []
        for s in range(ranks):
            for f in range(shards):
                goal = target(s, f)
                if goal is not None:
                    pairs.append((s * shards + f, goal[0] * shards + goal[1]))
        return lax.ppermute(value, both, pairs)

    def across(value):
        return move(value, lambda s, f: (s, f ^ 1))

    def send_near(value):
        return [(move(value, lambda s, f: (s, f ^ step)), step) for step in range(2, shards, 2)]

    def gather_quarters(value, crossed):
        quarter = value.shape[0] // 4
        side = rank & 1
        remote = []
        for step in range(2, shards, 2):
            near, far = [], []
            for part in range(2):
                sent = lax.dynamic_slice_in_dim(value, (2 * side + part) * quarter, quarter, 0)
                near.append(move(tie(sent, *near), lambda s, f: (s, f ^ step)))
                far.append(move(near[part], lambda s, f: (s ^ 1, f)))
            remote.append((near, far))
        crossed_near = [[across(piece) for piece in near] for near, _ in remote]
        places = [shard, shard ^ 1] + [shard ^ step for step in range(2, shards, 2)]
        places += [shard ^ step ^ 1 for step in range(2, shards, 2)] + [side]

        def pieces(ready):
            made = [value, crossed] + [piece for near, far in remote for piece in near + far]
            for near, (_, far) in zip(crossed_near, remote):
                made += near + [None] * 2 if ready is None else near + [across(far[0]), across(tie(far[1], ready))]
            return made

        return pieces, jnp.stack(places).astype(jnp.int32)

    def in_order(pieces, places, cuts):
        height = pieces[0].shape[1]
        whole = jnp.zeros((pieces[0].shape[0], height * shards), pieces[0].dtype)
        for at, piece in enumerate(pieces):
            first, place = 0, at
            if at >= 2:
                place, index = 2 + (at - 2) // (2 * cuts), (at - 2) % (2 * cuts)
                side = places[shards] if index < cuts else 1 - places[shards]
                first = (cuts * side + index % cuts) * piece.shape[0]
            whole = lax.dynamic_update_slice(whole, piece, (first, places[place] * height))
        return [whole], jnp.zeros((1,), jnp.int32)

    def exchange(states):
        return lax.all_to_all(states, "seq", split_axis=0, concat_axis=0, tiled=True)

    halo = move(tokens[0, -HALO:], lambda s, f: (s + 1, f) if s + 1 < ranks else None)
    longer = jnp.concatenate([halo, tokens[0]], axis=0).astype(F32)
    inverse = lax.rsqrt(jnp.mean(longer * longer, axis=-1, keepdims=True) + EPSILON)
    normed_long = (longer * inverse * norm_gain).astype(BF16)
    normed = normed_long[HALO:]

    cotan = cotangent[0]
    turned = w_in.T
    width_v = CONV + QUAD
    own_v = jnp.pad(turned[INNER:], ((0, width_v - (turned.shape[0] - INNER)), (0, 0)))
    chip_bits = [("fsdp", bit) for bit in (2, 4, 8) if bit < shards]
    seq_bits = [("seq", bit) for bit in (1, 2, 4, 8) if bit < ranks]
    first_bits = [seq_bits[0], chip_bits[0], seq_bits[1]] if chip_bits else [seq_bits[0], seq_bits[1], seq_bits[0]]
    orders = []
    for part in range(3):
        lead = list(dict.fromkeys(first_bits[part:] + first_bits[:part]))
        orders.append(lead + [bit for bit in chip_bits + seq_bits if bit not in lead])
    chips = ranks * (shards // 2)
    table = []
    for order in orders:
        line = []
        for place in range(chips):
            s, f = rank, shard
            for at, (axis, bit) in enumerate(order):
                if place >> (len(order) - 1 - at) & 1:
                    s, f = (s ^ bit, f) if axis == "seq" else (s, f ^ bit)
            line.append(s * (shards // 2) + (f >> 1))
        table.append(jnp.stack(line))
    table = jnp.stack(table).astype(jnp.int32)

    def halves(turned):
        blocks = turned.reshape(chips, 2, -1, turned.shape[1])
        core = shard & 1
        return lax.dynamic_index_in_dim(blocks, core, 1, False), lax.dynamic_index_in_dim(blocks, 1 - core, 1, False)

    own_g = turned[:INNER]
    crossed_v, crossed_g, crossed_o = across(own_v), across(own_g), across(w_out)
    pieces_of, places_v = gather_quarters(tie(own_v, halo), crossed_v)
    pieces_v = pieces_of(None)

    def flip(axis, bit):
        return lambda s, f: (s ^ bit, f) if axis == "seq" else (s, f ^ bit)

    def first_step(terms, *ahead):
        return [(kept, move(tie(sent, *ahead), flip(*orders[part][0]))) for part, (kept, sent) in enumerate(terms)]

    lanes_whole = w_in.shape[0] % 128 == 0
    last_near, first_far, places = pieces_v[3], pieces_v[4], places_v
    side = rank & 1
    half_g = lax.dynamic_slice_in_dim(own_g, side * (INNER // 2), INNER // 2, 0)
    near_g = [piece for piece, _ in send_near(tie(half_g, last_near, first_far))]
    if lanes_whole:
        pick_v = lambda first: pieces_v[:2] + sum([pieces_v[at + first : at + first + 2] for at in range(2, len(pieces_v), 4)], [])
        projected = weight_call(normed_long, pick_v(0), places_v, shards, width_v, width_v // 4, "project_near", "near")
        pieces_v = pieces_of(projected)
        projected = weight_call(normed_long, pick_v(2), places_v, shards, width_v, width_v // 4, "project_far", "far", projected)
    else:
        pieces_v, places_v = in_order(pieces_of(last_near), places_v, 2)
        projected = weight_call(normed_long, pieces_v, places_v, 1, width_v, width_v // 4, "project_v")
    far_g = [move(tie(piece, projected), lambda s, f: (s ^ 1, f)) for piece in near_g]
    near_o = send_near(tie(w_out, near_g[0], projected))
    lanes = lambda vec: jnp.pad(vec, (0, 128 - HEADS)).reshape(1, 128)
    rows, step_table, ecd, decay_all = step_call(projected, lanes(dt_bias), lanes(a_log))
    v = projected
    made = conv_call(ranks, v, conv_weight, conv_bias.reshape(1, CONV), rows, decay_all, ())
    x_act, slope, b_act, c_act, b_turned, c_turned, states = made
    skip_wide = jnp.repeat(skip_gain, HEAD_DIM).reshape(1, INNER)
    y_inside = inside_call(x_act, b_act, c_act, b_turned, rows, skip_wide)
    carried, totals = carry_call(ranks, exchange(states), None, [y_inside])
    s_in = exchange(carried)
    pieces_g = [own_g, crossed_g] + sum([[near, far] for near, far in zip(near_g, far_g)], [])
    for near, far in zip(near_g, far_g):
        pieces_g += [across(tie(near, projected)), across(tie(far, carried))]
    if lanes_whole:
        places_g, count_g = places, shards
        gate_in = weight_call(tie(normed, carried), pieces_g, places_g, count_g, INNER, INNER // 2, "project_gate", "halves")
    else:
        (pieces_g, places_g), count_g = in_order(pieces_g, places, 1), 1
        gate_in = weight_call(normed, pieces_g, places_g, count_g, INNER, INNER // 2, "project_gate")
    places_o = places[:shards]
    pieces_o = [w_out, crossed_o] + [piece for piece, _ in near_o]
    pieces_o += [across(tie(piece, carried)) for piece, _ in near_o]
    height_o = w_out.shape[0] * shards
    d_normed_out = weight_back_call(tie(cotan, gate_in, s_in), pieces_o[:2], places_o[:2], height_o)
    d_normed_out = weight_back_call(tie(cotan, s_in), pieces_o[2:], places_o[2:], height_o, d_normed_out)
    made = gate_call(y_inside, gate_in, d_normed_out, c_act, c_turned, ecd, out_gain.reshape(1, INNER), s_in)
    normed_out, d_gate, d_mixed, d_gain_out, states = made
    d_w_out = lax.dot_general(normed_out, cotan, TN, preferred_element_type=F32).astype(BF16)
    d_w_out_sum = lax.psum_scatter(d_w_out, both, scatter_dimension=0, tiled=True).astype(F32)
    d_gate_other = across(d_gate)
    block_out = residual_call(normed_out, pieces_o, places_o, tokens, states)
    own, other = halves(tie(normed, states).T)
    own_halo, other_halo = halves(tie(normed_long[:HALO], states).T)
    other, other_halo = across(other), across(other_halo)
    (carried,) = carry_call(ranks, exchange(states), totals, [d_w_out, block_out])
    lefts = pick_call(tie(table, carried), own, other, own_halo, other_halo)
    gate_terms = grad_call(lefts, d_gate, d_gate_other, 0, INNER // 3, False, "d_w_gate")
    r_in = exchange(carried)
    gate_parts = first_step(gate_terms, r_in)
    d_v_long, sums, heads = back_call(
        x_act, d_mixed, slope, v, conv_weight, b_act, c_act, b_turned, c_turned, rows, step_table, skip_wide, s_in, r_in, [kept for kept, _ in gate_terms]
    )
    d_v_long = tie(d_v_long, *[got for _, got in gate_parts])
    spill = move(d_v_long[tokens.shape[1] :], lambda s, f: (s - 1, f) if s > 0 else None)
    part = columns_call(tie(d_gate, d_v_long), pieces_g, places_g, count_g, lanes_whole)
    d_v_other = tie(across(d_v_long), spill, part)
    rest_terms = grad_call(lefts, d_v_long, d_v_other, 0, (CONV + 128) // 3, True, "d_w_rest")
    rest_parts = first_step(rest_terms)
    d_tokens, d_norm_gain = tokens_call(
        part, tie(d_v_long, rest_terms[0][0]), spill, pieces_v, places_v, lanes_whole,
        tokens, cotangent, norm_gain.reshape(1, D),
    )
    rest_parts = [(kept, tie(got, d_tokens)) for kept, got in rest_parts]

    heads = heads[:, :, 0].reshape(2, QUADS, 8)[:, :, :4].reshape(2, HEADS)
    d_skip = sums[KW + 1, :INNER].reshape(HEADS, HEAD_DIM).sum(axis=1)
    pieces = [
        sums[:KW].reshape(-1),
        sums[KW],
        heads[0],
        heads[1] * -jnp.exp(a_log),
        d_skip,
        d_gain_out.reshape(-1),
    ]
    flat = jnp.concatenate(pieces)
    width = flat.shape[0]
    flat = jnp.pad(flat, (0, -width % 1024)).reshape(-1, 128)
    flat = flat + across(flat)
    small_bits = seq_bits[:1] + chip_bits + seq_bits[1:]
    flat = flat + move(flat, flip(*small_bits[0]))

    def four(value, first, second):
        parts = [move(value, flip(*first)), move(value, flip(*second))]
        corner = lambda s, f: flip(*first)(*flip(*second)(s, f))
        return (value + parts[0]) + (parts[1] + move(value, corner))

    all_bits = [("fsdp", 1)] + small_bits
    pairs = [[gate_parts[part], rest_parts[part]] for part in range(3)]
    for at in range(1, len(orders[0])):
        sent = fold_call(pairs, "sent")
        kept = fold_call(pairs, "kept")
        pairs = [[(kept[part], move(sent[part], flip(*orders[part][at])))] for part in range(3)]
        flat = flat + move(tie(flat, kept[0]), flip(*small_bits[at]))
        use = all_bits[2 * at - 2 : 2 * at]
        if len(use) == 2:
            d_norm_gain = four(tie(d_norm_gain, kept[0]), *use)
        elif use:
            d_norm_gain = d_norm_gain + move(tie(d_norm_gain, kept[0]), flip(*use[0]))
    (d_w_in,) = fold_call(pairs, "last", w_in.shape[1])
    flat = flat.reshape(-1)
    small, at = [], 0
    for piece in pieces:
        small.append(flat[at : at + piece.shape[0]])
        at += piece.shape[0]
    d_norm_gain = d_norm_gain.reshape(-1)
    d_conv_weight, d_conv_bias, d_dt_bias, d_a_log, d_skip, d_gain_out = small
    return (
        block_out,
        d_tokens,
        d_norm_gain,
        d_w_in,
        d_conv_weight.reshape(KW, CONV),
        d_conv_bias,
        d_dt_bias,
        d_a_log,
        d_skip,
        d_gain_out,
        d_w_out_sum,
    )


def solution(mesh):
    split = P("fsdp", "seq", None)
    rows = P("fsdp", None)
    last = P(("seq", "fsdp"), None)
    return jax.shard_map(
        functools.partial(on_device, mesh.shape["seq"], mesh.shape["fsdp"]),
        mesh=mesh,
        in_specs=(split, P(), rows, P(), P(), P(), P(), P(), P(), rows, split),
        out_specs=(split, split, P(), last, P(), P(), P(), P(), P(), P(), last),
        check_vma=False,
    )
```

```python
import functools

import jax
import jax.numpy as jnp
from jax import lax
from jax.experimental import pallas as pl
from jax.experimental.pallas import tpu as pltpu
from jax.sharding import PartitionSpec as P

HEADS = 48
HEAD_DIM = 64
STATE = 128
KW = 4
INNER = 3072
D = 1536
CONV = INNER + 2 * STATE

EPSILON = 1e-05
CHUNK = 128
QUAD = 256
QUADS = INNER // QUAD
HALO = 16
VMEM_LIMIT = 56 * 1024 * 1024
LONG = pl.CostEstimate(flops=40000000000, bytes_accessed=1000000, transcendentals=0)
COST = pl.CostEstimate(flops=1000000, bytes_accessed=1000000, transcendentals=0)
F32 = jnp.float32
BF16 = jnp.bfloat16
HIGHEST = lax.Precision.HIGHEST
NT = (((1,), (1,)), ((), ()))
TN = (((0,), (0,)), ((), ()))


def iota(shape, axis):
    return lax.broadcasted_iota(jnp.int32, shape, axis)


def tie(value, *others):
    return lax.optimization_barrier((value,) + others)[0] if others else value


def mm(a, b):
    return jnp.dot(a, b, preferred_element_type=F32)


def mm_nt(a, b):
    return lax.dot_general(a, b, NT, preferred_element_type=F32)


def sigmoid(v):
    return 0.5 * jnp.tanh(0.5 * v) + 0.5


def split3(v):
    high = v.astype(BF16)
    rest = v - high.astype(F32)
    mid = rest.astype(BF16)
    low = (rest - mid.astype(F32)).astype(BF16)
    return high, mid, low


def mm_exact(v, ones):
    high, mid, low = split3(v)
    return mm(high, ones) + mm(mid, ones) + mm(low, ones)


def head_ones():
    return jnp.where((iota((128, INNER), 1) >> 6) == iota((128, INNER), 0), 1.0, 0.0).astype(BF16)


def two_heads(first, second):
    return jnp.where(iota((CHUNK, 128), 1) < HEAD_DIM, first, second)


def spread(cols, start):
    wide = [jnp.broadcast_to(cols[:, start + i : start + i + 1], (CHUNK, 128)) for i in range(4)]
    return wide, jnp.concatenate([two_heads(wide[0], wide[1]), two_heads(wide[2], wide[3])], axis=1)


def fold_rows(value):
    return jnp.sum(value.reshape(-1, 8, value.shape[1]), axis=0)


def columns_of(rows):
    count, length = rows.shape
    return jnp.concatenate([rows, jnp.zeros((128 - count, length), F32)], axis=0).T


def step_kernel(dt_ref, bias_ref, alog_ref, rows_ref, heads_ref, ecd_ref, total_ref):
    length = dt_ref.shape[0] - HALO
    raw = dt_ref[HALO:, :].astype(F32) + bias_ref[...]
    step = jnp.maximum(raw, 0.0) + jnp.log1p(jnp.exp(-jnp.abs(raw)))
    sig = 1.0 / (1.0 + jnp.exp(-raw))
    rate = -jnp.exp(alog_ref[...])
    pace = step * rate
    lower = jnp.where(iota((CHUNK, CHUNK), 0) >= iota((CHUNK, CHUNK), 1), 1.0, 0.0).astype(F32)
    inside, along = [], []
    offset = jnp.zeros((1, 128), F32)
    for start in range(0, length, CHUNK):
        part = jnp.dot(lower, pace[start : start + CHUNK], precision=HIGHEST, preferred_element_type=F32)
        inside.append(part)
        along.append(part + offset)
        offset = offset + part[CHUNK - 1 : CHUNK]
    cum = jnp.concatenate(inside, axis=0)
    along = jnp.concatenate(along, axis=0)
    ecd_ref[...] = jnp.exp(along)
    total_ref[...] = jnp.broadcast_to(jnp.exp(offset), (8, 128))
    left = jnp.exp(offset - along) * step
    heads_ref[...] = jnp.zeros_like(heads_ref)
    rows_ref[...] = jnp.zeros_like(rows_ref)
    for place, array in enumerate((cum, step, left)):
        turned = array.T
        for quad in range(QUADS):
            rows_ref[quad, 8 * place : 8 * place + 4, :] = turned[4 * quad : 4 * quad + 4, :]
    for place, array in enumerate((step, sig, jnp.broadcast_to(rate, (length, 128)))):
        turned = array.T
        for quad in range(QUADS):
            heads_ref[place, 8 * quad : 8 * quad + 4, :] = turned[4 * quad : 4 * quad + 4, :]


def step_call(projected, dt_bias, a_log):
    length = projected.shape[0] - HALO
    line = pl.BlockSpec((1, 128), lambda g: (0, 0))
    return pl.pallas_call(
        step_kernel,
        grid=(1,),
        in_specs=[pl.BlockSpec((length + HALO, 128), lambda g: (0, CONV // 128)), line, line],
        out_specs=(
            pl.BlockSpec((QUADS, 24, length), lambda g: (0, 0, 0)),
            pl.BlockSpec((3, 8 * QUADS, length), lambda g: (0, 0, 0)),
            pl.BlockSpec((length, 128), lambda g: (0, 0)),
            pl.BlockSpec((8, 128), lambda g: (0, 0)),
        ),
        out_shape=(
            jax.ShapeDtypeStruct((QUADS, 24, length), F32),
            jax.ShapeDtypeStruct((3, 8 * QUADS, length), F32),
            jax.ShapeDtypeStruct((length, 128), F32),
            jax.ShapeDtypeStruct((8, 128), F32),
        ),
        compiler_params=pltpu.CompilerParams(vmem_limit_bytes=VMEM_LIMIT),
        cost_estimate=COST,
        name="steps",
    )(projected, dt_bias, a_log)


def conv_kernel(
    share, v_ref, cw_ref, cb_ref, rows_ref, total_ref, *rest
):
    x_ref, slope_ref, b_ref, c_ref, bt_ref, ct_ref, state_ref, ext, weighted = rest[-9:]
    length = v_ref.shape[0] - HALO
    grid = pl.program_id(0)
    for plane in range(2):
        ext[plane] = v_ref[:, 128 * plane : 128 * plane + 128].astype(F32)

    def act(start):
        made = []
        for plane in range(2):
            lanes = slice(128 * plane, 128 * plane + 128)
            total = cb_ref[:, lanes] + cw_ref[0:1, lanes] * ext[plane, HALO - 3 + start : HALO - 3 + start + CHUNK, :]
            for tap in range(1, KW):
                at = HALO - 3 + tap + start
                total = total + cw_ref[tap : tap + 1, lanes] * ext[plane, at : at + CHUNK, :]
            sig = sigmoid(total)
            slope_ref[start : start + CHUNK, lanes] = (sig * (1.0 + total * (1.0 - sig))).astype(BF16)
            made.append(total * sig)
        return jnp.concatenate(made, axis=1)

    @pl.when(grid == 0)
    def _():
        for start in range(0, length, CHUNK):
            both = act(start)
            b_part, c_part = both[:, :STATE], both[:, STATE:]
            b_ref[start : start + CHUNK, :] = b_part.astype(BF16)
            c_ref[start : start + CHUNK, :] = c_part.astype(BF16)
            bt_ref[:, start : start + CHUNK] = b_part.T.astype(BF16)
            ct_ref[:, start : start + CHUNK] = c_part.T.astype(BF16)
        high, mid, low = split3(total_ref[0:1, :])
        row = iota((STATE, 128), 0) % share
        told = jnp.where(row == 0, high.astype(F32), jnp.where(row == 1, mid.astype(F32), jnp.where(row == 2, low.astype(F32), 0.0)))
        state_ref[:, :128] = told.astype(BF16)
        state_ref[:, 128:] = jnp.zeros((STATE, QUAD - 128), BF16)

    @pl.when(grid > 0)
    def _():
        cols = columns_of(rows_ref[0])
        for start in range(0, length, CHUNK):
            x_part = act(start)
            x_ref[start : start + CHUNK, :] = x_part.astype(BF16)
            _, left = spread(cols[start : start + CHUNK], 16)
            weighted[start : start + CHUNK, :] = (x_part * left).astype(BF16)
        state_ref[...] = mm(bt_ref[...], weighted[...]).astype(BF16)


def conv_call(ranks, v, conv_weight, conv_bias, rows, total, after):
    length = v.shape[0] - HALO
    last = QUADS
    block = lambda g: (0, (g + last) % (last + 1))
    quad = lambda g: (0, jnp.maximum(g - 1, 0))
    whole = lambda g: (0, 0)
    return pl.pallas_call(
        functools.partial(conv_kernel, STATE // ranks),
        grid=(last + 1,),
        in_specs=[
            pl.BlockSpec((length + HALO, QUAD), block),
            pl.BlockSpec((KW, QUAD), block),
            pl.BlockSpec((1, QUAD), block),
            pl.BlockSpec((1, 24, length), lambda g: (jnp.maximum(g - 1, 0), 0, 0)),
            pl.BlockSpec((8, 128), whole),
        ]
        + [pl.BlockSpec(memory_space=pl.ANY)] * len(after),
        out_specs=[
            pl.BlockSpec((length, QUAD), quad),
            pl.BlockSpec((length, QUAD), block),
            pl.BlockSpec((length, STATE), whole),
            pl.BlockSpec((length, STATE), whole),
            pl.BlockSpec((STATE, length), whole),
            pl.BlockSpec((STATE, length), whole),
            pl.BlockSpec((STATE, QUAD), block),
        ],
        scratch_shapes=[pltpu.VMEM((2, length + HALO, 128), F32), pltpu.VMEM((length, QUAD), BF16)],
        out_shape=[
            jax.ShapeDtypeStruct((length, INNER), BF16),
            jax.ShapeDtypeStruct((length, CONV), BF16),
            jax.ShapeDtypeStruct((length, STATE), BF16),
            jax.ShapeDtypeStruct((length, STATE), BF16),
            jax.ShapeDtypeStruct((STATE, length), BF16),
            jax.ShapeDtypeStruct((STATE, length), BF16),
            jax.ShapeDtypeStruct((STATE, CONV), BF16),
        ],
        compiler_params=pltpu.CompilerParams(vmem_limit_bytes=VMEM_LIMIT),
        cost_estimate=COST,
        name="conv_states",
    )(v, conv_weight, conv_bias, rows, total, *after)


def carry_kernel(ranks, backward, in_ref, *rest):
    share = STATE // ranks
    if backward:
        total_ref, out_ref = rest[0], rest[-1]
        decays = total_ref[...]
    else:
        out_ref, total_ref = rest[-2:]
        for place in range(ranks):
            told = in_ref[place * share : (place + 1) * share, INNER : INNER + 128].astype(F32)
            total_ref[place : place + 1, :] = told[0:1] + told[1:2] + told[2:3]
        decays = total_ref[...]
    wide = mm_exact(decays, head_ones())
    carry = jnp.zeros((share, INNER), F32)
    for place in range(ranks - 1, -1, -1) if backward else range(ranks):
        part = slice(place * share, (place + 1) * share)
        out_ref[part, :] = carry.astype(BF16)
        carry = wide[place : place + 1] * carry + in_ref[part, :INNER].astype(F32)


def carry_call(ranks, states, totals=None, after=()):
    backward = totals is not None
    vmem = pl.BlockSpec(memory_space=pltpu.VMEM)
    outs = [jax.ShapeDtypeStruct((STATE, INNER), BF16)]
    args = [states] + ([totals] if backward else [])
    if not backward:
        outs.append(jax.ShapeDtypeStruct((ranks, 128), F32))
    return pl.pallas_call(
        functools.partial(carry_kernel, ranks, backward),
        in_specs=[vmem] * len(args) + [pl.BlockSpec(memory_space=pl.ANY)] * len(after),
        out_specs=[vmem] * len(outs),
        out_shape=outs,
        compiler_params=pltpu.CompilerParams(vmem_limit_bytes=VMEM_LIMIT),
        cost_estimate=COST,
        name="carry_back" if backward else "carry",
    )(*args, *after)


def inside_kernel(x_ref, b_ref, c_ref, bt_ref, rows_ref, skip_ref, y_ref, scores):
    length = x_ref.shape[0]
    grid = pl.program_id(0)

    @pl.when(grid == 0)
    def _():
        for start in range(0, length, CHUNK):
            part = slice(start, start + CHUNK)
            scores[part, :] = mm_nt(c_ref[part, :], b_ref[part, :])

    cols = columns_of(rows_ref[0])
    lower = iota((CHUNK, CHUNK), 0) >= iota((CHUNK, CHUNK), 1)
    first = iota((CHUNK, 128), 1) < HEAD_DIM
    for start in range(0, length, CHUNK):
        part = slice(start, start + CHUNK)
        x_f = x_ref[part, :].astype(F32)
        wide, cum = spread(cols[part], 0)
        _, step = spread(cols[part], 8)
        weights = []
        for head in range(4):
            cum_row = rows_ref[0, head : head + 1, part]
            step_row = rows_ref[0, 8 + head : 9 + head, part]
            fade = jnp.exp(jnp.where(lower, wide[head] - cum_row, -1e30))
            weights.append((scores[part, :] * fade * step_row).astype(BF16))
        pieces = []
        for pair in range(2):
            x_pair = x_f[:, 128 * pair : 128 * pair + 128]
            both = jnp.concatenate([jnp.where(first, x_pair, 0.0), jnp.where(first, 0.0, x_pair)], axis=0)
            pieces.append(mm(jnp.concatenate(weights[2 * pair : 2 * pair + 2], axis=1), both.astype(BF16)))
        y_part = jnp.concatenate(pieces, axis=1) + skip_ref[...] * x_f
        if start > 0:
            y_part = y_part + jnp.exp(cum) * mm(c_ref[part, :], state.astype(BF16))
        y_ref[part, :] = y_part
        if start + CHUNK < length:
            end = cum[CHUNK - 1 : CHUNK]
            fresh = mm(bt_ref[:, part], (x_f * (jnp.exp(end - cum) * step)).astype(BF16))
            state = fresh if start == 0 else jnp.exp(end) * state + fresh


def inside_call(x_act, b_act, c_act, b_turned, rows, skip_wide):
    length = x_act.shape[0]
    whole = lambda g: (0, 0)
    quad = lambda g: (0, g)
    return pl.pallas_call(
        inside_kernel,
        grid=(QUADS,),
        in_specs=[
            pl.BlockSpec((length, QUAD), quad),
            pl.BlockSpec((length, STATE), whole),
            pl.BlockSpec((length, STATE), whole),
            pl.BlockSpec((STATE, length), whole),
            pl.BlockSpec((1, 24, length), lambda g: (g, 0, 0)),
            pl.BlockSpec((1, QUAD), quad),
        ],
        out_specs=pl.BlockSpec((length, QUAD), quad),
        out_shape=jax.ShapeDtypeStruct((length, INNER), F32),
        scratch_shapes=[pltpu.VMEM((length, CHUNK), F32)],
        compiler_params=pltpu.CompilerParams(vmem_limit_bytes=VMEM_LIMIT),
        cost_estimate=COST,
        name="ssd_inside",
    )(x_act, b_act, c_act, b_turned, rows, skip_wide)


def gate_kernel(
    y_ref, gate_ref, dn_ref, c_ref, ct_ref, ecd_ref, gain_ref, sin_ref,
    normed_ref, dgate_ref, dm_ref, dgain_ref, out_ref, ones, ecd, gated, silu, slope, back,
):
    grid = pl.program_id(0)

    @pl.when(grid == 0)
    def _():
        ones[...] = head_ones()
        back[...] = jnp.zeros_like(back)
        dgain_ref[...] = jnp.zeros_like(dgain_ref)

    high, mid, _ = split3(ecd_ref[...])
    squares = jnp.zeros((CHUNK, QUAD), F32)
    product = jnp.zeros((CHUNK, QUAD), F32)
    for at in range(0, INNER, QUAD):
        lanes = slice(at, at + QUAD)
        grown = mm(high, ones[:, lanes]) + mm(mid, ones[:, lanes])
        ecd[:, lanes] = grown
        mixed = y_ref[:, lanes] + grown * mm(c_ref[...], sin_ref[:, lanes])
        mixed = mixed.astype(BF16).astype(F32)
        gate = gate_ref[:, lanes].astype(F32)
        sig = sigmoid(gate)
        open_part = gate * sig
        value = mixed * open_part
        silu[:, lanes] = open_part
        slope[:, lanes] = mixed * (sig * (1.0 + gate * (1.0 - sig)))
        gated[:, lanes] = value
        squares = squares + value * value
        product = product + dn_ref[:, lanes] * gain_ref[:, lanes] * value
    inverse = lax.rsqrt(jnp.sum(squares, axis=1, keepdims=True) * (1.0 / INNER) + EPSILON)
    shift = inverse * inverse * inverse * (jnp.sum(product, axis=1, keepdims=True) * (1.0 / INNER))
    inverse = jnp.broadcast_to(inverse, (CHUNK, QUAD))
    shift = jnp.broadcast_to(shift, (CHUNK, QUAD))
    for at in range(0, INNER, QUAD):
        lanes = slice(at, at + QUAD)
        value = gated[:, lanes]
        scaled = value * inverse
        gain = gain_ref[:, lanes]
        dn = dn_ref[:, lanes]
        normed_ref[:, lanes] = (scaled * gain).astype(BF16)
        dgain_ref[:, lanes] += jnp.sum(dn * scaled, axis=0, keepdims=True)
        d_gated = inverse * (dn * gain) - value * shift
        dgate_ref[:, lanes] = (d_gated * slope[:, lanes]).astype(BF16)
        d_mixed = (d_gated * silu[:, lanes]).astype(BF16)
        dm_ref[:, lanes] = d_mixed
        back[:, lanes] += mm(ct_ref[...], (d_mixed.astype(F32) * ecd[:, lanes]).astype(BF16))

    @pl.when(grid == pl.num_programs(0) - 1)
    def _():
        out_ref[...] = back[...].astype(BF16)


def gate_call(y_inside, gate_in, d_normed, c_act, c_turned, ecd, out_gain, s_in):
    length = y_inside.shape[0]
    whole = lambda g: (0, 0)
    down = lambda g: (g, 0)
    wide = pl.BlockSpec((CHUNK, INNER), down)
    rows = jax.ShapeDtypeStruct((length, INNER), BF16)
    state = pl.BlockSpec((STATE, INNER), whole)
    line = pl.BlockSpec((1, INNER), whole)
    return pl.pallas_call(
        gate_kernel,
        grid=(length // CHUNK,),
        in_specs=[
            wide,
            wide,
            wide,
            pl.BlockSpec((CHUNK, STATE), down),
            pl.BlockSpec((STATE, CHUNK), lambda g: (0, g)),
            pl.BlockSpec((CHUNK, 128), down),
            line,
            state,
        ],
        out_specs=[wide, wide, wide, line, state],
        out_shape=[rows, rows, rows, jax.ShapeDtypeStruct((1, INNER), F32), jax.ShapeDtypeStruct((STATE, INNER), BF16)],
        scratch_shapes=[pltpu.VMEM((128, INNER), BF16)]
        + [pltpu.VMEM((CHUNK, INNER), F32)] * 4
        + [pltpu.VMEM((STATE, INNER), F32)],
        compiler_params=pltpu.CompilerParams(vmem_limit_bytes=VMEM_LIMIT),
        cost_estimate=COST,
        name="gated_norm",
    )(y_inside, gate_in, d_normed, c_act, c_turned, ecd, out_gain, s_in)


def back_kernel(
    x_ref, dm_ref, slope_ref, v_ref, cw_ref, b_ref, c_ref, bt_ref, ct_ref, rows_ref, table_ref, skip_ref, sin_ref, rin_ref, *rest
):
    dv_ref, sums_ref, heads_ref = rest[-14:-11]
    scores, d_scores, d_b, d_c, states, products, grads, ext, marks, across, crossing = rest[-11:]
    length = x_ref.shape[0]
    chunks = length // CHUNK
    grid = pl.program_id(0)

    @pl.when(grid == 0)
    def _():
        for start in range(0, length, CHUNK):
            part = slice(start, start + CHUNK)
            scores[part, :] = mm_nt(b_ref[part, :], c_ref[part, :])
        d_scores[...] = jnp.zeros_like(d_scores)
        d_b[...] = jnp.zeros_like(d_b)
        d_c[...] = jnp.zeros_like(d_c)
        marks[...] = jnp.zeros_like(marks)
        grads[:, 0:HALO, :] = jnp.zeros((2, HALO, 128), F32)
        grads[:, HALO + length :, :] = jnp.zeros((2, HALO, 128), F32)

    def finish(extra):
        for plane in range(2):
            lanes = slice(128 * plane, 128 * plane + 128)
            ext[plane] = v_ref[:, lanes].astype(F32)
            total = [jnp.zeros((8, 128), F32)] * (KW + 1)
            for start in range(0, length, CHUNK):
                here = grads[plane, HALO + start : HALO + start + CHUNK, :]
                for tap in range(KW):
                    at = HALO - 3 + tap + start
                    total[tap] = total[tap] + fold_rows(here * ext[plane, at : at + CHUNK, :])
                total[KW] = total[KW] + fold_rows(here)
            for at, rows in enumerate(total):
                sums_ref[at : at + 1, lanes] = jnp.sum(rows, axis=0, keepdims=True)
            for start in [0] + list(range(HALO, HALO + length, CHUNK)):
                count = HALO if start == 0 else CHUNK
                value = cw_ref[KW - 1 : KW, lanes] * grads[plane, start : start + count, :]
                for tap in range(KW - 1):
                    at = start + KW - 1 - tap
                    value = value + cw_ref[tap : tap + 1, lanes] * grads[plane, at : at + count, :]
                place = length if start == 0 else start - HALO
                dv_ref[place : place + count, lanes] = value.astype(BF16)
        sums_ref[KW + 1 : KW + 2, :] = extra
        sums_ref[KW + 2 : 8, :] = jnp.zeros((8 - KW - 2, QUAD), F32)

    def keep(start, value):
        for plane in range(2):
            grads[plane, HALO + start : HALO + start + CHUNK, :] = value[:, 128 * plane : 128 * plane + 128]

    @pl.when(grid < QUADS)
    def _():
        cols = columns_of(rows_ref[0])
        upper = iota((CHUNK, CHUNK), 0) <= iota((CHUNK, CHUNK), 1)
        first = iota((CHUNK, 128), 1) < HEAD_DIM
        lane = iota((CHUNK, 128), 1) - 8 * grid
        line = iota((8, 128), 0)
        ones = jnp.where(iota((QUAD, 128), 1) - 8 * grid == iota((QUAD, 128), 0) >> 6, 1.0, 0.0).astype(BF16)
        mine = pl.ds(pl.multiple_of(grid * 8, 8), 8)
        skip = skip_ref[...]
        after = rin_ref[...].astype(F32)
        state = sin_ref[...].astype(F32)
        spreads = []
        for chunk in range(chunks):
            part = slice(chunk * CHUNK, chunk * CHUNK + CHUNK)
            states[chunk] = state
            spreads.append(spread(cols[part], 0) + spread(cols[part], 8))
            _, cum, _, step = spreads[chunk]
            if chunk + 1 < chunks:
                end = cum[CHUNK - 1 : CHUNK]
                fed = (x_ref[part, :].astype(F32) * (jnp.exp(end - cum) * step)).astype(BF16)
                state = jnp.exp(end) * state + mm(bt_ref[:, part], fed)
        skip_sum = jnp.zeros((8, QUAD), F32)
        for chunk in range(chunks - 1, -1, -1):
            part = slice(chunk * CHUNK, chunk * CHUNK + CHUNK)
            x_f = x_ref[part, :].astype(F32)
            dm = dm_ref[part, :]
            dm_f = dm.astype(F32)
            cum_wide, cum, _, step = spreads[chunk]
            end = cum[CHUNK - 1 : CHUNK]
            after_low = after.astype(BF16)
            state = states[chunk]
            left = jnp.exp(end - cum)
            grown = dm_f * jnp.exp(cum)
            grown_low = grown.astype(BF16)
            faded = x_f * left
            fed = x_f * step
            from_after = mm(b_ref[part, :], after_low)
            from_state = mm(c_ref[part, :], state.astype(BF16))
            d_b[part, :] += mm_nt((faded * step).astype(BF16), after_low)
            d_c[part, :] += mm_nt(grown_low, state.astype(BF16))
            products[0, part, :] = (grown * from_state).astype(BF16)
            products[1, part, :] = (faded * from_after).astype(BF16)
            within = jnp.zeros((CHUNK, 128), F32)
            pair_sum = jnp.zeros((8, CHUNK), F32)
            cross_sum = jnp.zeros((8, 128), F32)
            cross = jnp.sum(state * after, axis=0, keepdims=True) * jnp.exp(end)
            summed = None
            pieces = []
            for pair in range(2):
                lanes = slice(128 * pair, 128 * pair + 128)
                x_pair, dm_pair = fed[:, lanes], dm_f[:, lanes]
                x_both = jnp.concatenate([jnp.where(first, x_pair, 0.0), jnp.where(first, 0.0, x_pair)], axis=0)
                dm_both = jnp.concatenate([jnp.where(first, dm_pair, 0.0), jnp.where(first, 0.0, dm_pair)], axis=0)
                d_weights = mm_nt(x_both.astype(BF16), dm[:, lanes])
                kept = []
                for half in range(2):
                    head = 2 * pair + half
                    cum_row = rows_ref[0, head : head + 1, part]
                    fade = jnp.exp(jnp.where(upper, cum_row - cum_wide[head], -1e30))
                    faded_grad = d_weights[half * CHUNK : half * CHUNK + CHUNK] * fade
                    summed = faded_grad if summed is None else summed + faded_grad
                    joint = faded_grad * scores[part, :]
                    within = jnp.where(lane == head, jnp.sum(joint, axis=1, keepdims=True), within)
                    pair_sum = jnp.where(line == head, jnp.sum(joint, axis=0, keepdims=True), pair_sum)
                    kept.append((scores[part, :] * fade).astype(BF16))
                    here = (iota((1, QUAD), 1) >> 6) == head
                    amount = jnp.sum(jnp.where(here, cross, 0.0), axis=1, keepdims=True)
                    cross_sum = jnp.where(line == head, amount, cross_sum)
                pieces.append(mm(jnp.concatenate(kept, axis=1), dm_both.astype(BF16)))
            d_scores[part, :] += summed
            marks[0, part, :] += within
            across[mine, part] = pair_sum
            crossing[chunk, mine, :] = cross_sum
            direct = jnp.concatenate(pieces, axis=1) + left * from_after
            products[2, part, :] = (x_f * direct).astype(BF16)
            d_x = step * direct + skip * dm_f
            keep(chunk * CHUNK, d_x * slope_ref[part, :].astype(F32))
            skip_sum = skip_sum + fold_rows(x_f * dm_f)
            after = jnp.exp(end) * after + mm(ct_ref[:, part], grown_low)
        for at in range(3):
            marks[1 + at] += mm(products[at], ones)
        finish(jnp.sum(skip_sum, axis=0, keepdims=True))

    @pl.when(grid == QUADS)
    def _():
        for start in range(0, length, CHUNK):
            part = slice(start, start + CHUNK)
            low = d_scores[part, :].astype(BF16)
            into_b = d_b[part, :] + mm(low, c_ref[part, :])
            into_c = d_c[part, :] + mm(d_scores[part, :].T.astype(BF16), b_ref[part, :])
            both = jnp.concatenate([into_b, into_c], axis=1)
            keep(start, both * slope_ref[part, :].astype(F32))
        finish(jnp.zeros((1, QUAD), F32))

    @pl.when(grid == QUADS + 1)
    def _():
        square = (CHUNK, CHUNK)
        later = jnp.where(iota(square, 0) >= iota(square, 1), 1.0, 0.0).astype(BF16)
        before = jnp.where(iota(square, 0) < iota(square, 1), 1.0, 0.0).astype(BF16)
        row, column = iota((128, QUAD), 0), iota((128, QUAD), 1)
        pick = (column < HEADS) & (row == 8 * (column >> 2) + (column & 3))
        pick = jnp.where(pick, 1.0, 0.0).astype(BF16)
        used = 8 * QUADS
        bias_sum = jnp.zeros((used, 1), F32)
        rate_sum = jnp.zeros((used, 1), F32)
        dv_ref[length:, :] = jnp.zeros((HALO, QUAD), BF16)
        for chunk in range(chunks):
            part = slice(chunk * CHUNK, chunk * CHUNK + CHUNK)
            within, carried, outward, direct = [marks[at, part, :].T[:used] for at in range(4)]
            step, sig, rate = [table_ref[at, :, part] for at in range(3)]
            change = across[0:used, part] - within + carried
            decay = mm_exact(change, later) + mm_exact(step * outward, before) + crossing[chunk]
            d_raw = (direct + rate * decay) * sig
            bias_sum = bias_sum + jnp.sum(d_raw, axis=1, keepdims=True)
            rate_sum = rate_sum + jnp.sum(step * decay, axis=1, keepdims=True)
            turned = jnp.concatenate([d_raw, jnp.zeros((128 - used, CHUNK), F32)], axis=0).T.astype(BF16)
            dv_ref[part, :] = mm(turned, pick).astype(BF16)
        heads_ref[0] = jnp.broadcast_to(bias_sum, (used, 128))
        heads_ref[1] = jnp.broadcast_to(rate_sum, (used, 128))


def back_call(x_act, d_mixed, slope, v, conv_weight, b_act, c_act, b_turned, c_turned, rows, table, skip_wide, s_in, r_in, after):
    length = x_act.shape[0]
    whole = lambda g: (0, 0)
    quad = lambda g: (0, jnp.minimum(g, QUADS - 1))
    block = lambda g: (0, jnp.minimum(g, QUADS))
    lead = lambda g: (jnp.minimum(g, QUADS - 1), 0, 0)
    return pl.pallas_call(
        back_kernel,
        grid=(QUADS + 2,),
        in_specs=[
            pl.BlockSpec((length, QUAD), quad),
            pl.BlockSpec((length, QUAD), quad),
            pl.BlockSpec((length, QUAD), block),
            pl.BlockSpec((length + HALO, QUAD), block),
            pl.BlockSpec((KW, QUAD), block),
            pl.BlockSpec((length, STATE), whole),
            pl.BlockSpec((length, STATE), whole),
            pl.BlockSpec((STATE, length), whole),
            pl.BlockSpec((STATE, length), whole),
            pl.BlockSpec((1, 24, length), lead),
            pl.BlockSpec((3, 8 * QUADS, length), lambda g: (0, 0, 0)),
            pl.BlockSpec((1, QUAD), quad),
            pl.BlockSpec((STATE, QUAD), quad),
            pl.BlockSpec((STATE, QUAD), quad),
        ]
        + [pl.BlockSpec(memory_space=pl.ANY)] * len(after),
        out_specs=[
            pl.BlockSpec((length + HALO, QUAD), lambda g: (0, g)),
            pl.BlockSpec((8, QUAD), block),
            pl.BlockSpec((2, 8 * QUADS, 128), lambda g: (0, 0, 0)),
        ],
        scratch_shapes=[
            pltpu.VMEM((length, CHUNK), F32),
            pltpu.VMEM((length, CHUNK), F32),
            pltpu.VMEM((length, STATE), F32),
            pltpu.VMEM((length, STATE), F32),
            pltpu.VMEM((length // CHUNK, STATE, QUAD), F32),
            pltpu.VMEM((3, length, QUAD), BF16),
            pltpu.VMEM((2, length + 2 * HALO, 128), F32),
            pltpu.VMEM((2, length + HALO, 128), F32),
            pltpu.VMEM((4, length, 128), F32),
            pltpu.VMEM((128, length), F32),
            pltpu.VMEM((length // CHUNK, 8 * QUADS, 128), F32),
        ],
        out_shape=[
            jax.ShapeDtypeStruct((length + HALO, CONV + QUAD), BF16),
            jax.ShapeDtypeStruct((8, CONV), F32),
            jax.ShapeDtypeStruct((2, 8 * QUADS, 128), F32),
        ],
        compiler_params=pltpu.CompilerParams(vmem_limit_bytes=VMEM_LIMIT),
        cost_estimate=LONG,
        name="ssd_back",
    )(x_act, d_mixed, slope, v, conv_weight, b_act, c_act, b_turned, c_turned, rows, table, skip_wide, s_in, r_in, *after)


def put_quarters(place_ref, count, step, refs, put):
    near = (step // 2) == place_ref[count]
    for at in range(2, count):
        for index in range(4):
            wanted = near if index < 2 else jnp.logical_not(near)

            @pl.when(wanted & (step % 2 == index % 2))
            def _():
                put(at, refs[2 + 4 * (at - 2) + index])


def put_quarters(place_ref, count, step, refs, put):
    near = (step // 2) == place_ref[count]
    for at in range(2, count):
        for index in range(4):
            wanted = near if index < 2 else jnp.logical_not(near)

            @pl.when(wanted & (step % 2 == index % 2))
            def _():
                put(at, refs[2 + 4 * (at - 2) + index])


def weight_kernel(height, split, count, place_ref, x_ref, *rest):
    piece_refs, (out_ref, w_ref) = rest[:-2], rest[-2:]

    def put(at, ref):
        w_ref[:, pl.ds(pl.multiple_of(place_ref[at] * height, 128), height)] = ref[...]

    for at in range(2 if split else count):
        put(at, piece_refs[at])
    for at in range(2, count if split else 2):
        for index in range(2):

            @pl.when(pl.program_id(0) == index)
            def _():
                put(at, piece_refs[2 + 2 * (at - 2) + index])

    out_ref[...] = mm_nt(x_ref[...], w_ref[...]).astype(BF16)


def weight_call(x, pieces, places, count, width, block, name, split="", into=None):
    rows, depth = x.shape
    height = pieces[0].shape[1]

    def block_of(g, place):
        if not split:
            return g
        side = place[count]
        if split == "halves":
            return jnp.where(g == 0, side, 1 - side)
        return 2 * (1 - side if split == "far" else side) + g

    def spec(at):
        if split and at >= 2:
            return pl.BlockSpec((block, height), lambda g, place: (0, 0))
        return pl.BlockSpec((block, height), lambda g, place: (block_of(g, place), 0))

    extra = [] if into is None else [into]
    grid_spec = pltpu.PrefetchScalarGridSpec(
        num_scalar_prefetch=1,
        grid=(2 if split else width // block,),
        in_specs=[pl.BlockSpec((rows, depth), lambda g, place: (0, 0))]
        + [spec(at) for at in range(len(pieces))]
        + [pl.BlockSpec(memory_space=pl.ANY)] * len(extra),
        out_specs=pl.BlockSpec((rows, block), lambda g, place: (0, block_of(g, place))),
        scratch_shapes=[pltpu.VMEM((block, depth), BF16)],
    )
    return pl.pallas_call(
        functools.partial(weight_kernel, height, split, count),
        grid_spec=grid_spec,
        out_shape=jax.ShapeDtypeStruct((rows, width), BF16),
        input_output_aliases={2 + len(pieces): 0} if extra else {},
        compiler_params=pltpu.CompilerParams(vmem_limit_bytes=VMEM_LIMIT),
        cost_estimate=COST,
        name=name,
    )(places, x, *pieces, *extra)


def weight_back_kernel(place_ref, g_ref, *rest):
    out_ref = rest[-1]
    for at, piece_ref in enumerate(rest[: place_ref.shape[0]]):

        @pl.when(pl.program_id(0) == at)
        def _():
            out_ref[...] = mm_nt(g_ref[...], piece_ref[...])


def weight_back_call(g, pieces, places, width, into=None):
    rows, depth = g.shape
    block = pieces[0].shape[0]
    extra = [] if into is None else [into]
    grid_spec = pltpu.PrefetchScalarGridSpec(
        num_scalar_prefetch=1,
        grid=(len(pieces),),
        in_specs=[pl.BlockSpec((rows, depth), lambda k, place: (0, 0))]
        + [pl.BlockSpec((block, depth), lambda k, place: (0, 0))] * len(pieces)
        + [pl.BlockSpec(memory_space=pl.ANY)] * len(extra),
        out_specs=pl.BlockSpec((rows, block), lambda k, place: (0, place[k])),
    )
    return pl.pallas_call(
        weight_back_kernel,
        grid_spec=grid_spec,
        out_shape=jax.ShapeDtypeStruct((rows, width), F32),
        input_output_aliases={2 + len(pieces): 0} if extra else {},
        compiler_params=pltpu.CompilerParams(vmem_limit_bytes=VMEM_LIMIT),
        cost_estimate=COST,
        name="d_normed_out",
    )(places, g, *pieces, *extra)


def pick_kernel(table_ref, own, other, own_halo, other_halo, own_out, other_out, halo_out):
    parts, blocks = own_out.shape[:2]
    for part in range(parts):

        @pl.loop(0, blocks)
        def _(at):
            block = table_ref[part, at]
            own_out[part, at] = own[block]
            other_out[part, at] = other[block]
            halo_out[part, at, :, :HALO] = own_halo[block]
            halo_out[part, at, :, HALO:] = other_halo[block]


def pick_call(table, own, other, own_halo, other_halo):
    parts, blocks = table.shape
    _, height, length = own.shape
    vmem = pl.BlockSpec(memory_space=pltpu.VMEM)
    made = pl.pallas_call(
        pick_kernel,
        in_specs=[pl.BlockSpec(memory_space=pltpu.SMEM)] + [vmem] * 4,
        out_specs=[vmem] * 3,
        out_shape=[jax.ShapeDtypeStruct((parts, blocks, height, length), BF16)] * 2
        + [jax.ShapeDtypeStruct((parts, blocks, height, 2 * HALO), BF16)],
        compiler_params=pltpu.CompilerParams(vmem_limit_bytes=VMEM_LIMIT),
        cost_estimate=COST,
        name="pick_rows",
    )(table, own, other, own_halo, other_halo)
    return [array.reshape(parts, blocks * height, -1) for array in made]


def grad_kernel(halo, *refs):
    outs = refs[-6:]
    own, other = refs[0][0], refs[1][0]
    if halo:
        edge, right, right_other, edge_right, edge_other = refs[2][0], refs[3], refs[4], refs[5], refs[6]
    else:
        right, right_other = refs[2], refs[3]
    total = mm(own, right[...]) + mm(other, right_other[...])
    if halo:
        total = total + mm(edge, jnp.concatenate([edge_right[...], edge_other[...]], axis=0))
    half = total.shape[0] // 2
    for part in range(3):

        @pl.when(pl.program_id(0) == part)
        def _():
            outs[2 * part][...] = total[:half].astype(BF16)
            outs[2 * part + 1][...] = total[half:].astype(BF16)


def grad_call(lefts, right, right_other, first, width, halo, name):
    own, other, edge = lefts
    _, rows, length = own.shape
    lead = lambda g: (g, 0, 0)
    column = lambda g: (0, first + g)
    below = lambda g: (length // HALO, first + g)
    specs = [pl.BlockSpec((1, rows, length), lead)] * 2
    args = [own, other]
    if halo:
        specs.append(pl.BlockSpec((1, rows, 2 * HALO), lead))
        args.append(edge)
    specs += [pl.BlockSpec((length, width), column)] * 2
    args += [right, right_other]
    if halo:
        specs += [pl.BlockSpec((HALO, width), below)] * 2
        args += [right, right_other]
    made = pl.pallas_call(
        functools.partial(grad_kernel, halo),
        grid=(3,),
        in_specs=specs,
        out_specs=[pl.BlockSpec((rows // 2, width), lambda g: (0, 0))] * 6,
        out_shape=[jax.ShapeDtypeStruct((rows // 2, width), BF16)] * 6,
        compiler_params=pltpu.CompilerParams(vmem_limit_bytes=VMEM_LIMIT),
        cost_estimate=COST,
        name=name,
    )(*args)
    return [(made[2 * part], made[2 * part + 1]) for part in range(3)]


def fold_kernel(counts, rows, first, last, *refs):
    at = 0

    def added(count):
        nonlocal at
        total = refs[at][first : first + rows, :].astype(F32)
        for ref in refs[at + 1 : at + count]:
            total = total + ref[first : first + rows, :].astype(F32)
        at += count
        return total

    parts = len(counts)
    for part, (gate_count, rest_count, both_count) in enumerate(counts):
        gate, rest = added(gate_count), added(rest_count)
        wide = gate.shape[1]
        if both_count:
            both = added(both_count)
            gate, rest = gate + both[:, :wide], rest + both[:, wide:]
        if last:
            out_ref = refs[-1]
            out_ref[:, part * wide : (part + 1) * wide] = gate
            begin = parts * wide + part * rest.shape[1]
            end = min(begin + rest.shape[1], out_ref.shape[1])
            out_ref[:, begin:end] = rest[:, : end - begin]
        else:
            refs[part - parts][:, :wide] = gate.astype(BF16)
            refs[part - parts][:, wide:] = rest.astype(BF16)


def fold_call(parts, first, rows, width=0):
    arrays = [array for terms in parts for group in terms for array in group]
    counts = [tuple(len(group) for group in terms) for terms in parts]
    if rows % 16 == 0 and first % rows == 0:
        specs = [pl.BlockSpec((rows, array.shape[1]), lambda g: (first // rows, 0)) for array in arrays]
        begin = 0
    else:
        specs = [pl.BlockSpec(array.shape, lambda g: (0, 0)) for array in arrays]
        begin = first
    if width:
        shapes = [jax.ShapeDtypeStruct((rows, width), F32)]
    else:
        shapes = [jax.ShapeDtypeStruct((rows, gate[0].shape[1] + rest[0].shape[1]), BF16) for gate, rest, _ in parts]
    return pl.pallas_call(
        functools.partial(fold_kernel, counts, rows, begin, bool(width)),
        grid=(1,),
        in_specs=specs,
        out_specs=[pl.BlockSpec(shape.shape, lambda g: (0, 0)) for shape in shapes],
        out_shape=shapes,
        compiler_params=pltpu.CompilerParams(vmem_limit_bytes=VMEM_LIMIT),
        cost_estimate=COST,
        name="fold",
    )(*arrays)


def residual_kernel(place_ref, *refs):
    count = len(refs) // 2 - 1
    total = refs[2 * count][0].astype(F32)
    for at in range(count):
        total = total + mm(refs[at][...], refs[count + at][...])
    refs[-1][0] = total


def residual_call(x, pieces, places, tokens, after):
    rows = x.shape[0]
    height, width = pieces[0].shape
    block = 768
    part = lambda at: pl.BlockSpec((rows, height), lambda g, place: (0, place[at]))
    whole = pl.BlockSpec((1, rows, block), lambda g, place: (0, 0, g))
    grid_spec = pltpu.PrefetchScalarGridSpec(
        num_scalar_prefetch=1,
        grid=(width // block,),
        in_specs=[part(at) for at in range(len(pieces))]
        + [pl.BlockSpec((height, block), lambda g, place: (0, g))] * len(pieces)
        + [whole],
        out_specs=whole,
    )
    return pl.pallas_call(
        residual_kernel,
        grid_spec=grid_spec,
        out_shape=jax.ShapeDtypeStruct((1, rows, width), F32),
        compiler_params=pltpu.CompilerParams(vmem_limit_bytes=VMEM_LIMIT),
        cost_estimate=LONG,
        name="block_out",
    )(tie(places, after), *([x] * len(pieces)), *pieces, tokens)


def columns_kernel(count, split, place_ref, g_ref, *refs):
    out_ref, w = refs[-2:]
    height = D // count
    step = pl.program_id(0)

    def put(at, ref):
        w[:, pl.ds(pl.multiple_of(place_ref[at] * height, 128), height)] = ref[...]

    for at in range(2 if split else count):
        put(at, refs[at])
    for at in range(2, count if split else 2):
        for index in range(2):
            side = place_ref[count]

            @pl.when(step == (side if index == 0 else 1 - side))
            def _():
                put(at, refs[2 + 2 * (at - 2) + index])

    product = mm(g_ref[...], w[...])

    @pl.when(step == 0)
    def _():
        out_ref[...] = product

    @pl.when(step > 0)
    def _():
        out_ref[...] += product


def columns_call(g, pieces, places, count, split):
    length, depth = g.shape
    height = pieces[0].shape[1]
    block = depth // 2
    down = lambda k, place: (k, 0)
    whole = lambda k, place: (0, 0)
    grid_spec = pltpu.PrefetchScalarGridSpec(
        num_scalar_prefetch=1,
        grid=(2,),
        in_specs=[pl.BlockSpec((length, block), lambda k, place: (0, k))]
        + [pl.BlockSpec((block, height), whole if split and at >= 2 else down) for at in range(len(pieces))],
        out_specs=pl.BlockSpec((length, D), whole),
        scratch_shapes=[pltpu.VMEM((block, D), BF16)],
    )
    return pl.pallas_call(
        functools.partial(columns_kernel, count, split),
        grid_spec=grid_spec,
        out_shape=jax.ShapeDtypeStruct((length, D), F32),
        compiler_params=pltpu.CompilerParams(vmem_limit_bytes=VMEM_LIMIT),
        cost_estimate=COST,
        name="d_normed_gate",
    )(places, g, *pieces)


def tokens_kernel(count, quarters, place_ref, *refs):
    part_ref, dv_ref, spill_ref, tokens_ref, cotan_ref, gain_ref = refs[:6]
    wv_refs = refs[6:-6]
    out_ref, dgain_ref, fixed, wv, total, inverse = refs[-6:]
    length = dv_ref.shape[0]
    height = D // count
    step, steps = pl.program_id(0), pl.num_programs(0)

    @pl.when(step == 0)
    def _():
        for start in range(0, length, CHUNK):
            part = slice(start, start + CHUNK)
            values = tokens_ref[0, part, :].astype(F32)
            mean = jnp.sum(values * values, axis=1, keepdims=True) * (1.0 / D)
            inverse[part, :] = jnp.broadcast_to(lax.rsqrt(mean + EPSILON), (CHUNK, 128))

    fixed[...] = dv_ref[...]
    ends = dv_ref[length - HALO :, :].astype(F32) + spill_ref[...].astype(F32)
    fixed[length - HALO :, :] = ends.astype(BF16)

    def put(at, ref):
        wv[:, pl.ds(pl.multiple_of(place_ref[at] * height, 128), height)] = ref[...]

    for at in range(2 if quarters else count):
        put(at, wv_refs[at])
    if quarters:
        put_quarters(place_ref, count, step, wv_refs, put)
    product = mm(fixed[...], wv[...])

    @pl.when(step == 0)
    def _():
        total[...] = part_ref[...] + product

    @pl.when(step > 0)
    def _():
        total[...] += product

    @pl.when(step == steps - 1)
    def _():
        sums = jnp.zeros((8, D), F32)
        for start in range(0, length, CHUNK):
            part = slice(start, start + CHUNK)
            values = tokens_ref[0, part, :].astype(F32)
            grad = total[part, :]
            a = grad * gain_ref[...]
            inv = inverse[part, 0:1]
            sums = sums + fold_rows(grad * values * inv)
            shift = inv * inv * inv * (jnp.sum(a * values, axis=1, keepdims=True) * (1.0 / D))
            out_ref[0, part, :] = cotan_ref[0, part, :].astype(F32) + inv * a - values * shift
        dgain_ref[...] = jnp.sum(sums, axis=0, keepdims=True)


def tokens_call(part, d_v, spill, pieces, places, quarters, tokens, cotangent, gain):
    length = part.shape[0]
    height = pieces[0].shape[1]
    wide = d_v.shape[1]
    steps = 4
    block = wide // steps
    count = D // height
    whole = lambda k, place: (0, 0)
    column = lambda k, place: (0, k)
    down = lambda k, place: (k, 0)
    all_rows = pl.BlockSpec((1, length, D), lambda k, place: (0, 0, 0))
    grid_spec = pltpu.PrefetchScalarGridSpec(
        num_scalar_prefetch=1,
        grid=(steps,),
        in_specs=[
            pl.BlockSpec((length, D), whole),
            pl.BlockSpec((length, block), column),
            pl.BlockSpec((HALO, block), column),
            all_rows,
            all_rows,
            pl.BlockSpec((1, D), whole),
        ]
        + [pl.BlockSpec((block, height), whole if quarters and at >= 2 else down) for at in range(len(pieces))],
        out_specs=[all_rows, pl.BlockSpec((1, D), whole)],
        scratch_shapes=[
            pltpu.VMEM((length, block), BF16),
            pltpu.VMEM((block, D), BF16),
            pltpu.VMEM((length, D), F32),
            pltpu.VMEM((length, 128), F32),
        ],
    )
    return pl.pallas_call(
        functools.partial(tokens_kernel, count, quarters),
        grid_spec=grid_spec,
        out_shape=[jax.ShapeDtypeStruct((1, length, D), F32), jax.ShapeDtypeStruct((1, D), F32)],
        compiler_params=pltpu.CompilerParams(vmem_limit_bytes=VMEM_LIMIT),
        cost_estimate=COST,
        name="d_tokens",
    )(places, part, d_v, spill, tokens, cotangent, gain, *pieces)


def on_device(
    ranks,
    shards,
    tokens,
    norm_gain,
    w_in,
    conv_weight,
    conv_bias,
    dt_bias,
    a_log,
    skip_gain,
    out_gain,
    w_out,
    cotangent,
):
    both = ("seq", "fsdp")
    rank = lax.axis_index("seq")
    shard = lax.axis_index("fsdp")

    def move(value, target):
        pairs = []
        for s in range(ranks):
            for f in range(shards):
                goal = target(s, f)
                if goal is not None:
                    pairs.append((s * shards + f, goal[0] * shards + goal[1]))
        return lax.ppermute(value, both, pairs)

    def across(value):
        return move(value, lambda s, f: (s, f ^ 1))

    def send_near(value):
        return [(move(value, lambda s, f: (s, f ^ step)), step) for step in range(2, shards, 2)]

    def gather_quarters(value, crossed):
        quarter = value.shape[0] // 4
        side = rank & 1
        remote = []
        for step in range(2, shards, 2):
            near, far = [], []
            for part in range(2):
                sent = lax.dynamic_slice_in_dim(value, (2 * side + part) * quarter, quarter, 0)
                near.append(move(tie(sent, *near), lambda s, f: (s, f ^ step)))
                far.append(move(near[part], lambda s, f: (s ^ 1, f)))
            remote.append((near, far))
        crossed_near = [[across(piece) for piece in near] for near, _ in remote]
        places = [shard, shard ^ 1] + [shard ^ step for step in range(2, shards, 2)]
        places += [shard ^ step ^ 1 for step in range(2, shards, 2)] + [side]

        def pieces(ready):
            made = [value, crossed] + [piece for near, far in remote for piece in near + far]
            for near, (_, far) in zip(crossed_near, remote):
                made += near + [None] * 2 if ready is None else near + [across(far[0]), across(tie(far[1], ready))]
            return made

        return pieces, jnp.stack(places).astype(jnp.int32)

    def in_order(pieces, places, cuts):
        height = pieces[0].shape[1]
        whole = jnp.zeros((pieces[0].shape[0], height * shards), pieces[0].dtype)
        for at, piece in enumerate(pieces):
            first, place = 0, at
            if at >= 2:
                place, index = 2 + (at - 2) // (2 * cuts), (at - 2) % (2 * cuts)
                side = places[shards] if index < cuts else 1 - places[shards]
                first = (cuts * side + index % cuts) * piece.shape[0]
            whole = lax.dynamic_update_slice(whole, piece, (first, places[place] * height))
        return [whole], jnp.zeros((1,), jnp.int32)

    def exchange(states):
        return lax.all_to_all(states, "seq", split_axis=0, concat_axis=0, tiled=True)

    halo = move(tokens[0, -HALO:], lambda s, f: (s + 1, f) if s + 1 < ranks else None)
    longer = jnp.concatenate([halo, tokens[0]], axis=0).astype(F32)
    inverse = lax.rsqrt(jnp.mean(longer * longer, axis=-1, keepdims=True) + EPSILON)
    normed_long = (longer * inverse * norm_gain).astype(BF16)
    normed = normed_long[HALO:]

    cotan = cotangent[0]
    turned = w_in.T
    width_v = CONV + QUAD
    own_v = jnp.pad(turned[INNER:], ((0, width_v - (turned.shape[0] - INNER)), (0, 0)))
    chip_bits = [("fsdp", bit) for bit in (2, 4, 8) if bit < shards]
    seq_bits = [("seq", bit) for bit in (1, 2, 4, 8) if bit < ranks]
    first_bits = [seq_bits[0], chip_bits[0], seq_bits[1]] if chip_bits else [seq_bits[0], seq_bits[1], seq_bits[0]]
    orders = []
    for part in range(3):
        lead = list(dict.fromkeys(first_bits[part:] + first_bits[:part]))
        orders.append(lead + [bit for bit in chip_bits + seq_bits if bit not in lead])
    chips = ranks * (shards // 2)
    table = []
    for order in orders:
        line = []
        for place in range(chips):
            s, f = rank, shard
            for at, (axis, bit) in enumerate(order):
                if place >> (len(order) - 1 - at) & 1:
                    s, f = (s ^ bit, f) if axis == "seq" else (s, f ^ bit)
            line.append(s * (shards // 2) + (f >> 1))
        table.append(jnp.stack(line))
    table = jnp.stack(table).astype(jnp.int32)

    def halves(turned):
        blocks = turned.reshape(chips, 2, -1, turned.shape[1])
        core = shard & 1
        return lax.dynamic_index_in_dim(blocks, core, 1, False), lax.dynamic_index_in_dim(blocks, 1 - core, 1, False)

    own_g = turned[:INNER]
    crossed_v, crossed_g, crossed_o = across(own_v), across(own_g), across(w_out)
    pieces_of, places_v = gather_quarters(tie(own_v, halo), crossed_v)
    pieces_v = pieces_of(None)

    def flip(axis, bit):
        return lambda s, f: (s ^ bit, f) if axis == "seq" else (s, f ^ bit)

    def first_step(terms, *ahead):
        return [(kept, move(tie(sent, *ahead), flip(*orders[part][0]))) for part, (kept, sent) in enumerate(terms)]

    lanes_whole = w_in.shape[0] % 128 == 0
    last_near, first_far, places = pieces_v[3], pieces_v[4], places_v
    side = rank & 1
    half_g = lax.dynamic_slice_in_dim(own_g, side * (INNER // 2), INNER // 2, 0)
    near_g = [piece for piece, _ in send_near(tie(half_g, last_near, first_far))]
    if lanes_whole:
        pick_v = lambda first: pieces_v[:2] + sum([pieces_v[at + first : at + first + 2] for at in range(2, len(pieces_v), 4)], [])
        projected = weight_call(normed_long, pick_v(0), places_v, shards, width_v, width_v // 4, "project_near", "near")
        pieces_v = pieces_of(projected)
        projected = weight_call(normed_long, pick_v(2), places_v, shards, width_v, width_v // 4, "project_far", "far", projected)
    else:
        pieces_v, places_v = in_order(pieces_of(last_near), places_v, 2)
        projected = weight_call(normed_long, pieces_v, places_v, 1, width_v, width_v // 4, "project_v")
    far_g = [move(tie(piece, projected), lambda s, f: (s ^ 1, f)) for piece in near_g]
    near_o = send_near(tie(w_out, near_g[0], projected))
    lanes = lambda vec: jnp.pad(vec, (0, 128 - HEADS)).reshape(1, 128)
    rows, step_table, ecd, decay_all = step_call(projected, lanes(dt_bias), lanes(a_log))
    v = projected
    made = conv_call(ranks, v, conv_weight, conv_bias.reshape(1, CONV), rows, decay_all, ())
    x_act, slope, b_act, c_act, b_turned, c_turned, states = made
    skip_wide = jnp.repeat(skip_gain, HEAD_DIM).reshape(1, INNER)
    y_inside = inside_call(x_act, b_act, c_act, b_turned, rows, skip_wide)
    carried, totals = carry_call(ranks, exchange(states), None, [y_inside])
    s_in = exchange(carried)
    pieces_g = [own_g, crossed_g] + sum([[near, far] for near, far in zip(near_g, far_g)], [])
    for near, far in zip(near_g, far_g):
        pieces_g += [across(tie(near, projected)), across(tie(far, carried))]
    if lanes_whole:
        places_g, count_g = places, shards
        gate_in = weight_call(tie(normed, carried), pieces_g, places_g, count_g, INNER, INNER // 2, "project_gate", "halves")
    else:
        (pieces_g, places_g), count_g = in_order(pieces_g, places, 1), 1
        gate_in = weight_call(normed, pieces_g, places_g, count_g, INNER, INNER // 2, "project_gate")
    places_o = places[:shards]
    pieces_o = [w_out, crossed_o] + [piece for piece, _ in near_o]
    pieces_o += [across(tie(piece, carried)) for piece, _ in near_o]
    height_o = w_out.shape[0] * shards
    d_normed_out = weight_back_call(tie(cotan, gate_in, s_in), pieces_o[:2], places_o[:2], height_o)
    d_normed_out = weight_back_call(tie(cotan, s_in), pieces_o[2:], places_o[2:], height_o, d_normed_out)
    made = gate_call(y_inside, gate_in, d_normed_out, c_act, c_turned, ecd, out_gain.reshape(1, INNER), s_in)
    normed_out, d_gate, d_mixed, d_gain_out, states = made
    d_w_out = lax.dot_general(normed_out, cotan, TN, preferred_element_type=F32).astype(BF16)
    d_w_out_sum = lax.psum_scatter(d_w_out, both, scatter_dimension=0, tiled=True).astype(F32)
    d_gate_other = across(d_gate)
    block_out = residual_call(normed_out, pieces_o, places_o, tokens, states)
    own, other = halves(tie(normed, states).T)
    own_halo, other_halo = halves(tie(normed_long[:HALO], states).T)
    other, other_halo = across(other), across(other_halo)
    (carried,) = carry_call(ranks, exchange(states), totals, [d_w_out, block_out])
    lefts = pick_call(tie(table, carried), own, other, own_halo, other_halo)
    gate_terms = grad_call(lefts, d_gate, d_gate_other, 0, INNER // 3, False, "d_w_gate")
    r_in = exchange(carried)
    gate_parts = first_step(gate_terms, r_in)
    d_v_long, sums, heads = back_call(
        x_act, d_mixed, slope, v, conv_weight, b_act, c_act, b_turned, c_turned, rows, step_table, skip_wide, s_in, r_in, [kept for kept, _ in gate_terms]
    )
    d_v_long = tie(d_v_long, *[got for _, got in gate_parts])
    spill = move(d_v_long[tokens.shape[1] :], lambda s, f: (s - 1, f) if s > 0 else None)
    d_v_other = tie(across(d_v_long), spill)
    rest_terms = grad_call(lefts, d_v_long, d_v_other, 0, (CONV + 128) // 3, True, "d_w_rest")
    rest_parts = first_step(rest_terms)
    part_gate = columns_call(tie(d_gate, rest_terms[0][0]), pieces_g, places_g, count_g, lanes_whole)

    heads = heads[:, :, 0].reshape(2, QUADS, 8)[:, :, :4].reshape(2, HEADS)
    d_skip = sums[KW + 1, :INNER].reshape(HEADS, HEAD_DIM).sum(axis=1)
    pieces = [
        sums[:KW].reshape(-1),
        sums[KW],
        heads[0],
        heads[1] * -jnp.exp(a_log),
        d_skip,
        d_gain_out.reshape(-1),
    ]
    flat = jnp.concatenate(pieces)
    width = flat.shape[0]
    flat = jnp.pad(flat, (0, -width % 1024)).reshape(-1, 128)
    flat = flat + across(flat)
    small_bits = seq_bits[:1] + chip_bits + seq_bits[1:]
    flat = flat + move(tie(flat, part_gate), flip(*small_bits[0]))

    def summed(value, bits, taken=()):
        if not bits:
            return move(value, functools.reduce(lambda goal, bit: lambda s, f: flip(*bit)(*goal(s, f)), taken, lambda s, f: (s, f))) if taken else value
        return summed(value, bits[:-1], taken) + summed(value, bits[:-1], taken + (bits[-1],))

    all_bits = (("fsdp", 1),) + tuple(small_bits)
    rounds = len(orders[0])
    rest_parts = [(kept, tie(got, part_gate, flat)) for kept, got in rest_parts]
    parts = [(list(gate_parts[part]), list(rest_parts[part]), []) for part in range(3)]
    rows_left = rest_parts[0][0].shape[0]
    for at in range(1, rounds):
        rows_left //= 2
        sent = fold_call(parts, rows_left, rows_left)
        got = [move(sent[part], flip(*orders[part][at])) for part in range(3)]
        if at == 1:
            d_tokens, d_norm_gain = tokens_call(
                tie(part_gate, sent[0]), d_v_long, spill, pieces_v, places_v, lanes_whole, tokens, cotangent, norm_gain.reshape(1, D)
            )
            got = [tie(array, d_tokens) for array in got]
            flat = flat + move(tie(flat, d_tokens), flip(*small_bits[at]))
        else:
            d_norm_gain = tie(d_norm_gain, sent[0])
            flat = flat + move(tie(flat, sent[0]), flip(*small_bits[at]))
        d_norm_gain = summed(d_norm_gain, all_bits[2 * at - 2 :] if at + 1 == rounds else all_bits[2 * at - 2 : 2 * at])
        parts = [(gate, rest, wide + [array]) for (gate, rest, wide), array in zip(parts, got)]
    (d_w_in,) = fold_call(parts, 0, rows_left, w_in.shape[1])
    flat = flat.reshape(-1)
    small, at = [], 0
    for piece in pieces:
        small.append(flat[at : at + piece.shape[0]])
        at += piece.shape[0]
    d_norm_gain = d_norm_gain.reshape(-1)
    d_conv_weight, d_conv_bias, d_dt_bias, d_a_log, d_skip, d_gain_out = small
    return (
        block_out,
        d_tokens,
        d_norm_gain,
        d_w_in,
        d_conv_weight.reshape(KW, CONV),
        d_conv_bias,
        d_dt_bias,
        d_a_log,
        d_skip,
        d_gain_out,
        d_w_out_sum,
    )


def solution(mesh):
    split = P("fsdp", "seq", None)
    rows = P("fsdp", None)
    last = P(("seq", "fsdp"), None)
    return jax.shard_map(
        functools.partial(on_device, mesh.shape["seq"], mesh.shape["fsdp"]),
        mesh=mesh,
        in_specs=(split, P(), rows, P(), P(), P(), P(), P(), P(), rows, split),
        out_specs=(split, split, P(), last, P(), P(), P(), P(), P(), P(), last),
        check_vma=False,
    )
```

```python
import functools

import jax
import jax.numpy as jnp
from jax import lax
from jax.experimental import pallas as pl
from jax.experimental.pallas import tpu as pltpu
from jax.sharding import PartitionSpec as P

HEADS = 48
HEAD_DIM = 64
STATE = 128
KW = 4
INNER = 3072
D = 1536
CONV = INNER + 2 * STATE

EPSILON = 1e-05
CHUNK = 128
QUAD = 256
QUADS = INNER // QUAD
HALO = 16
VMEM_LIMIT = 56 * 1024 * 1024
LONG = pl.CostEstimate(flops=40000000000, bytes_accessed=1000000, transcendentals=0)
COST = pl.CostEstimate(flops=1000000, bytes_accessed=1000000, transcendentals=0)
F32 = jnp.float32
BF16 = jnp.bfloat16
HIGHEST = lax.Precision.HIGHEST
NT = (((1,), (1,)), ((), ()))
TN = (((0,), (0,)), ((), ()))


def iota(shape, axis):
    return lax.broadcasted_iota(jnp.int32, shape, axis)


def tie(value, *others):
    return lax.optimization_barrier((value,) + others)[0] if others else value


def mm(a, b):
    return jnp.dot(a, b, preferred_element_type=F32)


def mm_nt(a, b):
    return lax.dot_general(a, b, NT, preferred_element_type=F32)


def sigmoid(v):
    return 0.5 * jnp.tanh(0.5 * v) + 0.5


def split3(v):
    high = v.astype(BF16)
    rest = v - high.astype(F32)
    mid = rest.astype(BF16)
    low = (rest - mid.astype(F32)).astype(BF16)
    return high, mid, low


def mm_exact(v, ones):
    high, mid, low = split3(v)
    return mm(high, ones) + mm(mid, ones) + mm(low, ones)


def head_ones():
    return jnp.where((iota((128, INNER), 1) >> 6) == iota((128, INNER), 0), 1.0, 0.0).astype(BF16)


def two_heads(first, second):
    return jnp.where(iota((CHUNK, 128), 1) < HEAD_DIM, first, second)


def spread(cols, start):
    wide = [jnp.broadcast_to(cols[:, start + i : start + i + 1], (CHUNK, 128)) for i in range(4)]
    return wide, jnp.concatenate([two_heads(wide[0], wide[1]), two_heads(wide[2], wide[3])], axis=1)


def fold_rows(value):
    return jnp.sum(value.reshape(-1, 8, value.shape[1]), axis=0)


def columns_of(rows):
    count, length = rows.shape
    return jnp.concatenate([rows, jnp.zeros((128 - count, length), F32)], axis=0).T


def step_kernel(dt_ref, bias_ref, alog_ref, rows_ref, heads_ref, ecd_ref, total_ref):
    length = dt_ref.shape[0] - HALO
    raw = dt_ref[HALO:, :].astype(F32) + bias_ref[...]
    step = jnp.maximum(raw, 0.0) + jnp.log1p(jnp.exp(-jnp.abs(raw)))
    sig = 1.0 / (1.0 + jnp.exp(-raw))
    rate = -jnp.exp(alog_ref[...])
    pace = step * rate
    lower = jnp.where(iota((CHUNK, CHUNK), 0) >= iota((CHUNK, CHUNK), 1), 1.0, 0.0).astype(F32)
    inside, along = [], []
    offset = jnp.zeros((1, 128), F32)
    for start in range(0, length, CHUNK):
        part = jnp.dot(lower, pace[start : start + CHUNK], precision=HIGHEST, preferred_element_type=F32)
        inside.append(part)
        along.append(part + offset)
        offset = offset + part[CHUNK - 1 : CHUNK]
    cum = jnp.concatenate(inside, axis=0)
    along = jnp.concatenate(along, axis=0)
    ecd_ref[...] = jnp.exp(along)
    total_ref[...] = jnp.broadcast_to(jnp.exp(offset), (8, 128))
    left = jnp.exp(offset - along) * step
    heads_ref[...] = jnp.zeros_like(heads_ref)
    rows_ref[...] = jnp.zeros_like(rows_ref)
    for place, array in enumerate((cum, step, left)):
        turned = array.T
        for quad in range(QUADS):
            rows_ref[quad, 8 * place : 8 * place + 4, :] = turned[4 * quad : 4 * quad + 4, :]
    for place, array in enumerate((step, sig, jnp.broadcast_to(rate, (length, 128)))):
        turned = array.T
        for quad in range(QUADS):
            heads_ref[place, 8 * quad : 8 * quad + 4, :] = turned[4 * quad : 4 * quad + 4, :]


def step_call(projected, dt_bias, a_log):
    length = projected.shape[0] - HALO
    line = pl.BlockSpec((1, 128), lambda g: (0, 0))
    return pl.pallas_call(
        step_kernel,
        grid=(1,),
        in_specs=[pl.BlockSpec((length + HALO, 128), lambda g: (0, CONV // 128)), line, line],
        out_specs=(
            pl.BlockSpec((QUADS, 24, length), lambda g: (0, 0, 0)),
            pl.BlockSpec((3, 8 * QUADS, length), lambda g: (0, 0, 0)),
            pl.BlockSpec((length, 128), lambda g: (0, 0)),
            pl.BlockSpec((8, 128), lambda g: (0, 0)),
        ),
        out_shape=(
            jax.ShapeDtypeStruct((QUADS, 24, length), F32),
            jax.ShapeDtypeStruct((3, 8 * QUADS, length), F32),
            jax.ShapeDtypeStruct((length, 128), F32),
            jax.ShapeDtypeStruct((8, 128), F32),
        ),
        compiler_params=pltpu.CompilerParams(vmem_limit_bytes=VMEM_LIMIT),
        cost_estimate=COST,
        name="steps",
    )(projected, dt_bias, a_log)


def conv_kernel(
    share, v_ref, cw_ref, cb_ref, rows_ref, total_ref, *rest
):
    x_ref, slope_ref, b_ref, c_ref, bt_ref, ct_ref, state_ref, ext, weighted = rest[-9:]
    length = v_ref.shape[0] - HALO
    grid = pl.program_id(0)
    for plane in range(2):
        ext[plane] = v_ref[:, 128 * plane : 128 * plane + 128].astype(F32)

    def act(start):
        made = []
        for plane in range(2):
            lanes = slice(128 * plane, 128 * plane + 128)
            total = cb_ref[:, lanes] + cw_ref[0:1, lanes] * ext[plane, HALO - 3 + start : HALO - 3 + start + CHUNK, :]
            for tap in range(1, KW):
                at = HALO - 3 + tap + start
                total = total + cw_ref[tap : tap + 1, lanes] * ext[plane, at : at + CHUNK, :]
            sig = sigmoid(total)
            slope_ref[start : start + CHUNK, lanes] = (sig * (1.0 + total * (1.0 - sig))).astype(BF16)
            made.append(total * sig)
        return jnp.concatenate(made, axis=1)

    @pl.when(grid == 0)
    def _():
        for start in range(0, length, CHUNK):
            both = act(start)
            b_part, c_part = both[:, :STATE], both[:, STATE:]
            b_ref[start : start + CHUNK, :] = b_part.astype(BF16)
            c_ref[start : start + CHUNK, :] = c_part.astype(BF16)
            bt_ref[:, start : start + CHUNK] = b_part.T.astype(BF16)
            ct_ref[:, start : start + CHUNK] = c_part.T.astype(BF16)
        high, mid, low = split3(total_ref[0:1, :])
        row = iota((STATE, 128), 0) % share
        told = jnp.where(row == 0, high.astype(F32), jnp.where(row == 1, mid.astype(F32), jnp.where(row == 2, low.astype(F32), 0.0)))
        state_ref[:, :128] = told.astype(BF16)
        state_ref[:, 128:] = jnp.zeros((STATE, QUAD - 128), BF16)

    @pl.when(grid > 0)
    def _():
        ones = jnp.where(iota((8, QUAD), 1) >> 6 == iota((8, QUAD), 0), 1.0, 0.0).astype(BF16)
        high, mid, _ = split3(rows_ref[0, 16:24, :])
        wide = lax.dot_general(high, ones, TN, preferred_element_type=F32)
        wide = wide + lax.dot_general(mid, ones, TN, preferred_element_type=F32)
        for start in range(0, length, CHUNK):
            x_part = act(start)
            x_ref[start : start + CHUNK, :] = x_part.astype(BF16)
            left = wide[start : start + CHUNK]
            weighted[start : start + CHUNK, :] = (x_part * left).astype(BF16)
        state_ref[...] = mm(bt_ref[...], weighted[...]).astype(BF16)


def conv_call(ranks, v, conv_weight, conv_bias, rows, total, after):
    length = v.shape[0] - HALO
    last = QUADS
    block = lambda g: (0, (g + last) % (last + 1))
    quad = lambda g: (0, jnp.maximum(g - 1, 0))
    whole = lambda g: (0, 0)
    return pl.pallas_call(
        functools.partial(conv_kernel, STATE // ranks),
        grid=(last + 1,),
        in_specs=[
            pl.BlockSpec((length + HALO, QUAD), block),
            pl.BlockSpec((KW, QUAD), block),
            pl.BlockSpec((1, QUAD), block),
            pl.BlockSpec((1, 24, length), lambda g: (jnp.maximum(g - 1, 0), 0, 0)),
            pl.BlockSpec((8, 128), whole),
        ]
        + [pl.BlockSpec(memory_space=pl.ANY)] * len(after),
        out_specs=[
            pl.BlockSpec((length, QUAD), quad),
            pl.BlockSpec((length, QUAD), block),
            pl.BlockSpec((length, STATE), whole),
            pl.BlockSpec((length, STATE), whole),
            pl.BlockSpec((STATE, length), whole),
            pl.BlockSpec((STATE, length), whole),
            pl.BlockSpec((STATE, QUAD), block),
        ],
        scratch_shapes=[pltpu.VMEM((2, length + HALO, 128), F32), pltpu.VMEM((length, QUAD), BF16)],
        out_shape=[
            jax.ShapeDtypeStruct((length, INNER), BF16),
            jax.ShapeDtypeStruct((length, CONV), BF16),
            jax.ShapeDtypeStruct((length, STATE), BF16),
            jax.ShapeDtypeStruct((length, STATE), BF16),
            jax.ShapeDtypeStruct((STATE, length), BF16),
            jax.ShapeDtypeStruct((STATE, length), BF16),
            jax.ShapeDtypeStruct((STATE, CONV), BF16),
        ],
        compiler_params=pltpu.CompilerParams(vmem_limit_bytes=VMEM_LIMIT),
        cost_estimate=COST,
        name="conv_states",
    )(v, conv_weight, conv_bias, rows, total, *after)


def carry_kernel(ranks, backward, in_ref, *rest):
    share = STATE // ranks
    if backward:
        total_ref, out_ref = rest[0], rest[-1]
        decays = total_ref[...]
    else:
        out_ref, total_ref = rest[-2:]
        for place in range(ranks):
            told = in_ref[place * share : (place + 1) * share, INNER : INNER + 128].astype(F32)
            total_ref[place : place + 1, :] = told[0:1] + told[1:2] + told[2:3]
        decays = total_ref[...]
    wide = mm_exact(decays, head_ones())
    carry = jnp.zeros((share, INNER), F32)
    for place in range(ranks - 1, -1, -1) if backward else range(ranks):
        part = slice(place * share, (place + 1) * share)
        out_ref[part, :] = carry.astype(BF16)
        carry = wide[place : place + 1] * carry + in_ref[part, :INNER].astype(F32)


def carry_call(ranks, states, totals=None, after=()):
    backward = totals is not None
    vmem = pl.BlockSpec(memory_space=pltpu.VMEM)
    outs = [jax.ShapeDtypeStruct((STATE, INNER), BF16)]
    args = [states] + ([totals] if backward else [])
    if not backward:
        outs.append(jax.ShapeDtypeStruct((ranks, 128), F32))
    return pl.pallas_call(
        functools.partial(carry_kernel, ranks, backward),
        in_specs=[vmem] * len(args) + [pl.BlockSpec(memory_space=pl.ANY)] * len(after),
        out_specs=[vmem] * len(outs),
        out_shape=outs,
        compiler_params=pltpu.CompilerParams(vmem_limit_bytes=VMEM_LIMIT),
        cost_estimate=COST,
        name="carry_back" if backward else "carry",
    )(*args, *after)


def inside_kernel(x_ref, b_ref, c_ref, bt_ref, rows_ref, skip_ref, y_ref, scores):
    length = x_ref.shape[0]
    grid = pl.program_id(0)

    @pl.when(grid == 0)
    def _():
        for start in range(0, length, CHUNK):
            part = slice(start, start + CHUNK)
            scores[part, :] = mm_nt(c_ref[part, :], b_ref[part, :])

    cols = columns_of(rows_ref[0])
    lower = iota((CHUNK, CHUNK), 0) >= iota((CHUNK, CHUNK), 1)
    first = iota((CHUNK, 128), 1) < HEAD_DIM
    for start in range(0, length, CHUNK):
        part = slice(start, start + CHUNK)
        x_f = x_ref[part, :].astype(F32)
        wide, cum = spread(cols[part], 0)
        _, step = spread(cols[part], 8)
        weights = []
        for head in range(4):
            cum_row = rows_ref[0, head : head + 1, part]
            step_row = rows_ref[0, 8 + head : 9 + head, part]
            fade = jnp.exp(jnp.where(lower, wide[head] - cum_row, -1e30))
            weights.append((scores[part, :] * fade * step_row).astype(BF16))
        pieces = []
        for pair in range(2):
            x_pair = x_f[:, 128 * pair : 128 * pair + 128]
            both = jnp.concatenate([jnp.where(first, x_pair, 0.0), jnp.where(first, 0.0, x_pair)], axis=0)
            pieces.append(mm(jnp.concatenate(weights[2 * pair : 2 * pair + 2], axis=1), both.astype(BF16)))
        y_part = jnp.concatenate(pieces, axis=1) + skip_ref[...] * x_f
        if start > 0:
            y_part = y_part + jnp.exp(cum) * mm(c_ref[part, :], state.astype(BF16))
        y_ref[part, :] = y_part
        if start + CHUNK < length:
            end = cum[CHUNK - 1 : CHUNK]
            fresh = mm(bt_ref[:, part], (x_f * (jnp.exp(end - cum) * step)).astype(BF16))
            state = fresh if start == 0 else jnp.exp(end) * state + fresh


def inside_call(x_act, b_act, c_act, b_turned, rows, skip_wide):
    length = x_act.shape[0]
    whole = lambda g: (0, 0)
    quad = lambda g: (0, g)
    return pl.pallas_call(
        inside_kernel,
        grid=(QUADS,),
        in_specs=[
            pl.BlockSpec((length, QUAD), quad),
            pl.BlockSpec((length, STATE), whole),
            pl.BlockSpec((length, STATE), whole),
            pl.BlockSpec((STATE, length), whole),
            pl.BlockSpec((1, 24, length), lambda g: (g, 0, 0)),
            pl.BlockSpec((1, QUAD), quad),
        ],
        out_specs=pl.BlockSpec((length, QUAD), quad),
        out_shape=jax.ShapeDtypeStruct((length, INNER), F32),
        scratch_shapes=[pltpu.VMEM((length, CHUNK), F32)],
        compiler_params=pltpu.CompilerParams(vmem_limit_bytes=VMEM_LIMIT),
        cost_estimate=COST,
        name="ssd_inside",
    )(x_act, b_act, c_act, b_turned, rows, skip_wide)


def gate_kernel(
    y_ref, gate_ref, dn_ref, c_ref, ct_ref, ecd_ref, gain_ref, sin_ref,
    normed_ref, dgate_ref, dm_ref, dgain_ref, out_ref, ones, ecd, gated, silu, slope, back,
):
    grid = pl.program_id(0)

    @pl.when(grid == 0)
    def _():
        ones[...] = head_ones()
        back[...] = jnp.zeros_like(back)
        dgain_ref[...] = jnp.zeros_like(dgain_ref)

    high, mid, _ = split3(ecd_ref[...])
    squares = jnp.zeros((CHUNK, QUAD), F32)
    product = jnp.zeros((CHUNK, QUAD), F32)
    for at in range(0, INNER, QUAD):
        lanes = slice(at, at + QUAD)
        grown = mm(high, ones[:, lanes]) + mm(mid, ones[:, lanes])
        ecd[:, lanes] = grown
        mixed = y_ref[:, lanes] + grown * mm(c_ref[...], sin_ref[:, lanes])
        mixed = mixed.astype(BF16).astype(F32)
        gate = gate_ref[:, lanes].astype(F32)
        sig = sigmoid(gate)
        open_part = gate * sig
        value = mixed * open_part
        silu[:, lanes] = open_part
        slope[:, lanes] = mixed * (sig * (1.0 + gate * (1.0 - sig)))
        gated[:, lanes] = value
        squares = squares + value * value
        product = product + dn_ref[:, lanes] * gain_ref[:, lanes] * value
    inverse = lax.rsqrt(jnp.sum(squares, axis=1, keepdims=True) * (1.0 / INNER) + EPSILON)
    shift = inverse * inverse * inverse * (jnp.sum(product, axis=1, keepdims=True) * (1.0 / INNER))
    inverse = jnp.broadcast_to(inverse, (CHUNK, QUAD))
    shift = jnp.broadcast_to(shift, (CHUNK, QUAD))
    for at in range(0, INNER, QUAD):
        lanes = slice(at, at + QUAD)
        value = gated[:, lanes]
        scaled = value * inverse
        gain = gain_ref[:, lanes]
        dn = dn_ref[:, lanes]
        normed_ref[:, lanes] = (scaled * gain).astype(BF16)
        dgain_ref[:, lanes] += jnp.sum(dn * scaled, axis=0, keepdims=True)
        d_gated = inverse * (dn * gain) - value * shift
        dgate_ref[:, lanes] = (d_gated * slope[:, lanes]).astype(BF16)
        d_mixed = (d_gated * silu[:, lanes]).astype(BF16)
        dm_ref[:, lanes] = d_mixed
        back[:, lanes] += mm(ct_ref[...], (d_mixed.astype(F32) * ecd[:, lanes]).astype(BF16))

    @pl.when(grid == pl.num_programs(0) - 1)
    def _():
        out_ref[...] = back[...].astype(BF16)


def gate_call(y_inside, gate_in, d_normed, c_act, c_turned, ecd, out_gain, s_in):
    length = y_inside.shape[0]
    whole = lambda g: (0, 0)
    down = lambda g: (g, 0)
    wide = pl.BlockSpec((CHUNK, INNER), down)
    rows = jax.ShapeDtypeStruct((length, INNER), BF16)
    state = pl.BlockSpec((STATE, INNER), whole)
    line = pl.BlockSpec((1, INNER), whole)
    return pl.pallas_call(
        gate_kernel,
        grid=(length // CHUNK,),
        in_specs=[
            wide,
            wide,
            wide,
            pl.BlockSpec((CHUNK, STATE), down),
            pl.BlockSpec((STATE, CHUNK), lambda g: (0, g)),
            pl.BlockSpec((CHUNK, 128), down),
            line,
            state,
        ],
        out_specs=[wide, wide, wide, line, state],
        out_shape=[rows, rows, rows, jax.ShapeDtypeStruct((1, INNER), F32), jax.ShapeDtypeStruct((STATE, INNER), BF16)],
        scratch_shapes=[pltpu.VMEM((128, INNER), BF16)]
        + [pltpu.VMEM((CHUNK, INNER), F32)] * 4
        + [pltpu.VMEM((STATE, INNER), F32)],
        compiler_params=pltpu.CompilerParams(vmem_limit_bytes=VMEM_LIMIT),
        cost_estimate=COST,
        name="gated_norm",
    )(y_inside, gate_in, d_normed, c_act, c_turned, ecd, out_gain, s_in)


def back_kernel(
    x_ref, dm_ref, slope_ref, v_ref, cw_ref, b_ref, c_ref, bt_ref, ct_ref, rows_ref, table_ref, skip_ref, sin_ref, rin_ref, *rest
):
    dv_ref, sums_ref, heads_ref = rest[-14:-11]
    scores, d_scores, d_b, d_c, states, products, grads, ext, marks, across, crossing = rest[-11:]
    length = x_ref.shape[0]
    chunks = length // CHUNK
    grid = pl.program_id(0)

    @pl.when(grid == 0)
    def _():
        for start in range(0, length, CHUNK):
            part = slice(start, start + CHUNK)
            scores[part, :] = mm_nt(b_ref[part, :], c_ref[part, :])
        d_scores[...] = jnp.zeros_like(d_scores)
        d_b[...] = jnp.zeros_like(d_b)
        d_c[...] = jnp.zeros_like(d_c)
        marks[...] = jnp.zeros_like(marks)
        grads[:, 0:HALO, :] = jnp.zeros((2, HALO, 128), F32)
        grads[:, HALO + length :, :] = jnp.zeros((2, HALO, 128), F32)

    def finish(extra):
        for plane in range(2):
            lanes = slice(128 * plane, 128 * plane + 128)
            ext[plane] = v_ref[:, lanes].astype(F32)
            total = [jnp.zeros((8, 128), F32)] * (KW + 1)
            for start in range(0, length, CHUNK):
                here = grads[plane, HALO + start : HALO + start + CHUNK, :]
                for tap in range(KW):
                    at = HALO - 3 + tap + start
                    total[tap] = total[tap] + fold_rows(here * ext[plane, at : at + CHUNK, :])
                total[KW] = total[KW] + fold_rows(here)
            for at, rows in enumerate(total):
                sums_ref[at : at + 1, lanes] = jnp.sum(rows, axis=0, keepdims=True)
            for start in [0] + list(range(HALO, HALO + length, CHUNK)):
                count = HALO if start == 0 else CHUNK
                value = cw_ref[KW - 1 : KW, lanes] * grads[plane, start : start + count, :]
                for tap in range(KW - 1):
                    at = start + KW - 1 - tap
                    value = value + cw_ref[tap : tap + 1, lanes] * grads[plane, at : at + count, :]
                place = length if start == 0 else start - HALO
                dv_ref[place : place + count, lanes] = value.astype(BF16)
        sums_ref[KW + 1 : KW + 2, :] = extra
        sums_ref[KW + 2 : 8, :] = jnp.zeros((8 - KW - 2, QUAD), F32)

    def keep(start, value):
        for plane in range(2):
            grads[plane, HALO + start : HALO + start + CHUNK, :] = value[:, 128 * plane : 128 * plane + 128]

    @pl.when(grid < QUADS)
    def _():
        cols = columns_of(rows_ref[0])
        upper = iota((CHUNK, CHUNK), 0) <= iota((CHUNK, CHUNK), 1)
        first = iota((CHUNK, 128), 1) < HEAD_DIM
        lane = iota((CHUNK, 128), 1) - 8 * grid
        line = iota((8, 128), 0)
        ones = jnp.where(iota((QUAD, 128), 1) - 8 * grid == iota((QUAD, 128), 0) >> 6, 1.0, 0.0).astype(BF16)
        mine = pl.ds(pl.multiple_of(grid * 8, 8), 8)
        skip = skip_ref[...]
        after = rin_ref[...].astype(F32)
        state = sin_ref[...].astype(F32)
        spreads = []
        for chunk in range(chunks):
            part = slice(chunk * CHUNK, chunk * CHUNK + CHUNK)
            states[chunk] = state
            spreads.append(spread(cols[part], 0) + spread(cols[part], 8))
            _, cum, _, step = spreads[chunk]
            if chunk + 1 < chunks:
                end = cum[CHUNK - 1 : CHUNK]
                fed = (x_ref[part, :].astype(F32) * (jnp.exp(end - cum) * step)).astype(BF16)
                state = jnp.exp(end) * state + mm(bt_ref[:, part], fed)
        skip_sum = jnp.zeros((8, QUAD), F32)
        for chunk in range(chunks - 1, -1, -1):
            part = slice(chunk * CHUNK, chunk * CHUNK + CHUNK)
            x_f = x_ref[part, :].astype(F32)
            dm = dm_ref[part, :]
            dm_f = dm.astype(F32)
            cum_wide, cum, _, step = spreads[chunk]
            end = cum[CHUNK - 1 : CHUNK]
            after_low = after.astype(BF16)
            state = states[chunk]
            left = jnp.exp(end - cum)
            grown = dm_f * jnp.exp(cum)
            grown_low = grown.astype(BF16)
            faded = x_f * left
            fed = x_f * step
            from_after = mm(b_ref[part, :], after_low)
            from_state = mm(c_ref[part, :], state.astype(BF16))
            d_b[part, :] += mm_nt((faded * step).astype(BF16), after_low)
            d_c[part, :] += mm_nt(grown_low, state.astype(BF16))
            products[0, part, :] = (grown * from_state).astype(BF16)
            products[1, part, :] = (faded * from_after).astype(BF16)
            within = jnp.zeros((CHUNK, 128), F32)
            pair_sum = jnp.zeros((8, CHUNK), F32)
            cross_sum = jnp.zeros((8, 128), F32)
            cross = jnp.sum(state * after, axis=0, keepdims=True) * jnp.exp(end)
            summed = None
            pieces = []
            for pair in range(2):
                lanes = slice(128 * pair, 128 * pair + 128)
                x_pair, dm_pair = fed[:, lanes], dm_f[:, lanes]
                x_both = jnp.concatenate([jnp.where(first, x_pair, 0.0), jnp.where(first, 0.0, x_pair)], axis=0)
                dm_both = jnp.concatenate([jnp.where(first, dm_pair, 0.0), jnp.where(first, 0.0, dm_pair)], axis=0)
                d_weights = mm_nt(x_both.astype(BF16), dm[:, lanes])
                kept = []
                for half in range(2):
                    head = 2 * pair + half
                    cum_row = rows_ref[0, head : head + 1, part]
                    fade = jnp.exp(jnp.where(upper, cum_row - cum_wide[head], -1e30))
                    faded_grad = d_weights[half * CHUNK : half * CHUNK + CHUNK] * fade
                    summed = faded_grad if summed is None else summed + faded_grad
                    joint = faded_grad * scores[part, :]
                    within = jnp.where(lane == head, jnp.sum(joint, axis=1, keepdims=True), within)
                    pair_sum = jnp.where(line == head, jnp.sum(joint, axis=0, keepdims=True), pair_sum)
                    kept.append((scores[part, :] * fade).astype(BF16))
                    here = (iota((1, QUAD), 1) >> 6) == head
                    amount = jnp.sum(jnp.where(here, cross, 0.0), axis=1, keepdims=True)
                    cross_sum = jnp.where(line == head, amount, cross_sum)
                pieces.append(mm(jnp.concatenate(kept, axis=1), dm_both.astype(BF16)))
            d_scores[part, :] += summed
            marks[0, part, :] += within
            across[mine, part] = pair_sum
            crossing[chunk, mine, :] = cross_sum
            direct = jnp.concatenate(pieces, axis=1) + left * from_after
            products[2, part, :] = (x_f * direct).astype(BF16)
            d_x = step * direct + skip * dm_f
            keep(chunk * CHUNK, d_x * slope_ref[part, :].astype(F32))
            skip_sum = skip_sum + fold_rows(x_f * dm_f)
            after = jnp.exp(end) * after + mm(ct_ref[:, part], grown_low)
        for at in range(3):
            marks[1 + at] += mm(products[at], ones)
        finish(jnp.sum(skip_sum, axis=0, keepdims=True))

    @pl.when(grid == QUADS)
    def _():
        for start in range(0, length, CHUNK):
            part = slice(start, start + CHUNK)
            low = d_scores[part, :].astype(BF16)
            into_b = d_b[part, :] + mm(low, c_ref[part, :])
            into_c = d_c[part, :] + mm(d_scores[part, :].T.astype(BF16), b_ref[part, :])
            both = jnp.concatenate([into_b, into_c], axis=1)
            keep(start, both * slope_ref[part, :].astype(F32))
        finish(jnp.zeros((1, QUAD), F32))

    @pl.when(grid == QUADS + 1)
    def _():
        square = (CHUNK, CHUNK)
        later = jnp.where(iota(square, 0) >= iota(square, 1), 1.0, 0.0).astype(BF16)
        before = jnp.where(iota(square, 0) < iota(square, 1), 1.0, 0.0).astype(BF16)
        row, column = iota((128, QUAD), 0), iota((128, QUAD), 1)
        pick = (column < HEADS) & (row == 8 * (column >> 2) + (column & 3))
        pick = jnp.where(pick, 1.0, 0.0).astype(BF16)
        used = 8 * QUADS
        bias_sum = jnp.zeros((used, 1), F32)
        rate_sum = jnp.zeros((used, 1), F32)
        dv_ref[length:, :] = jnp.zeros((HALO, QUAD), BF16)
        for chunk in range(chunks):
            part = slice(chunk * CHUNK, chunk * CHUNK + CHUNK)
            within, carried, outward, direct = [marks[at, part, :].T[:used] for at in range(4)]
            step, sig, rate = [table_ref[at, :, part] for at in range(3)]
            change = across[0:used, part] - within + carried
            decay = mm_exact(change, later) + mm_exact(step * outward, before) + crossing[chunk]
            d_raw = (direct + rate * decay) * sig
            bias_sum = bias_sum + jnp.sum(d_raw, axis=1, keepdims=True)
            rate_sum = rate_sum + jnp.sum(step * decay, axis=1, keepdims=True)
            turned = jnp.concatenate([d_raw, jnp.zeros((128 - used, CHUNK), F32)], axis=0).T.astype(BF16)
            dv_ref[part, :] = mm(turned, pick).astype(BF16)
        heads_ref[0] = jnp.broadcast_to(bias_sum, (used, 128))
        heads_ref[1] = jnp.broadcast_to(rate_sum, (used, 128))


def back_call(x_act, d_mixed, slope, v, conv_weight, b_act, c_act, b_turned, c_turned, rows, table, skip_wide, s_in, r_in, after):
    length = x_act.shape[0]
    whole = lambda g: (0, 0)
    quad = lambda g: (0, jnp.minimum(g, QUADS - 1))
    block = lambda g: (0, jnp.minimum(g, QUADS))
    lead = lambda g: (jnp.minimum(g, QUADS - 1), 0, 0)
    return pl.pallas_call(
        back_kernel,
        grid=(QUADS + 2,),
        in_specs=[
            pl.BlockSpec((length, QUAD), quad),
            pl.BlockSpec((length, QUAD), quad),
            pl.BlockSpec((length, QUAD), block),
            pl.BlockSpec((length + HALO, QUAD), block),
            pl.BlockSpec((KW, QUAD), block),
            pl.BlockSpec((length, STATE), whole),
            pl.BlockSpec((length, STATE), whole),
            pl.BlockSpec((STATE, length), whole),
            pl.BlockSpec((STATE, length), whole),
            pl.BlockSpec((1, 24, length), lead),
            pl.BlockSpec((3, 8 * QUADS, length), lambda g: (0, 0, 0)),
            pl.BlockSpec((1, QUAD), quad),
            pl.BlockSpec((STATE, QUAD), quad),
            pl.BlockSpec((STATE, QUAD), quad),
        ]
        + [pl.BlockSpec(memory_space=pl.ANY)] * len(after),
        out_specs=[
            pl.BlockSpec((length + HALO, QUAD), lambda g: (0, g)),
            pl.BlockSpec((8, QUAD), block),
            pl.BlockSpec((2, 8 * QUADS, 128), lambda g: (0, 0, 0)),
        ],
        scratch_shapes=[
            pltpu.VMEM((length, CHUNK), F32),
            pltpu.VMEM((length, CHUNK), F32),
            pltpu.VMEM((length, STATE), F32),
            pltpu.VMEM((length, STATE), F32),
            pltpu.VMEM((length // CHUNK, STATE, QUAD), F32),
            pltpu.VMEM((3, length, QUAD), BF16),
            pltpu.VMEM((2, length + 2 * HALO, 128), F32),
            pltpu.VMEM((2, length + HALO, 128), F32),
            pltpu.VMEM((4, length, 128), F32),
            pltpu.VMEM((128, length), F32),
            pltpu.VMEM((length // CHUNK, 8 * QUADS, 128), F32),
        ],
        out_shape=[
            jax.ShapeDtypeStruct((length + HALO, CONV + QUAD), BF16),
            jax.ShapeDtypeStruct((8, CONV), F32),
            jax.ShapeDtypeStruct((2, 8 * QUADS, 128), F32),
        ],
        compiler_params=pltpu.CompilerParams(vmem_limit_bytes=VMEM_LIMIT),
        cost_estimate=LONG,
        name="ssd_back",
    )(x_act, d_mixed, slope, v, conv_weight, b_act, c_act, b_turned, c_turned, rows, table, skip_wide, s_in, r_in, *after)


def put_quarters(place_ref, count, step, refs, put):
    near = (step // 2) == place_ref[count]
    for at in range(2, count):
        for index in range(4):
            wanted = near if index < 2 else jnp.logical_not(near)

            @pl.when(wanted & (step % 2 == index % 2))
            def _():
                put(at, refs[2 + 4 * (at - 2) + index])


def put_quarters(place_ref, count, step, refs, put):
    near = (step // 2) == place_ref[count]
    for at in range(2, count):
        for index in range(4):
            wanted = near if index < 2 else jnp.logical_not(near)

            @pl.when(wanted & (step % 2 == index % 2))
            def _():
                put(at, refs[2 + 4 * (at - 2) + index])


def weight_kernel(height, split, count, place_ref, x_ref, *rest):
    piece_refs, (out_ref, w_ref) = rest[:-2], rest[-2:]

    def put(at, ref):
        w_ref[:, pl.ds(pl.multiple_of(place_ref[at] * height, 128), height)] = ref[...]

    for at in range(2 if split else count):
        put(at, piece_refs[at])
    for at in range(2, count if split else 2):
        for index in range(2):

            @pl.when(pl.program_id(0) == index)
            def _():
                put(at, piece_refs[2 + 2 * (at - 2) + index])

    out_ref[...] = mm_nt(x_ref[...], w_ref[...]).astype(BF16)


def weight_call(x, pieces, places, count, width, block, name, split="", into=None):
    rows, depth = x.shape
    height = pieces[0].shape[1]

    def block_of(g, place):
        if not split:
            return g
        side = place[count]
        if split == "halves":
            return jnp.where(g == 0, side, 1 - side)
        return 2 * (1 - side if split == "far" else side) + g

    def spec(at):
        if split and at >= 2:
            return pl.BlockSpec((block, height), lambda g, place: (0, 0))
        return pl.BlockSpec((block, height), lambda g, place: (block_of(g, place), 0))

    extra = [] if into is None else [into]
    grid_spec = pltpu.PrefetchScalarGridSpec(
        num_scalar_prefetch=1,
        grid=(2 if split else width // block,),
        in_specs=[pl.BlockSpec((rows, depth), lambda g, place: (0, 0))]
        + [spec(at) for at in range(len(pieces))]
        + [pl.BlockSpec(memory_space=pl.ANY)] * len(extra),
        out_specs=pl.BlockSpec((rows, block), lambda g, place: (0, block_of(g, place))),
        scratch_shapes=[pltpu.VMEM((block, depth), BF16)],
    )
    return pl.pallas_call(
        functools.partial(weight_kernel, height, split, count),
        grid_spec=grid_spec,
        out_shape=jax.ShapeDtypeStruct((rows, width), BF16),
        input_output_aliases={2 + len(pieces): 0} if extra else {},
        compiler_params=pltpu.CompilerParams(vmem_limit_bytes=VMEM_LIMIT),
        cost_estimate=COST,
        name=name,
    )(places, x, *pieces, *extra)


def weight_back_kernel(place_ref, g_ref, *rest):
    out_ref = rest[-1]
    for at, piece_ref in enumerate(rest[: place_ref.shape[0]]):

        @pl.when(pl.program_id(0) == at)
        def _():
            out_ref[...] = mm_nt(g_ref[...], piece_ref[...])


def weight_back_call(g, pieces, places, width, into=None):
    rows, depth = g.shape
    block = pieces[0].shape[0]
    extra = [] if into is None else [into]
    grid_spec = pltpu.PrefetchScalarGridSpec(
        num_scalar_prefetch=1,
        grid=(len(pieces),),
        in_specs=[pl.BlockSpec((rows, depth), lambda k, place: (0, 0))]
        + [pl.BlockSpec((block, depth), lambda k, place: (0, 0))] * len(pieces)
        + [pl.BlockSpec(memory_space=pl.ANY)] * len(extra),
        out_specs=pl.BlockSpec((rows, block), lambda k, place: (0, place[k])),
    )
    return pl.pallas_call(
        weight_back_kernel,
        grid_spec=grid_spec,
        out_shape=jax.ShapeDtypeStruct((rows, width), F32),
        input_output_aliases={2 + len(pieces): 0} if extra else {},
        compiler_params=pltpu.CompilerParams(vmem_limit_bytes=VMEM_LIMIT),
        cost_estimate=COST,
        name="d_normed_out",
    )(places, g, *pieces, *extra)


def pick_kernel(table_ref, own, other, own_halo, other_halo, own_out, other_out, halo_out):
    parts, blocks = own_out.shape[:2]
    for part in range(parts):

        @pl.loop(0, blocks)
        def _(at):
            block = table_ref[part, at]
            own_out[part, at] = own[block]
            other_out[part, at] = other[block]
            halo_out[part, at, :, :HALO] = own_halo[block]
            halo_out[part, at, :, HALO:] = other_halo[block]


def pick_call(table, own, other, own_halo, other_halo):
    parts, blocks = table.shape
    _, height, length = own.shape
    vmem = pl.BlockSpec(memory_space=pltpu.VMEM)
    made = pl.pallas_call(
        pick_kernel,
        in_specs=[pl.BlockSpec(memory_space=pltpu.SMEM)] + [vmem] * 4,
        out_specs=[vmem] * 3,
        out_shape=[jax.ShapeDtypeStruct((parts, blocks, height, length), BF16)] * 2
        + [jax.ShapeDtypeStruct((parts, blocks, height, 2 * HALO), BF16)],
        compiler_params=pltpu.CompilerParams(vmem_limit_bytes=VMEM_LIMIT),
        cost_estimate=COST,
        name="pick_rows",
    )(table, own, other, own_halo, other_halo)
    return [array.reshape(parts, blocks * height, -1) for array in made]


def grad_kernel(halo, *refs):
    outs = refs[-6:]
    own, other = refs[0][0], refs[1][0]
    if halo:
        edge, right, right_other, edge_right, edge_other = refs[2][0], refs[3], refs[4], refs[5], refs[6]
    else:
        right, right_other = refs[2], refs[3]
    total = mm(own, right[...]) + mm(other, right_other[...])
    if halo:
        total = total + mm(edge, jnp.concatenate([edge_right[...], edge_other[...]], axis=0))
    half = total.shape[0] // 2
    for part in range(3):

        @pl.when(pl.program_id(0) == part)
        def _():
            outs[2 * part][...] = total[:half].astype(BF16)
            outs[2 * part + 1][...] = total[half:].astype(BF16)


def grad_call(lefts, right, right_other, first, width, halo, name):
    own, other, edge = lefts
    _, rows, length = own.shape
    lead = lambda g: (g, 0, 0)
    column = lambda g: (0, first + g)
    below = lambda g: (length // HALO, first + g)
    specs = [pl.BlockSpec((1, rows, length), lead)] * 2
    args = [own, other]
    if halo:
        specs.append(pl.BlockSpec((1, rows, 2 * HALO), lead))
        args.append(edge)
    specs += [pl.BlockSpec((length, width), column)] * 2
    args += [right, right_other]
    if halo:
        specs += [pl.BlockSpec((HALO, width), below)] * 2
        args += [right, right_other]
    made = pl.pallas_call(
        functools.partial(grad_kernel, halo),
        grid=(3,),
        in_specs=specs,
        out_specs=[pl.BlockSpec((rows // 2, width), lambda g: (0, 0))] * 6,
        out_shape=[jax.ShapeDtypeStruct((rows // 2, width), BF16)] * 6,
        compiler_params=pltpu.CompilerParams(vmem_limit_bytes=VMEM_LIMIT),
        cost_estimate=COST,
        name=name,
    )(*args)
    return [(made[2 * part], made[2 * part + 1]) for part in range(3)]


def fold_kernel(counts, rows, first, last, *refs):
    at = 0

    def added(count):
        nonlocal at
        total = refs[at][first : first + rows, :].astype(F32)
        for ref in refs[at + 1 : at + count]:
            total = total + ref[first : first + rows, :].astype(F32)
        at += count
        return total

    parts = len(counts)
    for part, (gate_count, rest_count, both_count) in enumerate(counts):
        gate, rest = added(gate_count), added(rest_count)
        wide = gate.shape[1]
        if both_count:
            both = added(both_count)
            gate, rest = gate + both[:, :wide], rest + both[:, wide:]
        if last:
            out_ref = refs[-1]
            out_ref[:, part * wide : (part + 1) * wide] = gate
            begin = parts * wide + part * rest.shape[1]
            end = min(begin + rest.shape[1], out_ref.shape[1])
            out_ref[:, begin:end] = rest[:, : end - begin]
        else:
            refs[part - parts][:, :wide] = gate.astype(BF16)
            refs[part - parts][:, wide:] = rest.astype(BF16)


def fold_call(parts, first, rows, width=0):
    arrays = [array for terms in parts for group in terms for array in group]
    counts = [tuple(len(group) for group in terms) for terms in parts]
    if rows % 16 == 0 and first % rows == 0:
        specs = [pl.BlockSpec((rows, array.shape[1]), lambda g: (first // rows, 0)) for array in arrays]
        begin = 0
    else:
        specs = [pl.BlockSpec(array.shape, lambda g: (0, 0)) for array in arrays]
        begin = first
    if width:
        shapes = [jax.ShapeDtypeStruct((rows, width), F32)]
    else:
        shapes = [jax.ShapeDtypeStruct((rows, gate[0].shape[1] + rest[0].shape[1]), BF16) for gate, rest, _ in parts]
    return pl.pallas_call(
        functools.partial(fold_kernel, counts, rows, begin, bool(width)),
        grid=(1,),
        in_specs=specs,
        out_specs=[pl.BlockSpec(shape.shape, lambda g: (0, 0)) for shape in shapes],
        out_shape=shapes,
        compiler_params=pltpu.CompilerParams(vmem_limit_bytes=VMEM_LIMIT),
        cost_estimate=COST,
        name="fold",
    )(*arrays)


def residual_kernel(place_ref, *refs):
    count = len(refs) // 2 - 1
    total = refs[2 * count][0].astype(F32)
    for at in range(count):
        total = total + mm(refs[at][...], refs[count + at][...])
    refs[-1][0] = total


def residual_call(x, pieces, places, tokens, after):
    rows = x.shape[0]
    height, width = pieces[0].shape
    block = 768
    part = lambda at: pl.BlockSpec((rows, height), lambda g, place: (0, place[at]))
    whole = pl.BlockSpec((1, rows, block), lambda g, place: (0, 0, g))
    grid_spec = pltpu.PrefetchScalarGridSpec(
        num_scalar_prefetch=1,
        grid=(width // block,),
        in_specs=[part(at) for at in range(len(pieces))]
        + [pl.BlockSpec((height, block), lambda g, place: (0, g))] * len(pieces)
        + [whole],
        out_specs=whole,
    )
    return pl.pallas_call(
        residual_kernel,
        grid_spec=grid_spec,
        out_shape=jax.ShapeDtypeStruct((1, rows, width), F32),
        compiler_params=pltpu.CompilerParams(vmem_limit_bytes=VMEM_LIMIT),
        cost_estimate=LONG,
        name="block_out",
    )(tie(places, after), *([x] * len(pieces)), *pieces, tokens)


def columns_kernel(count, split, place_ref, g_ref, *refs):
    out_ref, w = refs[-2:]
    height = D // count
    step = pl.program_id(0)

    def put(at, ref):
        w[:, pl.ds(pl.multiple_of(place_ref[at] * height, 128), height)] = ref[...]

    for at in range(2 if split else count):
        put(at, refs[at])
    for at in range(2, count if split else 2):
        for index in range(2):
            side = place_ref[count]

            @pl.when(step == (side if index == 0 else 1 - side))
            def _():
                put(at, refs[2 + 2 * (at - 2) + index])

    product = mm(g_ref[...], w[...])

    @pl.when(step == 0)
    def _():
        out_ref[...] = product

    @pl.when(step > 0)
    def _():
        out_ref[...] += product


def columns_call(g, pieces, places, count, split):
    length, depth = g.shape
    height = pieces[0].shape[1]
    block = depth // 2
    down = lambda k, place: (k, 0)
    whole = lambda k, place: (0, 0)
    grid_spec = pltpu.PrefetchScalarGridSpec(
        num_scalar_prefetch=1,
        grid=(2,),
        in_specs=[pl.BlockSpec((length, block), lambda k, place: (0, k))]
        + [pl.BlockSpec((block, height), whole if split and at >= 2 else down) for at in range(len(pieces))],
        out_specs=pl.BlockSpec((length, D), whole),
        scratch_shapes=[pltpu.VMEM((block, D), BF16)],
    )
    return pl.pallas_call(
        functools.partial(columns_kernel, count, split),
        grid_spec=grid_spec,
        out_shape=jax.ShapeDtypeStruct((length, D), F32),
        compiler_params=pltpu.CompilerParams(vmem_limit_bytes=VMEM_LIMIT),
        cost_estimate=COST,
        name="d_normed_gate",
    )(places, g, *pieces)


def tokens_kernel(count, quarters, place_ref, *refs):
    part_ref, dv_ref, spill_ref, tokens_ref, cotan_ref, gain_ref = refs[:6]
    wv_refs = refs[6:-6]
    out_ref, dgain_ref, fixed, wv, total, inverse = refs[-6:]
    length = dv_ref.shape[0]
    height = D // count
    step, steps = pl.program_id(0), pl.num_programs(0)

    @pl.when(step == 0)
    def _():
        for start in range(0, length, CHUNK):
            part = slice(start, start + CHUNK)
            values = tokens_ref[0, part, :].astype(F32)
            mean = jnp.sum(values * values, axis=1, keepdims=True) * (1.0 / D)
            inverse[part, :] = jnp.broadcast_to(lax.rsqrt(mean + EPSILON), (CHUNK, 128))

    fixed[...] = dv_ref[...]
    ends = dv_ref[length - HALO :, :].astype(F32) + spill_ref[...].astype(F32)
    fixed[length - HALO :, :] = ends.astype(BF16)

    def put(at, ref):
        wv[:, pl.ds(pl.multiple_of(place_ref[at] * height, 128), height)] = ref[...]

    for at in range(2 if quarters else count):
        put(at, wv_refs[at])
    if quarters:
        put_quarters(place_ref, count, step, wv_refs, put)
    product = mm(fixed[...], wv[...])

    @pl.when(step == 0)
    def _():
        total[...] = part_ref[...] + product

    @pl.when(step > 0)
    def _():
        total[...] += product

    @pl.when(step == steps - 1)
    def _():
        sums = jnp.zeros((8, D), F32)
        for start in range(0, length, CHUNK):
            part = slice(start, start + CHUNK)
            values = tokens_ref[0, part, :].astype(F32)
            grad = total[part, :]
            a = grad * gain_ref[...]
            inv = inverse[part, 0:1]
            sums = sums + fold_rows(grad * values * inv)
            shift = inv * inv * inv * (jnp.sum(a * values, axis=1, keepdims=True) * (1.0 / D))
            out_ref[0, part, :] = cotan_ref[0, part, :].astype(F32) + inv * a - values * shift
        dgain_ref[...] = jnp.sum(sums, axis=0, keepdims=True)


def tokens_call(part, d_v, spill, pieces, places, quarters, tokens, cotangent, gain):
    length = part.shape[0]
    height = pieces[0].shape[1]
    wide = d_v.shape[1]
    steps = 4
    block = wide // steps
    count = D // height
    whole = lambda k, place: (0, 0)
    column = lambda k, place: (0, k)
    down = lambda k, place: (k, 0)
    all_rows = pl.BlockSpec((1, length, D), lambda k, place: (0, 0, 0))
    grid_spec = pltpu.PrefetchScalarGridSpec(
        num_scalar_prefetch=1,
        grid=(steps,),
        in_specs=[
            pl.BlockSpec((length, D), whole),
            pl.BlockSpec((length, block), column),
            pl.BlockSpec((HALO, block), column),
            all_rows,
            all_rows,
            pl.BlockSpec((1, D), whole),
        ]
        + [pl.BlockSpec((block, height), whole if quarters and at >= 2 else down) for at in range(len(pieces))],
        out_specs=[all_rows, pl.BlockSpec((1, D), whole)],
        scratch_shapes=[
            pltpu.VMEM((length, block), BF16),
            pltpu.VMEM((block, D), BF16),
            pltpu.VMEM((length, D), F32),
            pltpu.VMEM((length, 128), F32),
        ],
    )
    return pl.pallas_call(
        functools.partial(tokens_kernel, count, quarters),
        grid_spec=grid_spec,
        out_shape=[jax.ShapeDtypeStruct((1, length, D), F32), jax.ShapeDtypeStruct((1, D), F32)],
        compiler_params=pltpu.CompilerParams(vmem_limit_bytes=VMEM_LIMIT),
        cost_estimate=COST,
        name="d_tokens",
    )(places, part, d_v, spill, tokens, cotangent, gain, *pieces)


def on_device(
    ranks,
    shards,
    tokens,
    norm_gain,
    w_in,
    conv_weight,
    conv_bias,
    dt_bias,
    a_log,
    skip_gain,
    out_gain,
    w_out,
    cotangent,
):
    both = ("seq", "fsdp")
    rank = lax.axis_index("seq")
    shard = lax.axis_index("fsdp")

    def move(value, target):
        pairs = []
        for s in range(ranks):
            for f in range(shards):
                goal = target(s, f)
                if goal is not None:
                    pairs.append((s * shards + f, goal[0] * shards + goal[1]))
        return lax.ppermute(value, both, pairs)

    def across(value):
        return move(value, lambda s, f: (s, f ^ 1))

    def send_near(value):
        return [(move(value, lambda s, f: (s, f ^ step)), step) for step in range(2, shards, 2)]

    def gather_quarters(value, crossed):
        quarter = value.shape[0] // 4
        side = rank & 1
        remote = []
        for step in range(2, shards, 2):
            near, far = [], []
            for part in range(2):
                sent = lax.dynamic_slice_in_dim(value, (2 * side + part) * quarter, quarter, 0)
                near.append(move(tie(sent, *near), lambda s, f: (s, f ^ step)))
                far.append(move(near[part], lambda s, f: (s ^ 1, f)))
            remote.append((near, far))
        crossed_near = [[across(piece) for piece in near] for near, _ in remote]
        places = [shard, shard ^ 1] + [shard ^ step for step in range(2, shards, 2)]
        places += [shard ^ step ^ 1 for step in range(2, shards, 2)] + [side]

        def pieces(ready):
            made = [value, crossed] + [piece for near, far in remote for piece in near + far]
            for near, (_, far) in zip(crossed_near, remote):
                made += near + [None] * 2 if ready is None else near + [across(far[0]), across(tie(far[1], ready))]
            return made

        return pieces, jnp.stack(places).astype(jnp.int32)

    def in_order(pieces, places, cuts):
        height = pieces[0].shape[1]
        whole = jnp.zeros((pieces[0].shape[0], height * shards), pieces[0].dtype)
        for at, piece in enumerate(pieces):
            first, place = 0, at
            if at >= 2:
                place, index = 2 + (at - 2) // (2 * cuts), (at - 2) % (2 * cuts)
                side = places[shards] if index < cuts else 1 - places[shards]
                first = (cuts * side + index % cuts) * piece.shape[0]
            whole = lax.dynamic_update_slice(whole, piece, (first, places[place] * height))
        return [whole], jnp.zeros((1,), jnp.int32)

    def exchange(states):
        return lax.all_to_all(states, "seq", split_axis=0, concat_axis=0, tiled=True)

    turned = w_in.T
    width_v = CONV + QUAD
    own_v = jnp.pad(turned[INNER:], ((0, width_v - (turned.shape[0] - INNER)), (0, 0)))
    halo = move(tie(tokens[0, -HALO:], own_v), lambda s, f: (s + 1, f) if s + 1 < ranks else None)
    longer = jnp.concatenate([halo, tokens[0]], axis=0).astype(F32)
    inverse = lax.rsqrt(jnp.mean(longer * longer, axis=-1, keepdims=True) + EPSILON)
    normed_long = (longer * inverse * norm_gain).astype(BF16)
    normed = normed_long[HALO:]

    cotan = cotangent[0]
    chip_bits = [("fsdp", bit) for bit in (2, 4, 8) if bit < shards]
    seq_bits = [("seq", bit) for bit in (1, 2, 4, 8) if bit < ranks]
    first_bits = [seq_bits[0], chip_bits[0], seq_bits[1]] if chip_bits else [seq_bits[0], seq_bits[1], seq_bits[0]]
    orders = []
    for part in range(3):
        lead = list(dict.fromkeys(first_bits[part:] + first_bits[:part]))
        orders.append(lead + [bit for bit in chip_bits + seq_bits if bit not in lead])
    chips = ranks * (shards // 2)
    table = []
    for order in orders:
        line = []
        for place in range(chips):
            s, f = rank, shard
            for at, (axis, bit) in enumerate(order):
                if place >> (len(order) - 1 - at) & 1:
                    s, f = (s ^ bit, f) if axis == "seq" else (s, f ^ bit)
            line.append(s * (shards // 2) + (f >> 1))
        table.append(jnp.stack(line))
    table = jnp.stack(table).astype(jnp.int32)

    def halves(turned):
        blocks = turned.reshape(chips, 2, -1, turned.shape[1])
        core = shard & 1
        return lax.dynamic_index_in_dim(blocks, core, 1, False), lax.dynamic_index_in_dim(blocks, 1 - core, 1, False)

    own_g = turned[:INNER]
    crossed_v, crossed_g, crossed_o = across(own_v), across(own_g), across(w_out)
    pieces_of, places_v = gather_quarters(own_v, crossed_v)
    pieces_v = pieces_of(None)

    def flip(axis, bit):
        return lambda s, f: (s ^ bit, f) if axis == "seq" else (s, f ^ bit)

    def first_step(terms, *ahead):
        return [(kept, move(tie(sent, *ahead), flip(*orders[part][0]))) for part, (kept, sent) in enumerate(terms)]

    lanes_whole = w_in.shape[0] % 128 == 0
    last_near, first_far, places = pieces_v[3], pieces_v[4], places_v
    side = rank & 1
    half_g = lax.dynamic_slice_in_dim(own_g, side * (INNER // 2), INNER // 2, 0)
    near_g = [piece for piece, _ in send_near(tie(half_g, last_near, first_far))]
    if lanes_whole:
        pick_v = lambda first: pieces_v[:2] + sum([pieces_v[at + first : at + first + 2] for at in range(2, len(pieces_v), 4)], [])
        projected = weight_call(normed_long, pick_v(0), places_v, shards, width_v, width_v // 4, "project_near", "near")
        pieces_v = pieces_of(projected)
        projected = weight_call(normed_long, pick_v(2), places_v, shards, width_v, width_v // 4, "project_far", "far", projected)
    else:
        pieces_v, places_v = in_order(pieces_of(last_near), places_v, 2)
        projected = weight_call(normed_long, pieces_v, places_v, 1, width_v, width_v // 4, "project_v")
    far_g = [move(tie(piece, projected), lambda s, f: (s ^ 1, f)) for piece in near_g]
    near_o = send_near(tie(w_out, near_g[0], projected))
    lanes = lambda vec: jnp.pad(vec, (0, 128 - HEADS)).reshape(1, 128)
    rows, step_table, ecd, decay_all = step_call(projected, lanes(dt_bias), lanes(a_log))
    v = projected
    made = conv_call(ranks, v, conv_weight, conv_bias.reshape(1, CONV), rows, decay_all, ())
    x_act, slope, b_act, c_act, b_turned, c_turned, states = made
    skip_wide = jnp.repeat(skip_gain, HEAD_DIM).reshape(1, INNER)
    y_inside = inside_call(x_act, b_act, c_act, b_turned, rows, skip_wide)
    carried, totals = carry_call(ranks, exchange(states), None, [y_inside])
    s_in = exchange(carried)
    pieces_g = [own_g, crossed_g] + sum([[near, far] for near, far in zip(near_g, far_g)], [])
    for near, far in zip(near_g, far_g):
        pieces_g += [across(tie(near, projected)), across(tie(far, carried))]
    if lanes_whole:
        places_g, count_g = places, shards
        gate_in = weight_call(tie(normed, carried), pieces_g, places_g, count_g, INNER, INNER // 2, "project_gate", "halves")
    else:
        (pieces_g, places_g), count_g = in_order(pieces_g, places, 1), 1
        gate_in = weight_call(normed, pieces_g, places_g, count_g, INNER, INNER // 2, "project_gate")
    places_o = places[:shards]
    pieces_o = [w_out, crossed_o] + [piece for piece, _ in near_o]
    pieces_o += [across(tie(piece, carried)) for piece, _ in near_o]
    height_o = w_out.shape[0] * shards
    d_normed_out = weight_back_call(tie(cotan, gate_in, s_in), pieces_o[:2], places_o[:2], height_o)
    d_normed_out = weight_back_call(tie(cotan, s_in), pieces_o[2:], places_o[2:], height_o, d_normed_out)
    made = gate_call(y_inside, gate_in, d_normed_out, c_act, c_turned, ecd, out_gain.reshape(1, INNER), s_in)
    normed_out, d_gate, d_mixed, d_gain_out, states = made
    d_w_out = lax.dot_general(normed_out, cotan, TN, preferred_element_type=F32).astype(BF16)
    d_w_out_sum = lax.psum_scatter(d_w_out, both, scatter_dimension=0, tiled=True).astype(F32)
    d_gate_other = across(d_gate)
    block_out = residual_call(normed_out, pieces_o, places_o, tokens, states)
    own, other = halves(tie(normed, states).T)
    own_halo, other_halo = halves(tie(normed_long[:HALO], states).T)
    other, other_halo = across(other), across(other_halo)
    (carried,) = carry_call(ranks, exchange(states), totals, [d_w_out, block_out])
    lefts = pick_call(tie(table, carried), own, other, own_halo, other_halo)
    gate_terms = grad_call(lefts, d_gate, d_gate_other, 0, INNER // 3, False, "d_w_gate")
    r_in = exchange(carried)
    gate_parts = first_step(gate_terms, r_in)
    d_v_long, sums, heads = back_call(
        x_act, d_mixed, slope, v, conv_weight, b_act, c_act, b_turned, c_turned, rows, step_table, skip_wide, s_in, r_in, [kept for kept, _ in gate_terms]
    )
    d_v_long = tie(d_v_long, *[got for _, got in gate_parts])
    spill = move(d_v_long[tokens.shape[1] :], lambda s, f: (s - 1, f) if s > 0 else None)
    d_v_other = tie(across(d_v_long), spill)
    rest_terms = grad_call(lefts, d_v_long, d_v_other, 0, (CONV + 128) // 3, True, "d_w_rest")
    rest_parts = first_step(rest_terms)
    part_gate = columns_call(tie(d_gate, rest_terms[0][0]), pieces_g, places_g, count_g, lanes_whole)

    heads = heads[:, :, 0].reshape(2, QUADS, 8)[:, :, :4].reshape(2, HEADS)
    d_skip = sums[KW + 1, :INNER].reshape(HEADS, HEAD_DIM).sum(axis=1)
    pieces = [
        sums[:KW].reshape(-1),
        sums[KW],
        heads[0],
        heads[1] * -jnp.exp(a_log),
        d_skip,
        d_gain_out.reshape(-1),
    ]
    flat = jnp.concatenate(pieces)
    width = flat.shape[0]
    flat = jnp.pad(flat, (0, -width % 1024)).reshape(-1, 128)
    flat = flat + across(flat)
    small_bits = seq_bits[:1] + chip_bits + seq_bits[1:]
    flat = flat + move(tie(flat, part_gate), flip(*small_bits[0]))

    def summed(value, bits, taken=()):
        if not bits:
            return move(value, functools.reduce(lambda goal, bit: lambda s, f: flip(*bit)(*goal(s, f)), taken, lambda s, f: (s, f))) if taken else value
        return summed(value, bits[:-1], taken) + summed(value, bits[:-1], taken + (bits[-1],))

    all_bits = (("fsdp", 1),) + tuple(small_bits)
    rounds = len(orders[0])
    rest_parts = [(kept, tie(got, part_gate, flat)) for kept, got in rest_parts]
    parts = [(list(gate_parts[part]), list(rest_parts[part]), []) for part in range(3)]
    rows_left = rest_parts[0][0].shape[0]
    for at in range(1, rounds):
        rows_left //= 2
        sent = fold_call(parts, rows_left, rows_left)
        got = [move(sent[part], flip(*orders[part][at])) for part in range(3)]
        if at == 1:
            d_tokens, d_norm_gain = tokens_call(
                tie(part_gate, sent[0]), d_v_long, spill, pieces_v, places_v, lanes_whole, tokens, cotangent, norm_gain.reshape(1, D)
            )
            got = [tie(array, d_tokens) for array in got]
            flat = flat + move(tie(flat, d_tokens), flip(*small_bits[at]))
        else:
            d_norm_gain = tie(d_norm_gain, sent[0])
            flat = flat + move(tie(flat, sent[0]), flip(*small_bits[at]))
        d_norm_gain = summed(d_norm_gain, all_bits[2 * at - 2 :] if at + 1 == rounds else all_bits[2 * at - 2 : 2 * at])
        parts = [(gate, rest, wide + [array]) for (gate, rest, wide), array in zip(parts, got)]
    (d_w_in,) = fold_call(parts, 0, rows_left, w_in.shape[1])
    flat = flat.reshape(-1)
    small, at = [], 0
    for piece in pieces:
        small.append(flat[at : at + piece.shape[0]])
        at += piece.shape[0]
    d_norm_gain = d_norm_gain.reshape(-1)
    d_conv_weight, d_conv_bias, d_dt_bias, d_a_log, d_skip, d_gain_out = small
    return (
        block_out,
        d_tokens,
        d_norm_gain,
        d_w_in,
        d_conv_weight.reshape(KW, CONV),
        d_conv_bias,
        d_dt_bias,
        d_a_log,
        d_skip,
        d_gain_out,
        d_w_out_sum,
    )


def solution(mesh):
    split = P("fsdp", "seq", None)
    rows = P("fsdp", None)
    last = P(("seq", "fsdp"), None)
    return jax.shard_map(
        functools.partial(on_device, mesh.shape["seq"], mesh.shape["fsdp"]),
        mesh=mesh,
        in_specs=(split, P(), rows, P(), P(), P(), P(), P(), P(), rows, split),
        out_specs=(split, split, P(), last, P(), P(), P(), P(), P(), P(), last),
        check_vma=False,
    )
```
